32 devices in a mesh: seq: 8 (over z, y), tp: 4 (over x, core).
Axes of the slice: x: 2, y: 2, z: 4, core: 2. Of those that a mesh axis runs over, the one named last changes fastest.
Arguments:
- states: bfloat16 [64, 3072], P(None, 'seq'), may hold values from -20 to 20
- norm_gain: bfloat16 [3072], P('seq'), may hold values from 0.25 to 1.75
- w_qkv: bfloat16 [3, 3072, 3072], P(None, 'seq', 'tp'), may hold values from -0.109375 to 0.109375
- w_out: bfloat16 [3072, 3072], P('tp', 'seq'), may hold values from -0.109375 to 0.109375
- cache: bfloat16 [192, 2, 64, 3072], P('seq', None, None, 'tp'), may hold values from -400 to 400
- context_len: int32 [64], replicated, may hold values from 1 to 4096, as said below
- block_owner: int32 [192], P('seq'), may hold values from 0 to 64, as said below
- block_index: int32 [192], P('seq'), may hold values from 0 to 63, as said below
Outputs:
- hidden: bfloat16 [64, 3072], P('tp', 'seq')
- updated: bfloat16 [192, 2, 64, 3072], P('seq', None, None, 'tp')
The draws below stay inside these ranges and needn't reach their ends.
Inputs may be any that keep to these rules, and one draw needn't show every extreme that they name: `context_len`: A request of length n owns exactly ceil(n / 64) pool blocks, with block_index 0, 1, ... once each; at least one pool block is unused. `context_len`: exactly 1 request own 64/2 blocks or more; every other request owns at most 2 blocks, all on one index of seq. `block_owner`: the value 64 marks an unused block. `block_index`: 0 for an unused block.
All inputs are finite; a program needn't handle non-finite values.
Results may differ from the reference program's by a relative error of at most 0.0068.
Values may be sent and summed in bfloat16 or wider, within the bound.
No kernel may reach another device: no remote copies, remote signals or barrier semaphores. Data moves between devices by JAX's collectives and lax.ppermute only.
A program may use at most 128 MiB of HBM per device.

```python
import jax
import jax.numpy as jnp
from jax import lax

D = 3072
HEAD_DIM = 96
BLOCK_TOKENS = 64
MAX_BLOCKS = 64
REQS = 64
BLOCKS_DEV = 24
POOL = 192
LONG_REQS = 1
ATT_WIDTH = 3072
N_SEQ = 8


def layout(key):
    base_key = jax.random.fold_in(key, 11)
    split_keys = jax.random.split(base_key, 5)
    order = jax.random.permutation(split_keys[0], REQS)
    ranks = jnp.argsort(order).astype(jnp.int32)
    short_rank = ranks - LONG_REQS
    short_count = jax.random.randint(split_keys[1], (REQS,), 1, 3)
    long_count = jax.random.randint(split_keys[2], (REQS,), MAX_BLOCKS // 2, MAX_BLOCKS + 1)
    counts = jnp.where(ranks == 0, MAX_BLOCKS, jnp.where(ranks < LONG_REQS, long_count, jnp.where(short_rank == 0, 1, short_count))).astype(jnp.int32)
    tails = jax.random.randint(split_keys[3], (REQS,), 1, BLOCK_TOKENS + 1)
    lengths = jnp.where(ranks == 0, MAX_BLOCKS * BLOCK_TOKENS, (counts - 1) * BLOCK_TOKENS + tails).astype(jnp.int32)
    place_j = jnp.arange(MAX_BLOCKS, dtype=jnp.int32)
    used = place_j[None, :] < counts[:, None]
    long_device = (ranks[:, None] * MAX_BLOCKS + place_j[None, :]) % N_SEQ
    short_device = jnp.broadcast_to((jnp.maximum(short_rank, 0) % N_SEQ)[:, None], (REQS, MAX_BLOCKS))
    device = jnp.where(ranks[:, None] < LONG_REQS, long_device, short_device).astype(jnp.int32).reshape(-1)
    used_flat = used.reshape(-1)
    onehot = ((device[:, None] == jnp.arange(N_SEQ, dtype=jnp.int32)[None, :]) & used_flat[:, None]).astype(jnp.int32)
    before = jnp.cumsum(onehot, axis=0).astype(jnp.int32) - onehot
    local = jnp.take_along_axis(before, device[:, None], axis=1)[:, 0]
    perms = jax.vmap(lambda sub_key: jax.random.permutation(sub_key, BLOCKS_DEV))(jax.random.split(split_keys[4], N_SEQ)).astype(jnp.int32)
    slot_place = device * BLOCKS_DEV + perms[device, jnp.minimum(local, BLOCKS_DEV - 1)]
    position = jnp.where(used_flat, slot_place, POOL).astype(jnp.int32)
    owners = jnp.repeat(jnp.arange(REQS, dtype=jnp.int32), MAX_BLOCKS)
    indices = jnp.tile(place_j, REQS)
    owner_table = jnp.full((POOL,), REQS, jnp.int32).at[position].set(owners, mode='drop')
    index_table = jnp.zeros((POOL,), jnp.int32).at[position].set(indices, mode='drop')
    return (lengths, owner_table, index_table)


def draw_context_len(key, part):
    return layout(key)[0]


def draw_block_owner(key, part):
    return layout(key)[1]


def draw_block_index(key, part):
    return layout(key)[2]


def draw_states(key, part):
    split_keys = jax.random.split(jax.random.fold_in(key, 23), 2)
    column_scale = 3.0 ** (jnp.arange(D, dtype=jnp.float32) / D) * jax.random.uniform(split_keys[1], (1, D), jnp.float32, 0.5, 1.5)
    base = jnp.clip(jax.random.normal(split_keys[0], (REQS, D), jnp.float32), -6.0, 6.0)
    values = 0.25 * base * column_scale
    return values.astype(jnp.bfloat16)


def draw_cache(key, part):
    split_keys = jax.random.split(jax.random.fold_in(key, 37), 1)
    base = jnp.clip(jax.random.normal(split_keys[0], (POOL, 2, BLOCK_TOKENS, ATT_WIDTH), jnp.float32), -6.0, 6.0)
    return base.astype(jnp.bfloat16)


def level_of(rng, dims, pieces, low, high):
    loudness = 1.0
    for dim, parts in pieces:
        steps = jax.random.uniform(jax.random.fold_in(jax.random.fold_in(rng, 6), dim), (parts,), jnp.float32, low / len(pieces), high / len(pieces))
        loudness = loudness * jnp.repeat(jnp.exp(steps), dims[dim] // parts).reshape((-1,) + (1,) * (len(dims) - 1 - dim))
    return loudness


def noise(own_key, shape, scale, reach, cuts=(), kind=jnp.bfloat16):
    gain = level_of(own_key, shape, cuts, -0.22, 0.18) if cuts else 1.0
    drawn = jax.random.normal(own_key, shape, jnp.float32) * scale * gain
    return jnp.minimum(jnp.maximum(drawn, -reach), reach).astype(kind)


def setup_inputs(seed: int = 0) -> dict:
    splits = jax.random.split(jax.random.key(seed), 9)
    return {
        "states": draw_states(jax.random.fold_in(splits[8], 71), 0),
        "norm_gain": jnp.clip(1.0 + 0.15 * jax.random.normal(splits[1], (D,), jnp.float32), 0.25, 1.75).astype(jnp.bfloat16),
        "w_qkv": noise(splits[2], (3, D, ATT_WIDTH), D ** -0.5, 0.109375, ((1, 8), (2, 4))),
        "w_out": noise(splits[3], (ATT_WIDTH, D), ATT_WIDTH ** -0.5, 0.109375, ((0, 4), (1, 8))),
        "cache": draw_cache(jax.random.fold_in(splits[8], 71), 0),
        "context_len": draw_context_len(jax.random.fold_in(splits[8], 71), 0),
        "block_owner": draw_block_owner(jax.random.fold_in(splits[8], 71), 0),
        "block_index": draw_block_index(jax.random.fold_in(splits[8], 71), 0),
    }


EPSILON = 1e-05
NEG_FLOOR = -1e+30

def rotate(values, positions):
    half_dim = HEAD_DIM // 2
    frequency = 10000.0 ** (-jnp.arange(half_dim, dtype=jnp.float32) * 2.0 / HEAD_DIM)
    angles = positions.astype(jnp.float32)[:, None] * frequency[None, :]
    cosine = jnp.cos(angles)[:, None, :]
    sine_part = jnp.sin(angles)[:, None, :]
    front_half = values[..., :half_dim]
    back_half = values[..., half_dim:]
    return jnp.concatenate([front_half * cosine - back_half * sine_part, back_half * cosine + front_half * sine_part], axis=-1)

def finish(projected, positions):
    row_count = projected.shape[0]
    columns = projected.shape[2]
    head_count = columns // HEAD_DIM
    query = rotate(projected[:, 0].reshape(row_count, head_count, HEAD_DIM), positions) * HEAD_DIM ** (-0.5)
    keys_new = rotate(projected[:, 1].reshape(row_count, head_count, HEAD_DIM), positions)
    return (query.astype(jnp.bfloat16).reshape(row_count, columns), keys_new.astype(jnp.bfloat16).reshape(row_count, columns), projected[:, 2].astype(jnp.bfloat16))

def append(cache, keys_new, values_new, context_len, block_owner, block_index):
    requests = context_len.shape[0]
    tokens = cache.shape[2]
    block_live = block_owner < requests
    owner_row = jnp.minimum(block_owner, requests - 1)
    last_position = context_len[owner_row] - 1
    block_hit = block_live & (block_index == last_position // tokens)
    slot_hit = block_hit[:, None] & (jnp.arange(tokens, dtype=jnp.int32)[None, :] == (last_position % tokens)[:, None])
    fresh_rows = jnp.stack([keys_new[owner_row], values_new[owner_row]], axis=1)
    return jnp.where(slot_hit[:, None, :, None], fresh_rows[:, :, None, :], cache)

def partials(query, cache, context_len, block_owner, block_index):
    blocks, _, tokens, columns = cache.shape
    head_count = columns // HEAD_DIM
    requests = context_len.shape[0]
    block_live = block_owner < requests
    owner_row = jnp.minimum(block_owner, requests - 1)
    query_rows = query[owner_row].reshape(blocks, head_count, HEAD_DIM)
    key_cache = cache[:, 0].reshape(blocks, tokens, head_count, HEAD_DIM)
    value_cache = cache[:, 1].reshape(blocks, tokens, head_count, HEAD_DIM)
    scores = jnp.einsum('bhd,bthd->bht', query_rows.astype(jnp.float32), key_cache.astype(jnp.float32))
    token_position = block_index[:, None] * tokens + jnp.arange(tokens, dtype=jnp.int32)[None, :]
    visible = block_live[:, None] & (token_position < context_len[owner_row][:, None])
    masked = jnp.where(visible[:, None, :], scores, NEG_FLOOR)
    block_max = lax.optimization_barrier(jnp.max(masked, axis=-1))
    weights = jnp.where(visible[:, None, :], jnp.exp(masked - block_max[..., None]), 0.0).astype(jnp.bfloat16)
    block_sum = lax.optimization_barrier(jnp.sum(weights.astype(jnp.float32), axis=-1))
    block_out = jnp.einsum('bht,bthd->bhd', weights.astype(jnp.float32), value_cache.astype(jnp.float32)).reshape(blocks, columns)
    return (block_max, block_sum, block_out)

def reference(states, norm_gain, w_qkv, w_out, cache, context_len, block_owner, block_index):
    wide_states = states.astype(jnp.float32)
    inverse = lax.rsqrt(lax.optimization_barrier(jnp.mean(wide_states * wide_states, axis=1, keepdims=True)) + EPSILON)
    normed = (wide_states * inverse * norm_gain.astype(jnp.float32)[None, :]).astype(jnp.bfloat16)
    projected = jnp.stack([jnp.dot(normed, w_qkv[index_c], preferred_element_type=jnp.float32) for index_c in range(3)], axis=1)
    positions = context_len - 1
    query, keys_new, values_new = finish(projected, positions)
    updated = append(cache, keys_new, values_new, context_len, block_owner, block_index)
    shape_group = (N_SEQ, BLOCKS_DEV)

    def group_part(group):
        return partials(query, group[0], context_len, group[1], group[2])
    block_max, block_sum, block_out = lax.map(group_part, (updated.reshape(shape_group + updated.shape[1:]), block_owner.reshape(shape_group), block_index.reshape(shape_group)))
    block_max = block_max.reshape(POOL, -1)
    block_sum = block_sum.reshape(POOL, -1)
    block_out = block_out.reshape(POOL, -1)
    requests = context_len.shape[0]
    block_live = block_owner < requests
    owner_row = jnp.minimum(block_owner, requests - 1)
    segment = jnp.where(block_live, block_owner, requests).astype(jnp.int32)
    member = segment[:, None] == jnp.arange(requests, dtype=jnp.int32)[None, :]
    request_max = lax.optimization_barrier(jnp.max(jnp.where(member[:, :, None], block_max[:, None, :], NEG_FLOOR), axis=0))
    factor = jnp.exp(block_max - request_max[owner_row])
    totals = jax.ops.segment_sum(block_sum * factor, segment, requests + 1)[:requests]
    outputs = jax.ops.segment_sum(block_out * jnp.repeat(factor, HEAD_DIM, axis=1), segment, requests + 1)[:requests]
    attended = (outputs / jnp.repeat(totals, HEAD_DIM, axis=1)).astype(jnp.bfloat16)
    hidden = (jnp.dot(attended, w_out, preferred_element_type=jnp.float32) + wide_states).astype(jnp.bfloat16)
    return (hidden, updated)
```

```python
import functools

import jax
import jax.numpy as jnp
from jax import lax
from jax.experimental import pallas as pl
from jax.experimental.pallas import tpu as pltpu
from jax.sharding import PartitionSpec as P

HEAD_DIM = 96
EPSILON = 1e-05
NEG_FLOOR = -1e30
LANES = 128
GROUP = 4

VMEM = pltpu.MemorySpace.VMEM


def split3(value):
    high = value.astype(jnp.bfloat16).astype(jnp.float32)
    rest = value - high
    mid = rest.astype(jnp.bfloat16).astype(jnp.float32)
    low = (rest - mid).astype(jnp.bfloat16).astype(jnp.float32)
    return high, mid, low


def project_kernel(states_ref, gain_ref, w_ref, out_ref, w_buf, sems):
    parts = w_ref.shape[0]
    columns = w_ref.shape[2]
    peers, share, _ = out_ref.shape
    copies = [pltpu.make_async_copy(w_ref.at[c], w_buf.at[c], sems.at[c]) for c in range(parts)]
    for copy in copies:
        copy.start()
    wide = states_ref[...].astype(jnp.float32)
    scaled = (wide * gain_ref[...].astype(jnp.float32)).astype(jnp.bfloat16)
    squares = jnp.sum(wide * wide, axis=1, keepdims=True)
    high, mid, low = split3(squares)
    lane = lax.broadcasted_iota(jnp.int32, (wide.shape[0], LANES), 1)
    stat = jnp.where(lane == 0, high, jnp.where(lane == 1, mid, jnp.where(lane == 2, low, 0.0)))
    for d in range(peers):
        out_ref[d, :, parts * columns :] = stat[d * share : (d + 1) * share].astype(jnp.bfloat16)
    for c in range(parts):
        copies[c].wait()
        term = jnp.dot(scaled, w_buf[c], preferred_element_type=jnp.float32)
        for d in range(peers):
            out_ref[d, :, c * columns : (c + 1) * columns] = term[
                d * share : (d + 1) * share
            ].astype(jnp.bfloat16)


def finish_kernel(width, recv_ref, cos_ref, sin_ref, out_ref):
    peers, _, _ = recv_ref.shape
    columns = cos_ref.shape[1]
    total = recv_ref[0].astype(jnp.float32)
    for d in range(1, peers):
        total = total + recv_ref[d].astype(jnp.float32)
    squares = jnp.sum(total[:, 3 * columns :], axis=1, keepdims=True)
    inverse = lax.rsqrt(squares * (1.0 / width) + EPSILON)
    cosine = cos_ref[...]
    sine = sin_ref[...]
    half = HEAD_DIM // 2
    front = lax.broadcasted_iota(jnp.int32, cosine.shape, 1) % HEAD_DIM < half

    def rotated(x):
        other = jnp.where(front, -pltpu.roll(x, columns - half, 1), pltpu.roll(x, half, 1))
        return x * cosine + other * sine

    query = rotated(total[:, :columns] * inverse) * HEAD_DIM ** (-0.5)
    keys_new = rotated(total[:, columns : 2 * columns] * inverse)
    values_new = total[:, 2 * columns : 3 * columns] * inverse
    for d in range(peers):
        out_ref[d, :, :columns] = query.astype(jnp.bfloat16)
        out_ref[d, :, columns : 2 * columns] = keys_new.astype(jnp.bfloat16)
        out_ref[d, :, 2 * columns :] = values_new.astype(jnp.bfloat16)


def attend_kernel(
    qkv_ref, owner_ref, seen_ref, slot_ref, cache_ref, out_ref, updated_ref, rows_q, fresh, sums
):
    step = pl.program_id(0)
    requests = qkv_ref.shape[0]
    blocks = owner_ref.shape[0] // (HEADS := 8)
    group, _, tokens, columns = cache_ref.shape
    peers = out_ref.shape[0]
    lane_head = lax.broadcasted_iota(jnp.int32, (HEADS, columns), 1) // HEAD_DIM
    head_mask = lane_head == lax.broadcasted_iota(jnp.int32, (HEADS, columns), 0)

    @pl.when(step == 0)
    def _():
        pick = owner_ref[...] == lax.broadcasted_iota(jnp.int32, (blocks * HEADS, requests), 1)
        pick = pick.astype(jnp.float32).astype(jnp.bfloat16)
        own = jnp.dot(pick, qkv_ref[...], preferred_element_type=jnp.float32)
        own = own.reshape(blocks, HEADS, 3 * columns)
        rows = jnp.where(head_mask[None], own[:, :, :columns], 0.0)
        rows_q[...] = rows.reshape(blocks * HEADS, columns).astype(jnp.bfloat16)
        fresh[...] = own[:, 0, columns:]

    rows = group * HEADS
    seen = seen_ref[pl.ds(step * rows, rows), :]
    slots = slot_ref[pl.ds(step * rows, rows), :]
    token = lax.broadcasted_iota(jnp.int32, (tokens, columns), 0)
    keys, values = [], []
    for g in range(group):
        b = step * group + g
        hit = token == slots[g * HEADS : g * HEADS + 1, 0:1]
        row = fresh[pl.ds(b, 1), :]
        key = jnp.where(hit, row[:, :columns], cache_ref[g, 0].astype(jnp.float32))
        value = jnp.where(hit, row[:, columns:], cache_ref[g, 1].astype(jnp.float32))
        keys.append(key.astype(jnp.bfloat16))
        values.append(value.astype(jnp.bfloat16))
        updated_ref[g, 0] = keys[-1]
        updated_ref[g, 1] = values[-1]
    keys = jnp.concatenate(keys, axis=0)
    values = jnp.concatenate(values, axis=0)
    scores = lax.dot_general(
        rows_q[pl.ds(pl.multiple_of(step * rows, rows), rows), :],
        keys,
        (((1,), (1,)), ((), ())),
        preferred_element_type=jnp.float32,
    )
    column = lax.broadcasted_iota(jnp.int32, scores.shape, 1)
    row = lax.broadcasted_iota(jnp.int32, scores.shape, 0)
    visible = (column // tokens == row // HEADS) & (column % tokens < seen)
    masked = jnp.where(visible, scores, NEG_FLOOR)
    top = jnp.max(masked, axis=1, keepdims=True)
    weights = jnp.where(visible, jnp.exp(masked - top), 0.0).astype(jnp.bfloat16)
    mass = jnp.sum(weights.astype(jnp.float32), axis=1, keepdims=True)
    part = jnp.dot(weights, values, preferred_element_type=jnp.float32)
    part = part * jnp.where(mass > 0.0, 1.0 / mass, 0.0)
    part = jnp.where(head_mask[None], part.reshape(group, HEADS, columns), 0.0)
    part = jnp.sum(part, axis=1)
    lane = lax.broadcasted_iota(jnp.int32, (rows, LANES), 1)
    head = lax.broadcasted_iota(jnp.int32, (rows, LANES), 0) % HEADS
    stat = jnp.zeros((rows, LANES), jnp.float32)
    for j, term in enumerate(split3(top) + split3(mass)):
        stat = jnp.where(lane == head + j * HEADS, term, stat)
    owner = owner_ref[pl.ds(step * rows, rows), :].astype(jnp.float32)
    stat = jnp.where((lane == 6 * HEADS) & (head == 0), owner, stat)
    stat = jnp.sum(stat.reshape(group, HEADS, LANES), axis=1)
    sums[step, :, :columns] = part
    sums[step, :, columns:] = stat

    @pl.when(step == pl.num_programs(0) - 1)
    def _():
        whole = sums[...].reshape(blocks, columns + LANES).astype(jnp.bfloat16)
        for d in range(peers):
            out_ref[d] = whole


def output_kernel(place_ref, recv_ref, w_ref, states_ref, own_ref, *rest):
    sends, product = rest[:-1], rest[-1]
    heads = 8
    peers, blocks, wide = recv_ref.shape
    columns = wide - LANES
    requests = states_ref.shape[0]
    total_blocks = peers * blocks
    both = recv_ref[...].astype(jnp.float32).reshape(total_blocks, wide).astype(jnp.bfloat16)
    parts, stat = both[:, :columns], both[:, columns:]
    row = lax.broadcasted_iota(jnp.int32, (3 * heads, LANES), 0)
    lane = lax.broadcasted_iota(jnp.int32, (3 * heads, LANES), 1)
    wanted = (row // heads == lane // (3 * heads)) & (row % heads == lane % heads)
    wanted = (wanted & (row < 2 * heads)) | ((row >= 2 * heads) & (lane == 6 * heads))
    stat = lax.dot_general(
        wanted.astype(jnp.float32).astype(jnp.bfloat16),
        stat,
        (((1,), (1,)), ((), ())),
        preferred_element_type=jnp.float32,
    )
    owner = stat[2 * heads : 2 * heads + 1]
    request = lax.broadcasted_iota(jnp.int32, (requests, total_blocks), 0).astype(jnp.float32)
    member = owner == request
    lane_head = lax.broadcasted_iota(jnp.int32, (requests, columns), 1) // HEAD_DIM
    attended = jnp.zeros((requests, columns), jnp.float32)
    for h in range(heads):
        top = jnp.where(member, stat[h : h + 1], NEG_FLOOR)
        highest = jnp.max(top, axis=1, keepdims=True)
        factor = jnp.where(member, jnp.exp(top - highest) * stat[heads + h : heads + h + 1], 0.0)
        factor = factor / jnp.sum(factor, axis=1, keepdims=True)
        joined = jnp.dot(factor.astype(jnp.bfloat16), parts, preferred_element_type=jnp.float32)
        attended = jnp.where(lane_head == h, joined, attended)
    product[...] = jnp.dot(
        attended.astype(jnp.bfloat16), w_ref[...], preferred_element_type=jnp.float32
    )
    place = place_ref[0]
    share = own_ref.shape[0]
    mine = pl.ds(pl.multiple_of(place * share, share), share)
    own_ref[...] = product[mine, :] + states_ref[mine, :].astype(jnp.float32)
    for m, send in enumerate(sends, 1):
        theirs = pl.ds(pl.multiple_of((place ^ m) * share, share), share)
        send[...] = product[theirs, :].astype(send.dtype)


def shards(states, norm_gain, w_qkv, w_out, cache, context_len, block_owner, block_index):
    requests, depth = states.shape
    peers = lax.axis_size("seq")
    ranks = lax.axis_size("tp")
    parts, _, columns = w_qkv.shape
    blocks, _, tokens, _ = cache.shape
    heads = columns // HEAD_DIM
    share = requests // peers
    out_columns = w_out.shape[1]
    limit = pltpu.CompilerParams(vmem_limit_bytes=40 * 1024 * 1024)

    terms = pl.pallas_call(
        project_kernel,
        out_shape=jax.ShapeDtypeStruct((peers, share, parts * columns + LANES), jnp.bfloat16),
        in_specs=[
            pl.BlockSpec(memory_space=VMEM),
            pl.BlockSpec(memory_space=VMEM),
            pl.BlockSpec(memory_space=pl.ANY),
        ],
        out_specs=pl.BlockSpec(memory_space=VMEM),
        scratch_shapes=[
            pltpu.VMEM((parts, depth, columns), jnp.bfloat16),
            pltpu.SemaphoreType.DMA((parts,)),
        ],
        compiler_params=limit,
        name="project",
    )(states, norm_gain.reshape(1, depth), w_qkv)
    received = lax.all_to_all(terms, "seq", split_axis=0, concat_axis=0, tiled=True)

    positions = lax.dynamic_slice_in_dim(context_len, lax.axis_index("seq") * share, share) - 1
    half = HEAD_DIM // 2
    pair = (jnp.arange(columns, dtype=jnp.int32) % half).astype(jnp.float32)
    frequency = 10000.0 ** (-pair * 2.0 / HEAD_DIM)
    angles = positions.astype(jnp.float32)[:, None] * frequency[None, :]
    shown = pl.pallas_call(
        functools.partial(finish_kernel, depth * peers),
        out_shape=jax.ShapeDtypeStruct((peers, share, parts * columns), jnp.bfloat16),
        compiler_params=limit,
        name="finish",
    )(received, jnp.cos(angles), jnp.sin(angles))
    qkv = lax.all_to_all(shown, "seq", split_axis=0, concat_axis=0, tiled=True)
    qkv = qkv.reshape(requests, parts * columns)

    live = block_owner < requests
    length = context_len[jnp.minimum(block_owner, requests - 1)]
    seen = jnp.where(live, jnp.clip(length - block_index * tokens, 0, tokens), 0)
    last = live & (block_index == (length - 1) // tokens)
    slot = jnp.where(last, (length - 1) % tokens, -1)

    def by_head(value):
        return jnp.repeat(value.astype(jnp.int32), heads)[:, None]

    steps = blocks // GROUP
    joined = pl.BlockSpec((GROUP, 2, tokens, columns), lambda i: (i, 0, 0, 0))
    whole = [
        pl.BlockSpec((requests, parts * columns), lambda i: (0, 0)),
        pl.BlockSpec((blocks * heads, 1), lambda i: (0, 0)),
        pl.BlockSpec((blocks * heads, 1), lambda i: (0, 0)),
        pl.BlockSpec((blocks * heads, 1), lambda i: (0, 0)),
    ]
    partial_rows, updated = pl.pallas_call(
        attend_kernel,
        grid=(steps,),
        out_shape=(
            jax.ShapeDtypeStruct((peers, blocks, columns + LANES), jnp.bfloat16),
            jax.ShapeDtypeStruct(cache.shape, cache.dtype),
        ),
        in_specs=whole + [joined],
        out_specs=(
            pl.BlockSpec((peers, blocks, columns + LANES), lambda i: (0, 0, 0)),
            joined,
        ),
        scratch_shapes=[
            pltpu.VMEM((blocks * heads, columns), jnp.bfloat16),
            pltpu.VMEM((blocks, 2 * columns), jnp.float32),
            pltpu.VMEM((steps, GROUP, columns + LANES), jnp.float32),
        ],
        compiler_params=limit,
        name="attend",
    )(qkv, by_head(block_owner), by_head(seen), by_head(slot), cache)
    gathered = lax.all_to_all(partial_rows, "seq", split_axis=0, concat_axis=0, tiled=True)

    place = lax.axis_index("tp")
    rows = requests // ranks
    own, *sends = pl.pallas_call(
        output_kernel,
        out_shape=tuple(
            jax.ShapeDtypeStruct((rows, out_columns), jnp.float32) for _ in range(ranks)
        ),
        in_specs=[pl.BlockSpec(memory_space=pltpu.MemorySpace.SMEM)]
        + [pl.BlockSpec(memory_space=VMEM)] * 3,
        out_specs=tuple(pl.BlockSpec(memory_space=VMEM) for _ in range(ranks)),
        scratch_shapes=[pltpu.VMEM((requests, out_columns), jnp.float32)],
        compiler_params=limit,
        name="output",
    )(place.reshape(1).astype(jnp.int32), gathered, w_out, states)
    total = own
    for m, send in enumerate(sends, 1):
        total = total + lax.ppermute(send, "tp", [(i, i ^ m) for i in range(ranks)])
    return (total.astype(jnp.bfloat16), updated)


def solution(mesh):
    return jax.shard_map(
        shards,
        mesh=mesh,
        in_specs=(
            P(None, "seq"),
            P("seq"),
            P(None, "seq", "tp"),
            P("tp", "seq"),
            P("seq", None, None, "tp"),
            P(),
            P("seq"),
            P("seq"),
        ),
        out_specs=(P("tp", "seq"), P("seq", None, None, "tp")),
        check_vma=False,
    )
```

```python
import functools

import jax
import jax.numpy as jnp
from jax import lax
from jax.experimental import pallas as pl
from jax.experimental.pallas import tpu as pltpu
from jax.sharding import PartitionSpec as P

HEAD_DIM = 96
EPSILON = 1e-05
NEG_FLOOR = -1e30
LANES = 128
GROUP = 4

VMEM = pltpu.MemorySpace.VMEM
HBM = pltpu.MemorySpace.HBM
SMEM = pltpu.MemorySpace.SMEM
HEADS = 8
ROWS = 16


def split3(value):
    high = value.astype(jnp.bfloat16).astype(jnp.float32)
    rest = value - high
    mid = rest.astype(jnp.bfloat16).astype(jnp.float32)
    low = (rest - mid).astype(jnp.bfloat16).astype(jnp.float32)
    return high, mid, low


def project_kernel(states_ref, gain_ref, w_ref, out_ref, states_buf, gain_buf, w_buf, sems):
    parts = w_ref.shape[0]
    columns = w_ref.shape[2]
    peers, share, _ = out_ref.shape
    small = [
        pltpu.make_async_copy(states_ref, states_buf, sems.at[parts]),
        pltpu.make_async_copy(gain_ref, gain_buf, sems.at[parts + 1]),
    ]
    copies = [pltpu.make_async_copy(w_ref.at[c], w_buf.at[c], sems.at[c]) for c in range(parts)]
    for copy in small + copies:
        copy.start()
    for copy in small:
        copy.wait()
    wide = states_buf[...].astype(jnp.float32)
    gain = gain_buf[...].astype(jnp.float32)
    scaled = (wide * gain.reshape(1, wide.shape[1])).astype(jnp.bfloat16)
    squares = jnp.sum(wide * wide, axis=1, keepdims=True)
    high, mid, low = split3(squares)
    lane = lax.broadcasted_iota(jnp.int32, (wide.shape[0], LANES), 1)
    stat = jnp.where(lane == 0, high, jnp.where(lane == 1, mid, jnp.where(lane == 2, low, 0.0)))
    for d in range(peers):
        out_ref[d, :, parts * columns :] = stat[d * share : (d + 1) * share].astype(jnp.bfloat16)
    for c in range(parts):
        copies[c].wait()
        term = jnp.dot(scaled, w_buf[c], preferred_element_type=jnp.float32)
        for d in range(peers):
            out_ref[d, :, c * columns : (c + 1) * columns] = term[
                d * share : (d + 1) * share
            ].astype(jnp.bfloat16)


def finish_kernel(width, recv_ref, cos_ref, sin_ref, out_ref):
    peers, _, _ = recv_ref.shape
    columns = cos_ref.shape[1]
    total = recv_ref[0].astype(jnp.float32)
    for d in range(1, peers):
        total = total + recv_ref[d].astype(jnp.float32)
    squares = jnp.sum(total[:, 3 * columns :], axis=1, keepdims=True)
    inverse = lax.rsqrt(squares * (1.0 / width) + EPSILON)
    cosine = cos_ref[...]
    sine = sin_ref[...]
    half = HEAD_DIM // 2
    front = lax.broadcasted_iota(jnp.int32, cosine.shape, 1) % HEAD_DIM < half

    def rotated(x):
        other = jnp.where(front, -pltpu.roll(x, columns - half, 1), pltpu.roll(x, half, 1))
        return x * cosine + other * sine

    query = rotated(total[:, :columns] * inverse) * HEAD_DIM ** (-0.5)
    keys_new = rotated(total[:, columns : 2 * columns] * inverse)
    values_new = total[:, 2 * columns : 3 * columns] * inverse
    for d in range(peers):
        out_ref[d, :, :columns] = query.astype(jnp.bfloat16)
        out_ref[d, :, columns : 2 * columns] = keys_new.astype(jnp.bfloat16)
        out_ref[d, :, 2 * columns :] = values_new.astype(jnp.bfloat16)


def stage_kernel(cache_ref, keys_ref, sem):
    copy = pltpu.make_async_copy(cache_ref.at[:, 0], keys_ref, sem)
    copy.start()
    copy.wait()


def read_block(b, owner_ref, index_ref, length_ref, tokens):
    requests = length_ref.shape[0]
    owner = owner_ref[b]
    reach = length_ref[jnp.minimum(owner, requests - 1)] - index_ref[b] * tokens
    live = owner < requests
    seen = jnp.where(live, jnp.clip(reach, 0, tokens), 0)
    slot = jnp.where(live & (reach >= 1) & (reach <= tokens), reach - 1, -1)
    return owner, seen, slot


def plan_kernel(
    tokens, owner_ref, index_ref, length_ref, pick_ref, single_ref, seen_ref, slot_ref, name_ref
):
    blocks = owner_ref.shape[0]
    requests = pick_ref.shape[1]
    padded = single_ref.shape[0]
    lane = lax.broadcasted_iota(jnp.int32, (HEADS, requests), 1)
    sole = lax.broadcasted_iota(jnp.int32, (padded, requests), 0)
    wide = lax.broadcasted_iota(jnp.int32, (padded, requests), 1)
    single = jnp.zeros((padded, requests), jnp.float32)
    picks = []
    for b in range(blocks):
        owner, seen, slot = read_block(b, owner_ref, index_ref, length_ref, tokens)
        here = pl.ds(b * HEADS, HEADS)
        picks.append((lane == owner).astype(jnp.float32))
        single = jnp.where((sole == b) & (wide == owner), 1.0, single)
        seen_ref[here, :] = jnp.full((HEADS, LANES), seen, jnp.int32)
        slot_ref[here, :] = jnp.full((HEADS, LANES), slot, jnp.int32)
        name_ref[here, :] = jnp.full((HEADS, LANES), owner, jnp.int32).astype(jnp.float32)
    pick_ref[...] = jnp.concatenate(picks, axis=0).astype(jnp.bfloat16)
    single_ref[...] = single.astype(jnp.bfloat16)


def attend_kernel(
    qkv_ref, pick_ref, single_ref, seen_ref, slot_ref, name_ref, keys_ref, cache_ref, out_ref, token_ref, near, sems
):
    blocks, _, tokens, columns = cache_ref.shape
    peers = out_ref.shape[0]
    steps = blocks // GROUP
    copies = [
        pltpu.make_async_copy(
            cache_ref.at[pl.ds(step * GROUP, GROUP), 1],
            near.at[pl.ds(step * GROUP, GROUP)],
            sems.at[step],
        )
        for step in range(steps)
    ]
    for copy in copies:
        copy.start()
    token_ref[...] = jnp.zeros_like(token_ref)

    def iota(shape, dim):
        return lax.broadcasted_iota(jnp.int32, shape, dim)

    def one_hot(hit):
        return hit.astype(jnp.float32).astype(jnp.bfloat16)

    rows = blocks * HEADS
    padded = single_ref.shape[0]
    own = jnp.dot(pick_ref[...], qkv_ref[:, :columns], preferred_element_type=jnp.float32)
    head_mask = iota((rows, columns), 1) // HEAD_DIM == iota((rows, columns), 0) % HEADS
    queries = jnp.where(head_mask, own, 0.0).astype(jnp.bfloat16)
    fresh = jnp.dot(single_ref[...], qkv_ref[:, columns:], preferred_element_type=jnp.float32)
    fresh = fresh.astype(jnp.bfloat16)
    contract = (((1,), (1,)), ((), ()))
    mine = iota((rows, padded), 1) == iota((rows, padded), 0) // HEADS
    newest = lax.dot_general(
        queries, fresh[:, :columns], contract, preferred_element_type=jnp.float32
    )
    newest = jnp.sum(jnp.where(mine, newest, 0.0), axis=1, keepdims=True)

    size = GROUP * HEADS
    width = GROUP * tokens
    scores = []
    for step in range(steps):
        keys = keys_ref[step * GROUP : (step + 1) * GROUP].reshape(width, columns)
        scores.append(
            lax.dot_general(
                queries[step * size : (step + 1) * size],
                keys,
                contract,
                preferred_element_type=jnp.float32,
            )
        )
    scores = jnp.concatenate(scores, axis=0)
    column = iota((rows, width), 1)
    same = column // tokens == iota((rows, width), 0) // HEADS % GROUP
    place = jnp.where(same, column % tokens, tokens)

    def across(value):
        return jnp.concatenate([value] * (width // LANES), axis=1)

    latest = place == across(slot_ref[...])
    visible = place < across(seen_ref[...])
    masked = jnp.where(visible, jnp.where(latest, newest, scores), NEG_FLOOR)
    top = jnp.max(masked, axis=1, keepdims=True)
    weights = jnp.where(visible, jnp.exp(masked - top), 0.0)
    weights = weights.astype(jnp.bfloat16).astype(jnp.float32)
    mass = jnp.sum(weights, axis=1, keepdims=True)
    last = jnp.sum(jnp.where(latest, weights, 0.0), axis=1, keepdims=True)
    weights = jnp.where(latest, 0.0, weights).astype(jnp.bfloat16)
    last = jnp.where(mine, last, 0.0).astype(jnp.bfloat16)
    parts = []
    for step in range(steps):
        copies[step].wait()
        values = near[step * GROUP : (step + 1) * GROUP].reshape(width, columns)
        parts.append(
            jnp.dot(
                weights[step * size : (step + 1) * size],
                values,
                preferred_element_type=jnp.float32,
            )
        )
    part = jnp.concatenate(parts, axis=0)
    part = part + jnp.dot(last, fresh[:, columns:], preferred_element_type=jnp.float32)
    part = part * jnp.where(mass > 0.0, 1.0 / mass, 0.0)
    part = jnp.where(head_mask, part, 0.0).astype(jnp.bfloat16)
    lane = iota((rows, LANES), 1)
    head = iota((rows, LANES), 0) % HEADS
    stat = jnp.where((lane == 6 * HEADS) & (head == 0), name_ref[...], 0.0)
    for j, term in enumerate(split3(top) + split3(mass)):
        stat = jnp.where(lane == head + j * HEADS, term, stat)
    fold = one_hot(iota((padded, rows), 1) // HEADS == iota((padded, rows), 0))
    part = jnp.dot(fold, part, preferred_element_type=jnp.float32)
    stat = jnp.dot(fold, stat.astype(jnp.bfloat16), preferred_element_type=jnp.float32)
    part = part[:blocks].astype(jnp.bfloat16)
    stat = stat[:blocks].astype(jnp.bfloat16)
    for d in range(peers):
        out_ref[d, :, :columns] = part
        out_ref[d, :, columns:] = stat


def append_kernel(
    owner_ref,
    index_ref,
    length_ref,
    qkv_ref,
    token_ref,
    cache_ref,
    updated_ref,
    end_ref,
    wide,
    near,
    loads,
    stores,
):
    blocks, _, tokens, columns = cache_ref.shape
    requests = qkv_ref.shape[0]
    steps = blocks // GROUP

    def load(step):
        part = pl.ds(step * GROUP, GROUP)
        return pltpu.make_async_copy(cache_ref.at[part], near.at[part], loads.at[step])

    def store(step):
        part = pl.ds(step * GROUP, GROUP)
        return pltpu.make_async_copy(near.at[part], updated_ref.at[part], stores.at[step])

    for step in range(steps):
        load(step).start()
    end_ref[...] = jnp.zeros_like(end_ref)
    wide[...] = qkv_ref[:, columns:].astype(jnp.float32)
    row = lax.broadcasted_iota(jnp.int32, (ROWS, columns), 0)

    def change(b, owner, slot):
        first = pl.multiple_of(slot // ROWS * ROWS, ROWS)
        fresh = wide[pl.ds(jnp.minimum(owner, requests - 1), 1), :]
        hit = row == slot - first
        for c in range(2):
            old = near[b, c, pl.ds(first, ROWS), :].astype(jnp.float32)
            both = jnp.where(hit, fresh[:, c * columns : (c + 1) * columns], old)
            near[b, c, pl.ds(first, ROWS), :] = both.astype(jnp.bfloat16)

    for step in range(steps):
        load(step).wait()
        for b in range(step * GROUP, (step + 1) * GROUP):
            owner, _, slot = read_block(b, owner_ref, index_ref, length_ref, tokens)
            pl.when(slot >= 0)(functools.partial(change, b, owner, slot))
        store(step).start()
    for step in range(steps):
        store(step).wait()


def output_kernel(place_ref, token_ref, recv_ref, w_ref, states_ref, own_ref, *rest):
    sends, product = rest[:-1], rest[-1]
    heads = HEADS
    peers, blocks, wide = recv_ref.shape
    columns = wide - LANES
    requests = states_ref.shape[0]
    total_blocks = peers * blocks
    both = recv_ref[...].astype(jnp.float32).reshape(total_blocks, wide).astype(jnp.bfloat16)
    parts, stat = both[:, :columns], both[:, columns:]
    row = lax.broadcasted_iota(jnp.int32, (3 * heads, LANES), 0)
    lane = lax.broadcasted_iota(jnp.int32, (3 * heads, LANES), 1)
    wanted = (row // heads == lane // (3 * heads)) & (row % heads == lane % heads)
    wanted = (wanted & (row < 2 * heads)) | ((row >= 2 * heads) & (lane == 6 * heads))
    stat = lax.dot_general(
        wanted.astype(jnp.float32).astype(jnp.bfloat16),
        stat,
        (((1,), (1,)), ((), ())),
        preferred_element_type=jnp.float32,
    )
    owner = stat[2 * heads : 2 * heads + 1]
    request = lax.broadcasted_iota(jnp.int32, (requests, total_blocks), 0).astype(jnp.float32)
    member = owner == request
    lane_head = lax.broadcasted_iota(jnp.int32, (requests, columns), 1) // HEAD_DIM
    attended = jnp.zeros((requests, columns), jnp.float32)
    for h in range(heads):
        top = jnp.where(member, stat[h : h + 1], NEG_FLOOR)
        highest = jnp.max(top, axis=1, keepdims=True)
        factor = jnp.where(member, jnp.exp(top - highest) * stat[heads + h : heads + h + 1], 0.0)
        factor = factor / jnp.sum(factor, axis=1, keepdims=True)
        joined = jnp.dot(factor.astype(jnp.bfloat16), parts, preferred_element_type=jnp.float32)
        attended = jnp.where(lane_head == h, joined, attended)
    product[...] = jnp.dot(
        attended.astype(jnp.bfloat16), w_ref[...], preferred_element_type=jnp.float32
    )
    place = place_ref[0]
    share = own_ref.shape[0]
    mine = pl.ds(pl.multiple_of(place * share, share), share)
    own_ref[...] = product[mine, :] + states_ref[mine, :].astype(jnp.float32)
    for m, send in enumerate(sends, 1):
        theirs = pl.ds(pl.multiple_of((place ^ m) * share, share), share)
        send[...] = product[theirs, :].astype(send.dtype)


def shards(states, norm_gain, w_qkv, w_out, cache, context_len, block_owner, block_index):
    requests, depth = states.shape
    peers = lax.axis_size("seq")
    ranks = lax.axis_size("tp")
    parts, _, columns = w_qkv.shape
    blocks, _, tokens, _ = cache.shape
    share = requests // peers
    out_columns = w_out.shape[1]
    limit = pltpu.CompilerParams(vmem_limit_bytes=24 * 1024 * 1024)
    most_room = pltpu.CompilerParams(vmem_limit_bytes=50 * 1024 * 1024)
    all_room = pltpu.CompilerParams(vmem_limit_bytes=60 * 1024 * 1024)

    terms = pl.pallas_call(
        project_kernel,
        out_shape=jax.ShapeDtypeStruct((peers, share, parts * columns + LANES), jnp.bfloat16),
        in_specs=[pl.BlockSpec(memory_space=HBM)] * 3,
        out_specs=pl.BlockSpec(memory_space=VMEM),
        scratch_shapes=[
            pltpu.VMEM(states.shape, jnp.bfloat16),
            pltpu.VMEM(norm_gain.shape, jnp.bfloat16),
            pltpu.VMEM((parts, depth, columns), jnp.bfloat16),
            pltpu.SemaphoreType.DMA((parts + 2,)),
        ],
        compiler_params=all_room,
        name="project",
    )(states, norm_gain, w_qkv)
    received = lax.all_to_all(terms, "seq", split_axis=0, concat_axis=0, tiled=True)

    positions = lax.dynamic_slice_in_dim(context_len, lax.axis_index("seq") * share, share) - 1
    half = HEAD_DIM // 2
    pair = (jnp.arange(columns, dtype=jnp.int32) % half).astype(jnp.float32)
    frequency = 10000.0 ** (-pair * 2.0 / HEAD_DIM)
    angles = positions.astype(jnp.float32)[:, None] * frequency[None, :]
    shown = pl.pallas_call(
        functools.partial(finish_kernel, depth * peers),
        out_shape=jax.ShapeDtypeStruct((peers, share, parts * columns), jnp.bfloat16),
        compiler_params=limit,
        name="finish",
    )(received, jnp.cos(angles), jnp.sin(angles))
    qkv = lax.all_to_all(shown, "seq", split_axis=0, concat_axis=0, tiled=True)
    qkv = qkv.reshape(requests, parts * columns)

    table = (block_owner, block_index, context_len)
    padded = blocks + -blocks % 16
    rows = blocks * HEADS
    plan = pl.pallas_call(
        functools.partial(plan_kernel, tokens),
        out_shape=(
            jax.ShapeDtypeStruct((rows, requests), jnp.bfloat16),
            jax.ShapeDtypeStruct((padded, requests), jnp.bfloat16),
            jax.ShapeDtypeStruct((rows, LANES), jnp.int32),
            jax.ShapeDtypeStruct((rows, LANES), jnp.int32),
            jax.ShapeDtypeStruct((rows, LANES), jnp.float32),
        ),
        in_specs=[pl.BlockSpec(memory_space=SMEM)] * 3,
        compiler_params=limit,
        name="plan",
    )(*table)
    keys = pl.pallas_call(
        stage_kernel,
        out_shape=jax.ShapeDtypeStruct((blocks, tokens, columns), cache.dtype),
        in_specs=[pl.BlockSpec(memory_space=HBM)],
        out_specs=pl.BlockSpec(memory_space=VMEM),
        scratch_shapes=[pltpu.SemaphoreType.DMA],
        compiler_params=most_room,
        name="stage",
    )(cache)
    partial_rows, token = pl.pallas_call(
        attend_kernel,
        out_shape=(
            jax.ShapeDtypeStruct((peers, blocks, columns + LANES), jnp.bfloat16),
            jax.ShapeDtypeStruct((8, LANES), jnp.float32),
        ),
        in_specs=[pl.BlockSpec(memory_space=VMEM)] * 7 + [pl.BlockSpec(memory_space=HBM)],
        scratch_shapes=[
            pltpu.VMEM((blocks, tokens, columns), jnp.bfloat16),
            pltpu.SemaphoreType.DMA((blocks // GROUP,)),
        ],
        compiler_params=most_room,
        name="attend",
    )(qkv, *plan, keys, cache)
    updated, token = pl.pallas_call(
        append_kernel,
        out_shape=(
            jax.ShapeDtypeStruct(cache.shape, cache.dtype),
            jax.ShapeDtypeStruct((8, LANES), jnp.float32),
        ),
        in_specs=[pl.BlockSpec(memory_space=SMEM)] * 3
        + [pl.BlockSpec(memory_space=VMEM), pl.BlockSpec(memory_space=pl.ANY)]
        + [pl.BlockSpec(memory_space=HBM)],
        out_specs=(pl.BlockSpec(memory_space=HBM), pl.BlockSpec(memory_space=VMEM)),
        scratch_shapes=[
            pltpu.VMEM((requests, 2 * columns), jnp.float32),
            pltpu.VMEM(cache.shape, jnp.bfloat16),
            pltpu.SemaphoreType.DMA((blocks // GROUP,)),
            pltpu.SemaphoreType.DMA((blocks // GROUP,)),
        ],
        compiler_params=most_room,
        cost_estimate=pl.CostEstimate(flops=0, bytes_accessed=2 * cache.size * 2, transcendentals=0),
        name="append",
    )(*table, qkv, token, cache)
    gathered = lax.all_to_all(partial_rows, "seq", split_axis=0, concat_axis=0, tiled=True)

    place = lax.axis_index("tp")
    kept = requests // ranks
    own, *sends = pl.pallas_call(
        output_kernel,
        out_shape=tuple(
            jax.ShapeDtypeStruct((kept, out_columns), jnp.float32) for _ in range(ranks)
        ),
        in_specs=[pl.BlockSpec(memory_space=SMEM), pl.BlockSpec(memory_space=pl.ANY)]
        + [pl.BlockSpec(memory_space=VMEM)] * 3,
        out_specs=tuple(pl.BlockSpec(memory_space=VMEM) for _ in range(ranks)),
        scratch_shapes=[pltpu.VMEM((requests, out_columns), jnp.float32)],
        compiler_params=limit,
        name="output",
    )(place.reshape(1).astype(jnp.int32), token, gathered, w_out, states)
    total = own
    for m, send in enumerate(sends, 1):
        total = total + lax.ppermute(send, "tp", [(i, i ^ m) for i in range(ranks)])
    return (total.astype(jnp.bfloat16), updated)


def solution(mesh):
    return jax.shard_map(
        shards,
        mesh=mesh,
        in_specs=(
            P(None, "seq"),
            P("seq"),
            P(None, "seq", "tp"),
            P("tp", "seq"),
            P("seq", None, None, "tp"),
            P(),
            P("seq"),
            P("seq"),
        ),
        out_specs=(P("tp", "seq"), P("seq", None, None, "tp")),
        check_vma=False,
    )
```

```python
import functools

import jax
import jax.numpy as jnp
from jax import lax
from jax.experimental import pallas as pl
from jax.experimental.pallas import tpu as pltpu
from jax.sharding import PartitionSpec as P

HEAD_DIM = 96
EPSILON = 1e-05
NEG_FLOOR = -1e30
LANES = 128
GROUP = 4

VMEM = pltpu.MemorySpace.VMEM
HBM = pltpu.MemorySpace.HBM
SMEM = pltpu.MemorySpace.SMEM
HEADS = 8
ROWS = 16


def split3(value):
    high = value.astype(jnp.bfloat16).astype(jnp.float32)
    rest = value - high
    mid = rest.astype(jnp.bfloat16).astype(jnp.float32)
    low = (rest - mid).astype(jnp.bfloat16).astype(jnp.float32)
    return high, mid, low


def lanes_of(terms):
    lane = lax.broadcasted_iota(jnp.int32, (terms[0].shape[0], LANES), 1)
    out = jnp.zeros(lane.shape, jnp.float32)
    for j, term in enumerate(terms):
        out = jnp.where(lane == j, term, out)
    return out


def project_kernel(
    place_ref, states_ref, gain_ref, w_ref, sent_ref, kept_ref, states_buf, gain_buf, w_buf, sems
):
    parts, _, columns = w_ref.shape
    half = sent_ref.shape[0]
    small = [
        pltpu.make_async_copy(states_ref, states_buf, sems.at[parts]),
        pltpu.make_async_copy(gain_ref, gain_buf, sems.at[parts + 1]),
    ]
    copies = [pltpu.make_async_copy(w_ref.at[c], w_buf.at[c], sems.at[c]) for c in range(parts)]
    for copy in small + copies:
        copy.start()
    for copy in small:
        copy.wait()
    side = place_ref[0] % 2
    rows = [
        states_buf[pl.ds(pl.multiple_of(first * half, half), half), :].astype(jnp.float32)
        for first in (1 - side, side)
    ]
    wide = jnp.concatenate(rows, axis=0)
    gain = gain_buf[...].astype(jnp.float32)
    scaled = (wide * gain.reshape(1, wide.shape[1])).astype(jnp.bfloat16)
    squares = jnp.sum(wide * wide, axis=1, keepdims=True)
    stat = lanes_of(split3(squares))
    sent_ref[:, parts * columns :] = stat[:half].astype(jnp.bfloat16)
    kept_ref[:, parts * columns :] = stat[half:]
    for c in range(parts):
        copies[c].wait()
        term = jnp.dot(scaled, w_buf[c], preferred_element_type=jnp.float32)
        here = slice(c * columns, (c + 1) * columns)
        sent_ref[:, here] = term[:half].astype(jnp.bfloat16)
        kept_ref[:, here] = term[half:]


def halve_kernel(place_ref, kept_ref, recv_ref, after_ref, *rest):
    sends, query_ref, fresh_ref, total = rest[:-3], rest[-3], rest[-2], rest[-1]
    columns = query_ref.shape[1] - LANES
    share = fresh_ref.shape[0]
    half = kept_ref.shape[0]
    total[...] = kept_ref[...] + recv_ref[...].astype(jnp.float32)
    squares = jnp.sum(total[:, 3 * columns :], axis=1, keepdims=True)
    stat = lanes_of(split3(squares))
    query_ref[:, :columns] = total[:, :columns]
    query_ref[:, columns:] = stat
    query = total[:, :columns].astype(jnp.bfloat16)
    stat = stat.astype(jnp.bfloat16)
    line = place_ref[0] // 2

    def rows_of(group):
        return total[pl.ds(pl.multiple_of(group * share, share), share), columns : 3 * columns]

    fresh_ref[...] = rows_of(line)
    for m, send in enumerate(sends, 1):
        other = rows_of(line ^ m)
        both = jnp.concatenate([other[:, :columns], other[:, columns:]], axis=0)
        send[:half, :columns] = query
        send[:half, columns:] = stat
        send[half:, :columns] = both.astype(jnp.bfloat16)
        send[half:, columns:] = jnp.zeros((2 * share, LANES), jnp.bfloat16)


def finish_kernel(width, place_ref, after_ref, query_ref, fresh_ref, cos_ref, sin_ref, *rest):
    received, out_ref, news_ref = rest[:-2], rest[-2], rest[-1]
    half, columns = out_ref.shape
    share = fresh_ref.shape[0]
    total = query_ref[...]
    fresh = fresh_ref[...]
    for piece in received:
        total = total + piece[:half, :].astype(jnp.float32)
        extra = piece[half:, :columns].astype(jnp.float32)
        fresh = fresh + jnp.concatenate([extra[:share], extra[share:]], axis=1)
    squares = jnp.sum(total[:, columns:], axis=1, keepdims=True)
    inverse = lax.rsqrt(squares * (1.0 / width) + EPSILON)
    span = HEAD_DIM // 2

    def rotated(x, cosine, sine):
        front = lax.broadcasted_iota(jnp.int32, x.shape, 1) % HEAD_DIM < span
        other = jnp.where(front, -pltpu.roll(x, columns - span, 1), pltpu.roll(x, span, 1))
        return x * cosine + other * sine

    query = rotated(total[:, :columns] * inverse, cos_ref[...], sin_ref[...])
    query = (query * HEAD_DIM ** (-0.5)).astype(jnp.bfloat16)
    out_ref[...] = query
    line = place_ref[0] // 2
    groups = half // share
    mine = jnp.zeros((share, columns), jnp.float32)
    scale = jnp.zeros((share, 1), jnp.float32)
    cosine, sine = mine, mine
    wide = query.astype(jnp.float32)
    for group in range(groups):
        here = slice(group * share, (group + 1) * share)
        mine = jnp.where(line == group, wide[here], mine)
        scale = jnp.where(line == group, inverse[here], scale)
        cosine = jnp.where(line == group, cos_ref[here, :], cosine)
        sine = jnp.where(line == group, sin_ref[here, :], sine)
    key = rotated(fresh[:, :columns] * scale, cosine, sine).astype(jnp.bfloat16)
    value = (fresh[:, columns:] * scale).astype(jnp.bfloat16)
    product = mine * key.astype(jnp.float32)
    lane_head = lax.broadcasted_iota(jnp.int32, product.shape, 1) // HEAD_DIM
    lane = lax.broadcasted_iota(jnp.int32, (share, LANES), 1)
    first = (place_ref[0] % 2) * half + line * share
    owner = lax.broadcasted_iota(jnp.int32, (share, LANES), 0) + first
    stat = jnp.where(lane == 6 * HEADS, owner.astype(jnp.float32), 0.0)
    for h in range(HEADS):
        score = jnp.sum(jnp.where(lane_head == h, product, 0.0), axis=1, keepdims=True)
        for j, term in enumerate(split3(score)):
            stat = jnp.where(lane == j * HEADS + h, term, stat)
        stat = jnp.where(lane == 3 * HEADS + h, 1.0, stat)
    none = jnp.where(lane == 6 * HEADS, -1.0, 0.0)
    both = jnp.concatenate([value.astype(jnp.float32), key.astype(jnp.float32)], axis=0)
    news_ref[:, :columns] = both.astype(jnp.bfloat16)
    news_ref[:, columns:] = jnp.concatenate([stat, none], axis=0).astype(jnp.bfloat16)


def stage_keys_kernel(cache_ref, keys_ref, updated_ref, loads, stores):
    steps = cache_ref.shape[0] // GROUP

    def load(step):
        part = pl.ds(step * GROUP, GROUP)
        return pltpu.make_async_copy(cache_ref.at[part, 0], keys_ref.at[part], loads.at[step])

    def store(step):
        part = pl.ds(step * GROUP, GROUP)
        return pltpu.make_async_copy(keys_ref.at[part], updated_ref.at[part, 0], stores.at[step])

    for step in range(steps):
        load(step).start()
    for step in range(steps):
        load(step).wait()
        store(step).start()
    for step in range(steps):
        store(step).wait()


def stage_values_kernel(cache_ref, held_ref, updated_ref, near, loads, stores):
    steps = cache_ref.shape[0] // GROUP

    def load(step):
        part = pl.ds(step * GROUP, GROUP)
        return pltpu.make_async_copy(cache_ref.at[part, 1], near.at[part], loads.at[step])

    def store(step):
        part = pl.ds(step * GROUP, GROUP)
        return pltpu.make_async_copy(near.at[part], updated_ref.at[part, 1], stores.at[step])

    for step in range(steps):
        load(step).start()
    for step in range(steps):
        load(step).wait()
        store(step).start()
    for step in range(steps):
        store(step).wait()


def read_block(b, owner_ref, index_ref, length_ref, tokens):
    requests = length_ref.shape[0]
    owner = owner_ref[b]
    reach = length_ref[jnp.minimum(owner, requests - 1)] - index_ref[b] * tokens
    live = owner < requests
    old = jnp.where(live, jnp.clip(reach - 1, 0, tokens), 0)
    slot = jnp.where(live & (reach >= 1) & (reach <= tokens), reach - 1, -1)
    return owner, old, slot


def plan_kernel(
    tokens,
    place_ref,
    owner_ref,
    index_ref,
    length_ref,
    mine_ref,
    other_ref,
    seen_ref,
    name_ref,
):
    blocks = owner_ref.shape[0]
    half = mine_ref.shape[1]
    side = place_ref[0] % 2
    lane = lax.broadcasted_iota(jnp.int32, (HEADS, half), 1)
    picks = [], []
    for b in range(blocks):
        owner, old, _ = read_block(b, owner_ref, index_ref, length_ref, tokens)
        here = pl.ds(b * HEADS, HEADS)
        for pick, first in zip(picks, (side, 1 - side)):
            pick.append((lane == owner - first * half).astype(jnp.float32))
        seen_ref[here, :] = jnp.full((HEADS, LANES), old, jnp.int32)
        name_ref[here, :] = jnp.full((HEADS, LANES), owner, jnp.int32).astype(jnp.float32)
    mine_ref[...] = jnp.concatenate(picks[0], axis=0).astype(jnp.bfloat16)
    other_ref[...] = jnp.concatenate(picks[1], axis=0).astype(jnp.bfloat16)


def attend_kernel(
    mine_ref,
    other_ref,
    pick_mine_ref,
    pick_other_ref,
    seen_ref,
    name_ref,
    news_ref,
    keys_ref,
    cache_ref,
    out_ref,
    near,
    sems,
):
    blocks, _, tokens, columns = cache_ref.shape
    extra = news_ref.shape[0]
    steps = blocks // GROUP
    copies = [
        pltpu.make_async_copy(
            cache_ref.at[pl.ds(step * GROUP, GROUP), 1],
            near.at[pl.ds(step * GROUP, GROUP)],
            sems.at[step],
        )
        for step in range(steps)
    ]
    for copy in copies:
        copy.start()
    out_ref[:extra, :] = news_ref[...]

    def iota(shape, dim):
        return lax.broadcasted_iota(jnp.int32, shape, dim)

    rows = blocks * HEADS
    size = GROUP * HEADS
    width = GROUP * tokens
    own = jnp.dot(pick_mine_ref[...], mine_ref[...], preferred_element_type=jnp.float32)
    own = own + jnp.dot(pick_other_ref[...], other_ref[...], preferred_element_type=jnp.float32)
    head_mask = iota((rows, columns), 1) // HEAD_DIM == iota((rows, columns), 0) % HEADS
    queries = jnp.where(head_mask, own, 0.0).astype(jnp.bfloat16)
    scores = []
    for step in range(steps):
        keys = keys_ref[step * GROUP : (step + 1) * GROUP].reshape(width, columns)
        scores.append(
            lax.dot_general(
                queries[step * size : (step + 1) * size],
                keys,
                (((1,), (1,)), ((), ())),
                preferred_element_type=jnp.float32,
            )
        )
    scores = jnp.concatenate(scores, axis=0)
    column = iota((rows, width), 1)
    same = column // tokens == iota((rows, width), 0) // HEADS % GROUP
    place = jnp.where(same, column % tokens, tokens)
    visible = place < jnp.concatenate([seen_ref[...]] * (width // LANES), axis=1)
    masked = jnp.where(visible, scores, NEG_FLOOR)
    top = jnp.max(masked, axis=1, keepdims=True)
    weights = jnp.where(visible, jnp.exp(masked - top), 0.0).astype(jnp.bfloat16)
    mass = jnp.sum(weights.astype(jnp.float32), axis=1, keepdims=True)
    parts = []
    for step in range(steps):
        copies[step].wait()
        values = near[step * GROUP : (step + 1) * GROUP].reshape(width, columns)
        parts.append(
            jnp.dot(
                weights[step * size : (step + 1) * size],
                values,
                preferred_element_type=jnp.float32,
            )
        )
    part = jnp.concatenate(parts, axis=0) * jnp.where(mass > 0.0, 1.0 / mass, 0.0)
    part = jnp.where(head_mask, part, 0.0).astype(jnp.bfloat16)
    lane = iota((rows, LANES), 1)
    head = iota((rows, LANES), 0) % HEADS
    stat = jnp.where((lane == 6 * HEADS) & (head == 0), name_ref[...], 0.0)
    for j, term in enumerate(split3(top) + split3(mass)):
        stat = jnp.where(lane == head + j * HEADS, term, stat)
    padded = blocks + -blocks % 16
    fold = iota((padded, rows), 1) // HEADS == iota((padded, rows), 0)
    fold = fold.astype(jnp.float32).astype(jnp.bfloat16)
    part = jnp.dot(fold, part, preferred_element_type=jnp.float32)
    stat = jnp.dot(fold, stat.astype(jnp.bfloat16), preferred_element_type=jnp.float32)
    out_ref[extra:, :columns] = part[:blocks].astype(jnp.bfloat16)
    out_ref[extra:, columns:] = stat[:blocks].astype(jnp.bfloat16)


def patch_kernel(count, place_ref, owner_ref, index_ref, length_ref, after_ref, *rest):
    pieces, cache_ref, held_ref, updated_ref = rest[:count], rest[count], rest[count + 1], rest[count + 2]
    fresh, patch, loads, stores = rest[count + 3 :]
    blocks, _, tokens, columns = cache_ref.shape
    requests = length_ref.shape[0]
    share = fresh.shape[1] // 2
    half = requests // 2

    def each(do):
        for b in range(blocks):
            owner, _, slot = read_block(b, owner_ref, index_ref, length_ref, tokens)
            first = pl.multiple_of(jnp.maximum(slot, 0) // ROWS * ROWS, ROWS)
            pl.when(slot >= 0)(functools.partial(do, b, owner, slot, first))

    def fetch(b, owner, slot, first):
        return pltpu.make_async_copy(
            cache_ref.at[b, :, pl.ds(first, ROWS), :], patch.at[b], loads.at[b]
        )

    def store(b, owner, slot, first):
        return pltpu.make_async_copy(
            patch.at[b], updated_ref.at[b, :, pl.ds(first, ROWS), :], stores.at[b]
        )

    each(lambda *at: fetch(*at).start())
    for m in range(count):
        fresh[m] = pieces[m][: 2 * share, :columns].astype(jnp.float32)
    row = lax.broadcasted_iota(jnp.int32, (ROWS, columns), 0)

    def change(b, owner, slot, first):
        fetch(b, owner, slot, first).wait()
        request = jnp.minimum(owner, requests - 1)
        device = request % half // share * 2 + request // half
        piece = place_ref[0] ^ device
        line = request % share
        for c in range(2):
            new = fresh[piece, pl.ds(line + (1 - c) * share, 1), :]
            old = patch[b, c].astype(jnp.float32)
            patch[b, c] = jnp.where(row == slot - first, new, old).astype(jnp.bfloat16)
        store(b, owner, slot, first).start()

    each(change)
    each(lambda *at: store(*at).wait())


def output_kernel(count, place_ref, *rest):
    pieces, w_ref, states_ref, own_ref = rest[:count], rest[count], rest[count + 1], rest[count + 2]
    sends, product = rest[count + 3 : -1], rest[-1]
    heads = HEADS
    blocks, wide = pieces[0].shape
    columns = wide - LANES
    requests = states_ref.shape[0]
    total_blocks = count * blocks
    both = [piece[...].astype(jnp.float32) for piece in pieces]
    both = jnp.concatenate(both, axis=0).astype(jnp.bfloat16)
    parts, stat = both[:, :columns], both[:, columns:]
    row = lax.broadcasted_iota(jnp.int32, (3 * heads, LANES), 0)
    lane = lax.broadcasted_iota(jnp.int32, (3 * heads, LANES), 1)
    wanted = (row // heads == lane // (3 * heads)) & (row % heads == lane % heads)
    wanted = (wanted & (row < 2 * heads)) | ((row >= 2 * heads) & (lane == 6 * heads))
    stat = lax.dot_general(
        wanted.astype(jnp.float32).astype(jnp.bfloat16),
        stat,
        (((1,), (1,)), ((), ())),
        preferred_element_type=jnp.float32,
    )
    owner = stat[2 * heads : 2 * heads + 1]
    request = lax.broadcasted_iota(jnp.int32, (requests, total_blocks), 0).astype(jnp.float32)
    member = owner == request
    lane_head = lax.broadcasted_iota(jnp.int32, (requests, columns), 1) // HEAD_DIM
    attended = jnp.zeros((requests, columns), jnp.float32)
    for h in range(heads):
        top = jnp.where(member, stat[h : h + 1], NEG_FLOOR)
        highest = jnp.max(top, axis=1, keepdims=True)
        factor = jnp.where(member, jnp.exp(top - highest) * stat[heads + h : heads + h + 1], 0.0)
        factor = factor / jnp.sum(factor, axis=1, keepdims=True)
        joined = jnp.dot(factor.astype(jnp.bfloat16), parts, preferred_element_type=jnp.float32)
        attended = jnp.where(lane_head == h, joined, attended)
    product[...] = jnp.dot(
        attended.astype(jnp.bfloat16), w_ref[...], preferred_element_type=jnp.float32
    )
    place = place_ref[0]
    share = own_ref.shape[0]
    mine = pl.ds(pl.multiple_of(place * share, share), share)
    own_ref[...] = product[mine, :] + states_ref[mine, :].astype(jnp.float32)
    for m, send in enumerate(sends, 1):
        theirs = pl.ds(pl.multiple_of((place ^ m) * share, share), share)
        send[...] = product[theirs, :].astype(send.dtype)


def shards(states, norm_gain, w_qkv, w_out, cache, context_len, block_owner, block_index):
    requests, depth = states.shape
    peers = lax.axis_size("seq")
    ranks = lax.axis_size("tp")
    parts, _, columns = w_qkv.shape
    blocks, _, tokens, _ = cache.shape
    half = requests // 2
    share = requests // peers
    lines = peers // 2
    out_columns = w_out.shape[1]
    rows = blocks * HEADS
    steps = blocks // GROUP
    limit = pltpu.CompilerParams(vmem_limit_bytes=24 * 1024 * 1024)
    most_room = pltpu.CompilerParams(vmem_limit_bytes=50 * 1024 * 1024)
    all_room = pltpu.CompilerParams(vmem_limit_bytes=60 * 1024 * 1024)
    in_vmem = pl.BlockSpec(memory_space=VMEM)
    in_hbm = pl.BlockSpec(memory_space=HBM)
    in_smem = pl.BlockSpec(memory_space=SMEM)
    anywhere = pl.BlockSpec(memory_space=pl.ANY)
    place = lax.axis_index("seq")
    at = place.reshape(1).astype(jnp.int32)

    def array(*shape, dtype=jnp.bfloat16):
        return jax.ShapeDtypeStruct(shape, dtype)

    def to_peer(value, m):
        return lax.ppermute(value, "seq", [(i, i ^ m) for i in range(peers)])

    def moves(size):
        return pl.CostEstimate(flops=0, bytes_accessed=size, transcendentals=0)

    sent, kept = pl.pallas_call(
        project_kernel,
        out_shape=(
            array(half, parts * columns + LANES),
            array(half, parts * columns + LANES, dtype=jnp.float32),
        ),
        in_specs=[in_smem] + [in_hbm] * 3,
        out_specs=(in_vmem, in_vmem),
        scratch_shapes=[
            pltpu.VMEM(states.shape, jnp.bfloat16),
            pltpu.VMEM(norm_gain.shape, jnp.bfloat16),
            pltpu.VMEM((parts, depth, columns), jnp.bfloat16),
            pltpu.SemaphoreType.DMA((parts + 2,)),
        ],
        compiler_params=all_room,
        name="project",
    )(at, states, norm_gain, w_qkv)
    received = to_peer(sent, 1)

    positions = lax.dynamic_slice_in_dim(context_len, place % 2 * half, half) - 1
    pair = (jnp.arange(columns, dtype=jnp.int32) % (HEAD_DIM // 2)).astype(jnp.float32)
    frequency = 10000.0 ** (-pair * 2.0 / HEAD_DIM)
    angles = positions.astype(jnp.float32)[:, None] * frequency[None, :]

    table = (block_owner, block_index, context_len)
    plan = pl.pallas_call(
        functools.partial(plan_kernel, tokens),
        out_shape=(
            array(rows, half),
            array(rows, half),
            array(rows, LANES, dtype=jnp.int32),
            array(rows, LANES, dtype=jnp.float32),
        ),
        in_specs=[in_smem] * 4,
        compiler_params=limit,
        name="plan",
    )(at, *table)
    keys, updated = pl.pallas_call(
        stage_keys_kernel,
        out_shape=(array(blocks, tokens, columns), array(*cache.shape)),
        in_specs=[in_hbm],
        out_specs=(in_vmem, in_hbm),
        scratch_shapes=[pltpu.SemaphoreType.DMA((steps,))] * 2,
        compiler_params=most_room,
        cost_estimate=moves(cache.size * 2),
        name="stage_keys",
    )(cache)

    *sends, query, fresh = pl.pallas_call(
        halve_kernel,
        out_shape=(
            *(array(half + 2 * share, columns + LANES) for _ in range(1, lines)),
            array(half, columns + LANES, dtype=jnp.float32),
            array(share, 2 * columns, dtype=jnp.float32),
        ),
        in_specs=[in_smem, in_vmem, in_vmem, anywhere],
        scratch_shapes=[pltpu.VMEM((half, parts * columns + LANES), jnp.float32)],
        compiler_params=limit,
        name="halve",
    )(at, kept, received, keys)
    received = [to_peer(send, 2 * m) for m, send in enumerate(sends, 1)]
    updated = pl.pallas_call(
        stage_values_kernel,
        out_shape=array(*cache.shape),
        in_specs=[in_hbm, in_hbm],
        out_specs=in_hbm,
        scratch_shapes=[pltpu.VMEM((blocks, tokens, columns), jnp.bfloat16)]
        + [pltpu.SemaphoreType.DMA((steps,))] * 2,
        input_output_aliases={1: 0},
        compiler_params=most_room,
        cost_estimate=moves(cache.size * 2),
        name="stage_values",
    )(cache, updated)
    mine, news = pl.pallas_call(
        functools.partial(finish_kernel, depth * peers),
        out_shape=(array(half, columns), array(2 * share, columns + LANES)),
        in_specs=[in_smem, in_hbm] + [in_vmem] * (4 + len(received)),
        compiler_params=most_room,
        name="finish",
    )(at, updated, query, fresh, jnp.cos(angles), jnp.sin(angles), *received)
    other = to_peer(mine, 1)

    piece = pl.pallas_call(
        attend_kernel,
        out_shape=array(2 * share + blocks, columns + LANES),
        in_specs=[in_vmem] * 8 + [in_hbm],
        scratch_shapes=[
            pltpu.VMEM((blocks, tokens, columns), jnp.bfloat16),
            pltpu.SemaphoreType.DMA((steps,)),
        ],
        compiler_params=most_room,
        name="attend",
    )(mine, other, *plan, news, keys, cache)
    column = [piece] + [to_peer(piece, 2 * m) for m in range(1, lines)]
    pieces = [p for near in column for p in (near, to_peer(near, 1))]

    rank = lax.axis_index("tp")
    kept_rows = requests // ranks
    own, *sends = pl.pallas_call(
        functools.partial(output_kernel, peers),
        out_shape=tuple(array(kept_rows, out_columns, dtype=jnp.float32) for _ in range(ranks)),
        in_specs=[in_smem] + [in_vmem] * (peers + 2),
        out_specs=(in_vmem,) * ranks,
        scratch_shapes=[pltpu.VMEM((requests, out_columns), jnp.float32)],
        compiler_params=limit,
        name="output",
    )(rank.reshape(1).astype(jnp.int32), *pieces, w_out, states)
    total = own
    for m, send in enumerate(sends, 1):
        total = total + lax.ppermute(send, "tp", [(i, i ^ m) for i in range(ranks)])
    updated = pl.pallas_call(
        functools.partial(patch_kernel, peers),
        out_shape=array(*cache.shape),
        in_specs=[in_smem] * 4 + [anywhere] + [in_vmem] * peers + [in_hbm] * 2,
        out_specs=in_hbm,
        scratch_shapes=[
            pltpu.VMEM((peers, 2 * share, columns), jnp.float32),
            pltpu.VMEM((blocks, 2, ROWS, columns), jnp.bfloat16),
            pltpu.SemaphoreType.DMA((blocks,)),
            pltpu.SemaphoreType.DMA((blocks,)),
        ],
        input_output_aliases={6 + peers: 0},
        compiler_params=most_room,
        cost_estimate=moves(cache.size),
        name="patch",
    )(at, *table, sends[0], *pieces, cache, updated)
    return (total.astype(jnp.bfloat16), updated)


def solution(mesh):
    return jax.shard_map(
        shards,
        mesh=mesh,
        in_specs=(
            P(None, "seq"),
            P("seq"),
            P(None, "seq", "tp"),
            P("tp", "seq"),
            P("seq", None, None, "tp"),
            P(),
            P("seq"),
            P("seq"),
        ),
        out_specs=(P("tp", "seq"), P("seq", None, None, "tp")),
        check_vma=False,
    )
```

```python
import functools

import jax
import jax.numpy as jnp
from jax import lax
from jax.experimental import pallas as pl
from jax.experimental.pallas import tpu as pltpu
from jax.sharding import PartitionSpec as P

HEAD_DIM = 96
EPSILON = 1e-05
NEG_FLOOR = -1e30
LANES = 128
GROUP = 4

VMEM = pltpu.MemorySpace.VMEM
HBM = pltpu.MemorySpace.HBM
SMEM = pltpu.MemorySpace.SMEM
HEADS = 8
ROWS = 16


def split3(value):
    high = value.astype(jnp.bfloat16).astype(jnp.float32)
    rest = value - high
    mid = rest.astype(jnp.bfloat16).astype(jnp.float32)
    low = (rest - mid).astype(jnp.bfloat16).astype(jnp.float32)
    return high, mid, low


def lanes_of(terms):
    lane = lax.broadcasted_iota(jnp.int32, (terms[0].shape[0], LANES), 1)
    out = jnp.zeros(lane.shape, jnp.float32)
    for j, term in enumerate(terms):
        out = jnp.where(lane == j, term, out)
    return out


def project_kernel(
    place_ref, states_ref, gain_ref, w_ref, sent_ref, kept_ref, states_buf, gain_buf, w_buf, sems
):
    parts, _, columns = w_ref.shape
    half = sent_ref.shape[0]
    small = [
        pltpu.make_async_copy(states_ref, states_buf, sems.at[parts]),
        pltpu.make_async_copy(gain_ref, gain_buf, sems.at[parts + 1]),
    ]
    copies = [pltpu.make_async_copy(w_ref.at[c], w_buf.at[c], sems.at[c]) for c in range(parts)]
    for copy in small + copies:
        copy.start()
    for copy in small:
        copy.wait()
    side = place_ref[0] % 2
    rows = [
        states_buf[pl.ds(pl.multiple_of(first * half, half), half), :].astype(jnp.float32)
        for first in (1 - side, side)
    ]
    wide = jnp.concatenate(rows, axis=0)
    gain = gain_buf[...].astype(jnp.float32)
    scaled = (wide * gain.reshape(1, wide.shape[1])).astype(jnp.bfloat16)
    squares = jnp.sum(wide * wide, axis=1, keepdims=True)
    stat = lanes_of(split3(squares))
    sent_ref[:, parts * columns :] = stat[:half].astype(jnp.bfloat16)
    kept_ref[:, parts * columns :] = stat[half:]
    for c in range(parts):
        copies[c].wait()
        term = jnp.dot(scaled, w_buf[c], preferred_element_type=jnp.float32)
        here = slice(c * columns, (c + 1) * columns)
        sent_ref[:, here] = term[:half].astype(jnp.bfloat16)
        kept_ref[:, here] = term[half:]


def flat(value):
    chunks = value.shape[1] // LANES
    return [value[:, c * LANES : (c + 1) * LANES] for c in range(chunks)]


def halve_kernel(place_ref, kept_ref, recv_ref, after_ref, *rest):
    sends, query_ref, fresh_ref, total = rest[:-3], rest[-3], rest[-2], rest[-1]
    columns = query_ref.shape[1] - LANES
    share = fresh_ref.shape[0]
    half = kept_ref.shape[0]
    total[...] = kept_ref[...] + recv_ref[...].astype(jnp.float32)
    squares = jnp.sum(total[:, 3 * columns :], axis=1, keepdims=True)
    query_ref[:, :columns] = total[:, :columns]
    query_ref[:, columns:] = lanes_of([squares])
    query = jnp.concatenate(flat(total[:, :columns]), axis=0).astype(jnp.bfloat16)
    pads = -half % LANES
    stat = [jnp.pad(term, ((0, pads), (0, 0))) for term in split3(squares)]
    lane = lax.broadcasted_iota(jnp.int32, (half + pads, half + pads), 1)
    row = lax.broadcasted_iota(jnp.int32, (half + pads, half + pads), 0)
    stat = [jnp.sum(jnp.where(lane == row, t, 0.0), axis=0, keepdims=True) for t in stat]
    stat = jnp.concatenate(stat + [jnp.zeros((ROWS - 3, half + pads), jnp.float32)], axis=0)
    stat = jnp.concatenate(flat(stat), axis=0).astype(jnp.bfloat16)
    line = place_ref[0] // 2
    chunks = columns // LANES

    def rows_of(group):
        return total[pl.ds(pl.multiple_of(group * share, share), share), columns : 3 * columns]

    fresh_ref[...] = rows_of(line)
    for m, send in enumerate(sends, 1):
        other = jnp.concatenate(flat(rows_of(line ^ m)), axis=0)
        send[: chunks * half, :] = query
        send[chunks * half : chunks * (half + 2 * share), :] = other.astype(jnp.bfloat16)
        send[chunks * (half + 2 * share) :, :] = stat


def finish_kernel(width, place_ref, after_ref, query_ref, fresh_ref, cos_ref, sin_ref, *rest):
    received, out_ref, news_ref = rest[:-2], rest[-2], rest[-1]
    half, columns = out_ref.shape
    share = fresh_ref.shape[0]
    chunks = columns // LANES
    total = flat(query_ref[:, :columns])
    squares = query_ref[:, columns : columns + 1]
    fresh = flat(fresh_ref[...])
    pads = -half % LANES
    stat = jnp.zeros((ROWS * (half + pads) // LANES, LANES), jnp.float32)
    for piece in received:
        for c in range(chunks):
            total[c] = total[c] + piece[c * half : (c + 1) * half, :].astype(jnp.float32)
        extra = piece[chunks * half : chunks * (half + 2 * share), :].astype(jnp.float32)
        for c in range(2 * chunks):
            fresh[c] = fresh[c] + extra[c * share : (c + 1) * share]
        stat = stat + piece[chunks * (half + 2 * share) :, :].astype(jnp.float32)
    total = jnp.concatenate(total, axis=1)
    fresh = jnp.concatenate(fresh, axis=1)
    stat = [jnp.sum(stat[r : r + ROWS], axis=0, keepdims=True) for r in range(0, stat.shape[0], ROWS)]
    stat = jnp.concatenate(stat, axis=1)[:, :half] if len(stat) * LANES == half else stat[0]
    lane = lax.broadcasted_iota(jnp.int32, (half, stat.shape[1]), 1)
    row = lax.broadcasted_iota(jnp.int32, (half, stat.shape[1]), 0)
    squares = squares + jnp.sum(jnp.where(lane == row, stat, 0.0), axis=1, keepdims=True)
    inverse = lax.rsqrt(squares * (1.0 / width) + EPSILON)
    span = HEAD_DIM // 2

    def rotated(x, cosine, sine):
        front = lax.broadcasted_iota(jnp.int32, x.shape, 1) % HEAD_DIM < span
        other = jnp.where(front, -pltpu.roll(x, columns - span, 1), pltpu.roll(x, span, 1))
        return x * cosine + other * sine

    query = rotated(total[:, :columns] * inverse, cos_ref[...], sin_ref[...])
    query = (query * HEAD_DIM ** (-0.5)).astype(jnp.bfloat16)
    out_ref[...] = query
    line = place_ref[0] // 2
    groups = half // share
    mine = jnp.zeros((share, columns), jnp.float32)
    scale = jnp.zeros((share, 1), jnp.float32)
    cosine, sine = mine, mine
    wide = query.astype(jnp.float32)
    for group in range(groups):
        here = slice(group * share, (group + 1) * share)
        mine = jnp.where(line == group, wide[here], mine)
        scale = jnp.where(line == group, inverse[here], scale)
        cosine = jnp.where(line == group, cos_ref[here, :], cosine)
        sine = jnp.where(line == group, sin_ref[here, :], sine)
    key = rotated(fresh[:, :columns] * scale, cosine, sine).astype(jnp.bfloat16)
    value = (fresh[:, columns:] * scale).astype(jnp.bfloat16)
    product = mine * key.astype(jnp.float32)
    lane_head = lax.broadcasted_iota(jnp.int32, product.shape, 1) // HEAD_DIM
    lane = lax.broadcasted_iota(jnp.int32, (share, LANES), 1)
    first = (place_ref[0] % 2) * half + line * share
    owner = lax.broadcasted_iota(jnp.int32, (share, LANES), 0) + first
    stat = jnp.where(lane == 6 * HEADS, owner.astype(jnp.float32), 0.0)
    for h in range(HEADS):
        score = jnp.sum(jnp.where(lane_head == h, product, 0.0), axis=1, keepdims=True)
        for j, term in enumerate(split3(score)):
            stat = jnp.where(lane == j * HEADS + h, term, stat)
        stat = jnp.where(lane == 3 * HEADS + h, 1.0, stat)
    none = jnp.where(lane == 6 * HEADS, -1.0, 0.0)
    both = jnp.concatenate([value.astype(jnp.float32), key.astype(jnp.float32)], axis=0)
    news_ref[:, :columns] = both.astype(jnp.bfloat16)
    news_ref[:, columns:] = jnp.concatenate([stat, none], axis=0).astype(jnp.bfloat16)


def stage(part, cache_ref, near_ref, updated_ref, loads, stores):
    spans = [pl.ds(first, GROUP) for first in range(0, cache_ref.shape[0], GROUP)]
    load = [
        pltpu.make_async_copy(cache_ref.at[span, part], near_ref.at[span], loads.at[i])
        for i, span in enumerate(spans)
    ]
    store = [
        pltpu.make_async_copy(near_ref.at[span], updated_ref.at[span, part], stores.at[i])
        for i, span in enumerate(spans)
    ]
    for copy in load:
        copy.start()
    for arriving, leaving in zip(load, store):
        arriving.wait()
        leaving.start()
    for copy in store:
        copy.wait()


def stage_keys_kernel(cache_ref, keys_ref, updated_ref, loads, stores):
    stage(0, cache_ref, keys_ref, updated_ref, loads, stores)


def stage_values_kernel(cache_ref, held_ref, values_ref, updated_ref, loads, stores):
    stage(1, cache_ref, values_ref, updated_ref, loads, stores)


def read_block(b, owner_ref, index_ref, length_ref, tokens):
    requests = length_ref.shape[0]
    owner = owner_ref[b]
    reach = length_ref[jnp.minimum(owner, requests - 1)] - index_ref[b] * tokens
    live = owner < requests
    old = jnp.where(live, jnp.clip(reach - 1, 0, tokens), 0)
    slot = jnp.where(live & (reach >= 1) & (reach <= tokens), reach - 1, -1)
    return owner, old, slot


def plan_kernel(
    tokens,
    place_ref,
    owner_ref,
    index_ref,
    length_ref,
    mine_ref,
    other_ref,
    seen_ref,
    name_ref,
):
    blocks = owner_ref.shape[0]
    half = mine_ref.shape[1]
    side = place_ref[0] % 2
    lane = lax.broadcasted_iota(jnp.int32, (HEADS, half), 1)
    picks = [], []
    for b in range(blocks):
        owner, old, _ = read_block(b, owner_ref, index_ref, length_ref, tokens)
        here = pl.ds(b * HEADS, HEADS)
        for pick, first in zip(picks, (side, 1 - side)):
            pick.append((lane == owner - first * half).astype(jnp.float32))
        seen_ref[here, :] = jnp.full((HEADS, LANES), old, jnp.int32)
        name_ref[here, :] = jnp.full((HEADS, LANES), owner, jnp.int32).astype(jnp.float32)
    mine_ref[...] = jnp.concatenate(picks[0], axis=0).astype(jnp.bfloat16)
    other_ref[...] = jnp.concatenate(picks[1], axis=0).astype(jnp.bfloat16)


def attend_kernel(
    mine_ref,
    other_ref,
    pick_mine_ref,
    pick_other_ref,
    seen_ref,
    name_ref,
    news_ref,
    keys_ref,
    values_ref,
    out_ref,
):
    blocks, tokens, columns = keys_ref.shape
    extra = news_ref.shape[0]
    steps = blocks // GROUP
    out_ref[:extra, :] = news_ref[...]

    def iota(shape, dim):
        return lax.broadcasted_iota(jnp.int32, shape, dim)

    rows = blocks * HEADS
    size = GROUP * HEADS
    width = GROUP * tokens
    own = jnp.dot(pick_mine_ref[...], mine_ref[...], preferred_element_type=jnp.float32)
    own = own + jnp.dot(pick_other_ref[...], other_ref[...], preferred_element_type=jnp.float32)
    head_mask = iota((rows, columns), 1) // HEAD_DIM == iota((rows, columns), 0) % HEADS
    queries = jnp.where(head_mask, own, 0.0).astype(jnp.bfloat16)
    scores = []
    for step in range(steps):
        keys = keys_ref[step * GROUP : (step + 1) * GROUP].reshape(width, columns)
        scores.append(
            lax.dot_general(
                queries[step * size : (step + 1) * size],
                keys,
                (((1,), (1,)), ((), ())),
                preferred_element_type=jnp.float32,
            )
        )
    scores = jnp.concatenate(scores, axis=0)
    column = iota((rows, width), 1)
    same = column // tokens == iota((rows, width), 0) // HEADS % GROUP
    place = jnp.where(same, column % tokens, tokens)
    visible = place < jnp.concatenate([seen_ref[...]] * (width // LANES), axis=1)
    masked = jnp.where(visible, scores, NEG_FLOOR)
    top = jnp.max(masked, axis=1, keepdims=True)
    weights = jnp.where(visible, jnp.exp(masked - top), 0.0).astype(jnp.bfloat16)
    mass = jnp.sum(weights.astype(jnp.float32), axis=1, keepdims=True)
    parts = []
    for step in range(steps):
        values = values_ref[step * GROUP : (step + 1) * GROUP].reshape(width, columns)
        parts.append(
            jnp.dot(
                weights[step * size : (step + 1) * size],
                values,
                preferred_element_type=jnp.float32,
            )
        )
    part = jnp.concatenate(parts, axis=0) * jnp.where(mass > 0.0, 1.0 / mass, 0.0)
    part = jnp.where(head_mask, part, 0.0).astype(jnp.bfloat16)
    lane = iota((rows, LANES), 1)
    head = iota((rows, LANES), 0) % HEADS
    stat = jnp.where((lane == 6 * HEADS) & (head == 0), name_ref[...], 0.0)
    for j, term in enumerate(split3(top) + split3(mass)):
        stat = jnp.where(lane == head + j * HEADS, term, stat)
    padded = blocks + -blocks % 16
    fold = iota((padded, rows), 1) // HEADS == iota((padded, rows), 0)
    fold = fold.astype(jnp.float32).astype(jnp.bfloat16)
    part = jnp.dot(fold, part, preferred_element_type=jnp.float32)
    stat = jnp.dot(fold, stat.astype(jnp.bfloat16), preferred_element_type=jnp.float32)
    out_ref[extra:, :columns] = part[:blocks].astype(jnp.bfloat16)
    out_ref[extra:, columns:] = stat[:blocks].astype(jnp.bfloat16)


def each_slot(tokens, owner_ref, index_ref, length_ref, do):
    for b in range(owner_ref.shape[0]):
        owner, _, slot = read_block(b, owner_ref, index_ref, length_ref, tokens)
        first = pl.multiple_of(jnp.maximum(slot, 0) // ROWS * ROWS, ROWS)
        pl.when(slot >= 0)(functools.partial(do, b, owner, slot, first))


def fetch_kernel(owner_ref, index_ref, length_ref, after_ref, cache_ref, near_ref, loads):
    tokens = cache_ref.shape[2]

    def fetch(b, owner, slot, first):
        return pltpu.make_async_copy(
            cache_ref.at[b, :, pl.ds(first, ROWS), :], near_ref.at[b], loads.at[b]
        )

    each_slot(tokens, owner_ref, index_ref, length_ref, lambda *at: fetch(*at).start())
    each_slot(tokens, owner_ref, index_ref, length_ref, lambda *at: fetch(*at).wait())


def patch_kernel(count, place_ref, owner_ref, index_ref, length_ref, after_ref, *rest):
    pieces, near_ref, held_ref, updated_ref = rest[:count], rest[count], rest[count + 1], rest[count + 2]
    fresh, patch, stores = rest[count + 3 :]
    _, _, tokens, columns = updated_ref.shape
    requests = length_ref.shape[0]
    share = fresh.shape[1] // 2
    half = requests // 2

    def store(b, owner, slot, first):
        return pltpu.make_async_copy(
            patch.at[b], updated_ref.at[b, :, pl.ds(first, ROWS), :], stores.at[b]
        )

    for m in range(count):
        fresh[m] = pieces[m][: 2 * share, :columns].astype(jnp.float32)
    row = lax.broadcasted_iota(jnp.int32, (ROWS, columns), 0)

    def change(b, owner, slot, first):
        request = jnp.minimum(owner, requests - 1)
        device = request % half // share * 2 + request // half
        piece = place_ref[0] ^ device
        line = request % share
        for c in range(2):
            new = fresh[piece, pl.ds(line + (1 - c) * share, 1), :]
            old = near_ref[b, c].astype(jnp.float32)
            patch[b, c] = jnp.where(row == slot - first, new, old).astype(jnp.bfloat16)
        store(b, owner, slot, first).start()

    each_slot(tokens, owner_ref, index_ref, length_ref, change)
    each_slot(tokens, owner_ref, index_ref, length_ref, lambda *at: store(*at).wait())


def output_kernel(count, place_ref, *rest):
    pieces, w_ref, states_ref, own_ref = rest[:count], rest[count], rest[count + 1], rest[count + 3]
    sends, product = rest[count + 4 : -1], rest[-1]
    heads = HEADS
    blocks, wide = pieces[0].shape
    columns = wide - LANES
    requests = states_ref.shape[0]
    total_blocks = count * blocks
    both = [piece[...].astype(jnp.float32) for piece in pieces]
    both = jnp.concatenate(both, axis=0).astype(jnp.bfloat16)
    parts, stat = both[:, :columns], both[:, columns:]
    row = lax.broadcasted_iota(jnp.int32, (3 * heads, LANES), 0)
    lane = lax.broadcasted_iota(jnp.int32, (3 * heads, LANES), 1)
    wanted = (row // heads == lane // (3 * heads)) & (row % heads == lane % heads)
    wanted = (wanted & (row < 2 * heads)) | ((row >= 2 * heads) & (lane == 6 * heads))
    stat = lax.dot_general(
        wanted.astype(jnp.float32).astype(jnp.bfloat16),
        stat,
        (((1,), (1,)), ((), ())),
        preferred_element_type=jnp.float32,
    )
    owner = stat[2 * heads : 2 * heads + 1]
    request = lax.broadcasted_iota(jnp.int32, (requests, total_blocks), 0).astype(jnp.float32)
    member = owner == request
    lane_head = lax.broadcasted_iota(jnp.int32, (requests, columns), 1) // HEAD_DIM
    attended = jnp.zeros((requests, columns), jnp.float32)
    for h in range(heads):
        top = jnp.where(member, stat[h : h + 1], NEG_FLOOR)
        highest = jnp.max(top, axis=1, keepdims=True)
        factor = jnp.where(member, jnp.exp(top - highest) * stat[heads + h : heads + h + 1], 0.0)
        factor = factor / jnp.sum(factor, axis=1, keepdims=True)
        joined = jnp.dot(factor.astype(jnp.bfloat16), parts, preferred_element_type=jnp.float32)
        attended = jnp.where(lane_head == h, joined, attended)
    product[...] = jnp.dot(
        attended.astype(jnp.bfloat16), w_ref[...], preferred_element_type=jnp.float32
    )
    place = place_ref[0]
    share = own_ref.shape[0]
    mine = pl.ds(pl.multiple_of(place * share, share), share)
    own_ref[...] = product[mine, :] + states_ref[mine, :].astype(jnp.float32)
    for m, send in enumerate(sends, 1):
        theirs = pl.ds(pl.multiple_of((place ^ m) * share, share), share)
        send[...] = product[theirs, :].astype(send.dtype)


def shards(states, norm_gain, w_qkv, w_out, cache, context_len, block_owner, block_index):
    requests, depth = states.shape
    peers = lax.axis_size("seq")
    ranks = lax.axis_size("tp")
    parts, _, columns = w_qkv.shape
    blocks, _, tokens, _ = cache.shape
    half = requests // 2
    share = requests // peers
    lines = peers // 2
    out_columns = w_out.shape[1]
    rows = blocks * HEADS
    steps = blocks // GROUP
    limit = pltpu.CompilerParams(vmem_limit_bytes=24 * 1024 * 1024)
    most_room = pltpu.CompilerParams(vmem_limit_bytes=50 * 1024 * 1024)
    all_room = pltpu.CompilerParams(vmem_limit_bytes=60 * 1024 * 1024)
    in_vmem = pl.BlockSpec(memory_space=VMEM)
    in_hbm = pl.BlockSpec(memory_space=HBM)
    in_smem = pl.BlockSpec(memory_space=SMEM)
    anywhere = pl.BlockSpec(memory_space=pl.ANY)
    place = lax.axis_index("seq")
    at = place.reshape(1).astype(jnp.int32)

    def array(*shape, dtype=jnp.bfloat16):
        return jax.ShapeDtypeStruct(shape, dtype)

    def to_peer(value, m):
        return lax.ppermute(value, "seq", [(i, i ^ m) for i in range(peers)])

    def moves(size):
        return pl.CostEstimate(flops=0, bytes_accessed=size, transcendentals=0)

    sent, kept = pl.pallas_call(
        project_kernel,
        out_shape=(
            array(half, parts * columns + LANES),
            array(half, parts * columns + LANES, dtype=jnp.float32),
        ),
        in_specs=[in_smem] + [in_hbm] * 3,
        out_specs=(in_vmem, in_vmem),
        scratch_shapes=[
            pltpu.VMEM(states.shape, jnp.bfloat16),
            pltpu.VMEM(norm_gain.shape, jnp.bfloat16),
            pltpu.VMEM((parts, depth, columns), jnp.bfloat16),
            pltpu.SemaphoreType.DMA((parts + 2,)),
        ],
        compiler_params=all_room,
        name="project",
    )(at, states, norm_gain, w_qkv)
    received = to_peer(sent, 1)

    positions = lax.dynamic_slice_in_dim(context_len, place % 2 * half, half) - 1
    pair = (jnp.arange(columns, dtype=jnp.int32) % (HEAD_DIM // 2)).astype(jnp.float32)
    frequency = 10000.0 ** (-pair * 2.0 / HEAD_DIM)
    angles = positions.astype(jnp.float32)[:, None] * frequency[None, :]

    table = (block_owner, block_index, context_len)
    plan = pl.pallas_call(
        functools.partial(plan_kernel, tokens),
        out_shape=(
            array(rows, half),
            array(rows, half),
            array(rows, LANES, dtype=jnp.int32),
            array(rows, LANES, dtype=jnp.float32),
        ),
        in_specs=[in_smem] * 4,
        compiler_params=limit,
        name="plan",
    )(at, *table)
    keys, updated = pl.pallas_call(
        stage_keys_kernel,
        out_shape=(array(blocks, tokens, columns), array(*cache.shape)),
        in_specs=[in_hbm],
        out_specs=(in_vmem, in_hbm),
        scratch_shapes=[pltpu.SemaphoreType.DMA((steps,))] * 2,
        compiler_params=most_room,
        cost_estimate=moves(cache.size * 2),
        name="stage_keys",
    )(cache)

    message = columns // LANES * (half + 2 * share) + ROWS * pl.cdiv(half, LANES)
    *sends, query, fresh = pl.pallas_call(
        halve_kernel,
        out_shape=(
            *(array(message, LANES) for _ in range(1, lines)),
            array(half, columns + LANES, dtype=jnp.float32),
            array(share, 2 * columns, dtype=jnp.float32),
        ),
        in_specs=[in_smem, in_vmem, in_vmem, anywhere],
        scratch_shapes=[pltpu.VMEM((half, parts * columns + LANES), jnp.float32)],
        compiler_params=limit,
        name="halve",
    )(at, kept, received, keys)
    received = [to_peer(sends[m - 1], 2 * m) for m in sorted(range(1, lines), key=lambda m: m)]
    values, updated = pl.pallas_call(
        stage_values_kernel,
        out_shape=(array(blocks, tokens, columns), array(*cache.shape)),
        in_specs=[in_hbm, in_hbm],
        out_specs=(in_vmem, in_hbm),
        scratch_shapes=[pltpu.SemaphoreType.DMA((steps,))] * 2,
        input_output_aliases={1: 1},
        compiler_params=pltpu.CompilerParams(vmem_limit_bytes=47 * 1024 * 1024),
        cost_estimate=moves(cache.size * 2),
        name="stage_values",
    )(cache, updated)
    mine, news = pl.pallas_call(
        functools.partial(finish_kernel, depth * peers),
        out_shape=(array(half, columns), array(2 * share, columns + LANES)),
        in_specs=[in_smem, anywhere] + [in_vmem] * (4 + len(received)),
        compiler_params=pltpu.CompilerParams(vmem_limit_bytes=47 * 1024 * 1024),
        name="finish",
    )(at, values, query, fresh, jnp.cos(angles), jnp.sin(angles), *received)
    other = to_peer(mine, 1)

    piece = pl.pallas_call(
        attend_kernel,
        out_shape=array(2 * share + blocks, columns + LANES),
        in_specs=[in_vmem] * 9,
        compiler_params=pltpu.CompilerParams(vmem_limit_bytes=47 * 1024 * 1024),
        name="attend",
    )(mine, other, *plan, news, keys, values)
    pieces = [piece] * peers
    far = sorted(range(1, lines), key=lambda m: m)
    for m in far:
        pieces[2 * m] = to_peer(piece, 2 * m)
    for m in (*far, 0):
        pieces[2 * m + 1] = to_peer(pieces[2 * m], 1)

    near = pl.pallas_call(
        fetch_kernel,
        out_shape=array(blocks, 2, ROWS, columns),
        in_specs=[in_smem] * 3 + [anywhere, in_hbm],
        out_specs=in_vmem,
        scratch_shapes=[pltpu.SemaphoreType.DMA((blocks,))],
        compiler_params=most_room,
        cost_estimate=moves(blocks * ROWS * columns * 8),
        name="fetch",
    )(*table, piece, cache)
    rank = lax.axis_index("tp")
    kept_rows = requests // ranks
    own, *sends = pl.pallas_call(
        functools.partial(output_kernel, peers),
        out_shape=(
            array(kept_rows, out_columns, dtype=jnp.float32),
            *(array(kept_rows, out_columns, dtype=jnp.float32) for _ in range(1, ranks)),
        ),
        in_specs=[in_smem] + [in_vmem] * (peers + 2) + [anywhere],
        out_specs=(in_vmem,) * ranks,
        scratch_shapes=[pltpu.VMEM((requests, out_columns), jnp.float32)],
        compiler_params=limit,
        name="output",
    )(rank.reshape(1).astype(jnp.int32), *pieces, w_out, states, near)
    total = own
    for m in range(1, ranks):
        moved = lax.ppermute(sends[m - 1], "tp", [(i, i ^ m) for i in range(ranks)])
        total = total + moved.astype(jnp.float32)
    updated = pl.pallas_call(
        functools.partial(patch_kernel, peers),
        out_shape=array(*cache.shape),
        in_specs=[in_smem] * 4 + [anywhere] + [in_vmem] * (peers + 1) + [in_hbm],
        out_specs=in_hbm,
        scratch_shapes=[
            pltpu.VMEM((peers, 2 * share, columns), jnp.float32),
            pltpu.VMEM((blocks, 2, ROWS, columns), jnp.bfloat16),
            pltpu.SemaphoreType.DMA((blocks,)),
        ],
        input_output_aliases={6 + peers: 0},
        compiler_params=most_room,
        cost_estimate=moves(blocks * ROWS * columns * 8),
        name="patch",
    )(at, *table, sends[0], *pieces, near, updated)
    return (total.astype(jnp.bfloat16), updated)


def solution(mesh):
    return jax.shard_map(
        shards,
        mesh=mesh,
        in_specs=(
            P(None, "seq"),
            P("seq"),
            P(None, "seq", "tp"),
            P("tp", "seq"),
            P("seq", None, None, "tp"),
            P(),
            P("seq"),
            P("seq"),
        ),
        out_specs=(P("tp", "seq"), P("seq", None, None, "tp")),
        check_vma=False,
    )
```

```python
import functools

import jax
import jax.numpy as jnp
from jax import lax
from jax.experimental import pallas as pl
from jax.experimental.pallas import tpu as pltpu
from jax.sharding import PartitionSpec as P

HEAD_DIM = 96
EPSILON = 1e-05
NEG_FLOOR = -1e30
LANES = 128
GROUP = 4

VMEM = pltpu.MemorySpace.VMEM
HBM = pltpu.MemorySpace.HBM
SMEM = pltpu.MemorySpace.SMEM
HEADS = 8
ROWS = 16


def split3(value):
    high = value.astype(jnp.bfloat16).astype(jnp.float32)
    rest = value - high
    mid = rest.astype(jnp.bfloat16).astype(jnp.float32)
    low = (rest - mid).astype(jnp.bfloat16).astype(jnp.float32)
    return high, mid, low


def lanes_of(terms):
    lane = lax.broadcasted_iota(jnp.int32, (terms[0].shape[0], LANES), 1)
    out = jnp.zeros(lane.shape, jnp.float32)
    for j, term in enumerate(terms):
        out = jnp.where(lane == j, term, out)
    return out


def project_kernel(
    place_ref, states_ref, gain_ref, w_ref, sent_ref, kept_ref, states_buf, gain_buf, w_buf, sems
):
    parts, _, columns = w_ref.shape
    half = sent_ref.shape[0]
    small = [
        pltpu.make_async_copy(states_ref, states_buf, sems.at[parts]),
        pltpu.make_async_copy(gain_ref, gain_buf, sems.at[parts + 1]),
    ]
    copies = [pltpu.make_async_copy(w_ref.at[c], w_buf.at[c], sems.at[c]) for c in range(parts)]
    for copy in small + copies:
        copy.start()
    for copy in small:
        copy.wait()
    side = place_ref[0] % 2
    rows = [
        states_buf[pl.ds(pl.multiple_of(first * half, half), half), :].astype(jnp.float32)
        for first in (1 - side, side)
    ]
    wide = jnp.concatenate(rows, axis=0)
    gain = gain_buf[...].astype(jnp.float32)
    scaled = (wide * gain.reshape(1, wide.shape[1])).astype(jnp.bfloat16)
    squares = jnp.sum(wide * wide, axis=1, keepdims=True)
    stat = lanes_of(split3(squares))
    sent_ref[:, parts * columns :] = stat[:half].astype(jnp.bfloat16)
    kept_ref[:, parts * columns :] = stat[half:]
    for c in range(parts):
        copies[c].wait()
        term = jnp.dot(scaled, w_buf[c], preferred_element_type=jnp.float32)
        here = slice(c * columns, (c + 1) * columns)
        sent_ref[:, here] = term[:half].astype(jnp.bfloat16)
        kept_ref[:, here] = term[half:]


def flat(value):
    chunks = value.shape[1] // LANES
    return [value[:, c * LANES : (c + 1) * LANES] for c in range(chunks)]


def halve_kernel(place_ref, kept_ref, recv_ref, after_ref, *rest):
    sends, query_ref, fresh_ref, total = rest[:-3], rest[-3], rest[-2], rest[-1]
    columns = query_ref.shape[1] - LANES
    share = fresh_ref.shape[0]
    half = kept_ref.shape[0]
    total[...] = kept_ref[...] + recv_ref[...].astype(jnp.float32)
    squares = jnp.sum(total[:, 3 * columns :], axis=1, keepdims=True)
    query_ref[:, :columns] = total[:, :columns]
    query_ref[:, columns:] = lanes_of([squares])
    query = jnp.concatenate(flat(total[:, :columns]), axis=0).astype(jnp.bfloat16)
    pads = -half % LANES
    stat = [jnp.pad(term, ((0, pads), (0, 0))) for term in split3(squares)]
    lane = lax.broadcasted_iota(jnp.int32, (half + pads, half + pads), 1)
    row = lax.broadcasted_iota(jnp.int32, (half + pads, half + pads), 0)
    stat = [jnp.sum(jnp.where(lane == row, t, 0.0), axis=0, keepdims=True) for t in stat]
    stat = jnp.concatenate(stat + [jnp.zeros((ROWS - 3, half + pads), jnp.float32)], axis=0)
    stat = jnp.concatenate(flat(stat), axis=0).astype(jnp.bfloat16)
    line = place_ref[0] // 2
    chunks = columns // LANES

    def rows_of(group):
        return total[pl.ds(pl.multiple_of(group * share, share), share), columns : 3 * columns]

    fresh_ref[...] = rows_of(line)
    for m, send in enumerate(sends, 1):
        other = jnp.concatenate(flat(rows_of(line ^ m)), axis=0)
        send[: chunks * half, :] = query
        send[chunks * half : chunks * (half + 2 * share), :] = other.astype(jnp.bfloat16)
        send[chunks * (half + 2 * share) :, :] = stat


def finish_kernel(width, place_ref, after_ref, query_ref, fresh_ref, cos_ref, sin_ref, *rest):
    received, out_ref, news_ref = rest[:-2], rest[-2], rest[-1]
    half, columns = out_ref.shape
    share = fresh_ref.shape[0]
    chunks = columns // LANES
    total = flat(query_ref[:, :columns])
    squares = query_ref[:, columns : columns + 1]
    fresh = flat(fresh_ref[...])
    pads = -half % LANES
    stat = jnp.zeros((ROWS * (half + pads) // LANES, LANES), jnp.float32)
    for piece in received:
        for c in range(chunks):
            total[c] = total[c] + piece[c * half : (c + 1) * half, :].astype(jnp.float32)
        extra = piece[chunks * half : chunks * (half + 2 * share), :].astype(jnp.float32)
        for c in range(2 * chunks):
            fresh[c] = fresh[c] + extra[c * share : (c + 1) * share]
        stat = stat + piece[chunks * (half + 2 * share) :, :].astype(jnp.float32)
    total = jnp.concatenate(total, axis=1)
    fresh = jnp.concatenate(fresh, axis=1)
    stat = [jnp.sum(stat[r : r + ROWS], axis=0, keepdims=True) for r in range(0, stat.shape[0], ROWS)]
    stat = jnp.concatenate(stat, axis=1)[:, :half] if len(stat) * LANES == half else stat[0]
    lane = lax.broadcasted_iota(jnp.int32, (half, stat.shape[1]), 1)
    row = lax.broadcasted_iota(jnp.int32, (half, stat.shape[1]), 0)
    squares = squares + jnp.sum(jnp.where(lane == row, stat, 0.0), axis=1, keepdims=True)
    inverse = lax.rsqrt(squares * (1.0 / width) + EPSILON)
    span = HEAD_DIM // 2

    def rotated(x, cosine, sine):
        front = lax.broadcasted_iota(jnp.int32, x.shape, 1) % HEAD_DIM < span
        other = jnp.where(front, -pltpu.roll(x, columns - span, 1), pltpu.roll(x, span, 1))
        return x * cosine + other * sine

    query = rotated(total[:, :columns] * inverse, cos_ref[...], sin_ref[...])
    query = (query * HEAD_DIM ** (-0.5)).astype(jnp.bfloat16)
    out_ref[...] = query
    line = place_ref[0] // 2
    groups = half // share
    mine = jnp.zeros((share, columns), jnp.float32)
    scale = jnp.zeros((share, 1), jnp.float32)
    cosine, sine = mine, mine
    wide = query.astype(jnp.float32)
    for group in range(groups):
        here = slice(group * share, (group + 1) * share)
        mine = jnp.where(line == group, wide[here], mine)
        scale = jnp.where(line == group, inverse[here], scale)
        cosine = jnp.where(line == group, cos_ref[here, :], cosine)
        sine = jnp.where(line == group, sin_ref[here, :], sine)
    key = rotated(fresh[:, :columns] * scale, cosine, sine).astype(jnp.bfloat16)
    value = (fresh[:, columns:] * scale).astype(jnp.bfloat16)
    product = mine * key.astype(jnp.float32)
    lane_head = lax.broadcasted_iota(jnp.int32, product.shape, 1) // HEAD_DIM
    lane = lax.broadcasted_iota(jnp.int32, (share, LANES), 1)
    first = (place_ref[0] % 2) * half + line * share
    owner = lax.broadcasted_iota(jnp.int32, (share, LANES), 0) + first
    stat = jnp.where(lane == 6 * HEADS, owner.astype(jnp.float32), 0.0)
    for h in range(HEADS):
        score = jnp.sum(jnp.where(lane_head == h, product, 0.0), axis=1, keepdims=True)
        for j, term in enumerate(split3(score)):
            stat = jnp.where(lane == j * HEADS + h, term, stat)
        stat = jnp.where(lane == 3 * HEADS + h, 1.0, stat)
    none = jnp.where(lane == 6 * HEADS, -1.0, 0.0)
    both = jnp.concatenate([value.astype(jnp.float32), key.astype(jnp.float32)], axis=0)
    news_ref[:, :columns] = both.astype(jnp.bfloat16)
    news_ref[:, columns:] = jnp.concatenate([stat, none], axis=0).astype(jnp.bfloat16)


def stage(part, cache_ref, near_ref, updated_ref, loads, stores):
    spans = [pl.ds(first, GROUP) for first in range(0, cache_ref.shape[0], GROUP)]
    load = [
        pltpu.make_async_copy(cache_ref.at[span, part], near_ref.at[span], loads.at[i])
        for i, span in enumerate(spans)
    ]
    store = [
        pltpu.make_async_copy(near_ref.at[span], updated_ref.at[span, part], stores.at[i])
        for i, span in enumerate(spans)
    ]
    for copy in load:
        copy.start()
    for arriving, leaving in zip(load, store):
        arriving.wait()
        leaving.start()
    for copy in store:
        copy.wait()


def stage_keys_kernel(cache_ref, keys_ref, updated_ref, loads, stores):
    stage(0, cache_ref, keys_ref, updated_ref, loads, stores)


def stage_values_kernel(cache_ref, held_ref, values_ref, updated_ref, loads, stores):
    stage(1, cache_ref, values_ref, updated_ref, loads, stores)


def read_block(b, owner_ref, index_ref, length_ref, tokens):
    requests = length_ref.shape[0]
    owner = owner_ref[b]
    reach = length_ref[jnp.minimum(owner, requests - 1)] - index_ref[b] * tokens
    live = owner < requests
    old = jnp.where(live, jnp.clip(reach - 1, 0, tokens), 0)
    slot = jnp.where(live & (reach >= 1) & (reach <= tokens), reach - 1, -1)
    return owner, old, slot


def plan_kernel(
    tokens,
    place_ref,
    owner_ref,
    index_ref,
    length_ref,
    mine_ref,
    other_ref,
    seen_ref,
    name_ref,
):
    blocks = owner_ref.shape[0]
    half = mine_ref.shape[1]
    side = place_ref[0] % 2
    lane = lax.broadcasted_iota(jnp.int32, (HEADS, half), 1)
    picks = [], []
    for b in range(blocks):
        owner, old, _ = read_block(b, owner_ref, index_ref, length_ref, tokens)
        here = pl.ds(b * HEADS, HEADS)
        for pick, first in zip(picks, (side, 1 - side)):
            pick.append((lane == owner - first * half).astype(jnp.float32))
        seen_ref[here, :] = jnp.full((HEADS, LANES), old, jnp.int32)
        name_ref[here, :] = jnp.full((HEADS, LANES), owner, jnp.int32).astype(jnp.float32)
    mine_ref[...] = jnp.concatenate(picks[0], axis=0).astype(jnp.bfloat16)
    other_ref[...] = jnp.concatenate(picks[1], axis=0).astype(jnp.bfloat16)


def attend_kernel(
    mine_ref,
    other_ref,
    pick_mine_ref,
    pick_other_ref,
    seen_ref,
    name_ref,
    news_ref,
    keys_ref,
    values_ref,
    out_ref,
):
    blocks, tokens, columns = keys_ref.shape
    extra = news_ref.shape[0]
    steps = blocks // GROUP
    out_ref[:extra, :] = news_ref[...]

    def iota(shape, dim):
        return lax.broadcasted_iota(jnp.int32, shape, dim)

    rows = blocks * HEADS
    size = GROUP * HEADS
    width = GROUP * tokens
    own = jnp.dot(pick_mine_ref[...], mine_ref[...], preferred_element_type=jnp.float32)
    own = own + jnp.dot(pick_other_ref[...], other_ref[...], preferred_element_type=jnp.float32)
    head_mask = iota((rows, columns), 1) // HEAD_DIM == iota((rows, columns), 0) % HEADS
    queries = jnp.where(head_mask, own, 0.0).astype(jnp.bfloat16)
    scores = []
    for step in range(steps):
        keys = keys_ref[step * GROUP : (step + 1) * GROUP].reshape(width, columns)
        scores.append(
            lax.dot_general(
                queries[step * size : (step + 1) * size],
                keys,
                (((1,), (1,)), ((), ())),
                preferred_element_type=jnp.float32,
            )
        )
    scores = jnp.concatenate(scores, axis=0)
    column = iota((rows, width), 1)
    same = column // tokens == iota((rows, width), 0) // HEADS % GROUP
    place = jnp.where(same, column % tokens, tokens)
    visible = place < jnp.concatenate([seen_ref[...]] * (width // LANES), axis=1)
    masked = jnp.where(visible, scores, NEG_FLOOR)
    top = jnp.max(masked, axis=1, keepdims=True)
    weights = jnp.where(visible, jnp.exp(masked - top), 0.0).astype(jnp.bfloat16)
    mass = jnp.sum(weights.astype(jnp.float32), axis=1, keepdims=True)
    parts = []
    for step in range(steps):
        values = values_ref[step * GROUP : (step + 1) * GROUP].reshape(width, columns)
        parts.append(
            jnp.dot(
                weights[step * size : (step + 1) * size],
                values,
                preferred_element_type=jnp.float32,
            )
        )
    part = jnp.concatenate(parts, axis=0) * jnp.where(mass > 0.0, 1.0 / mass, 0.0)
    part = jnp.where(head_mask, part, 0.0).astype(jnp.bfloat16)
    lane = iota((rows, LANES), 1)
    head = iota((rows, LANES), 0) % HEADS
    stat = jnp.where((lane == 6 * HEADS) & (head == 0), name_ref[...], 0.0)
    for j, term in enumerate(split3(top) + split3(mass)):
        stat = jnp.where(lane == head + j * HEADS, term, stat)
    padded = blocks + -blocks % 16
    fold = iota((padded, rows), 1) // HEADS == iota((padded, rows), 0)
    fold = fold.astype(jnp.float32).astype(jnp.bfloat16)
    part = jnp.dot(fold, part, preferred_element_type=jnp.float32)
    stat = jnp.dot(fold, stat.astype(jnp.bfloat16), preferred_element_type=jnp.float32)
    out_ref[extra:, :columns] = part[:blocks].astype(jnp.bfloat16)
    out_ref[extra:, columns:] = stat[:blocks].astype(jnp.bfloat16)


def each_slot(tokens, owner_ref, index_ref, length_ref, do):
    for b in range(owner_ref.shape[0]):
        owner, _, slot = read_block(b, owner_ref, index_ref, length_ref, tokens)
        first = pl.multiple_of(jnp.maximum(slot, 0) // ROWS * ROWS, ROWS)
        pl.when(slot >= 0)(functools.partial(do, b, owner, slot, first))


def fetch_kernel(owner_ref, index_ref, length_ref, after_ref, cache_ref, near_ref, loads):
    tokens = cache_ref.shape[2]

    def fetch(b, owner, slot, first):
        return pltpu.make_async_copy(
            cache_ref.at[b, :, pl.ds(first, ROWS), :], near_ref.at[b], loads.at[b]
        )

    each_slot(tokens, owner_ref, index_ref, length_ref, lambda *at: fetch(*at).start())
    each_slot(tokens, owner_ref, index_ref, length_ref, lambda *at: fetch(*at).wait())


def patch_kernel(count, place_ref, owner_ref, index_ref, length_ref, after_ref, *rest):
    pieces, near_ref, held_ref, updated_ref = rest[:count], rest[count], rest[count + 1], rest[count + 2]
    fresh, patch, stores = rest[count + 3 :]
    _, _, tokens, columns = updated_ref.shape
    requests = length_ref.shape[0]
    share = fresh.shape[1] // 2
    half = requests // 2

    def store(b, owner, slot, first):
        return pltpu.make_async_copy(
            patch.at[b], updated_ref.at[b, :, pl.ds(first, ROWS), :], stores.at[b]
        )

    for m in range(count):
        fresh[m] = pieces[m][: 2 * share, :columns].astype(jnp.float32)
    row = lax.broadcasted_iota(jnp.int32, (ROWS, columns), 0)

    def change(b, owner, slot, first):
        request = jnp.minimum(owner, requests - 1)
        device = request % half // share * 2 + request // half
        piece = place_ref[0] ^ device
        line = request % share
        for c in range(2):
            new = fresh[piece, pl.ds(line + (1 - c) * share, 1), :]
            old = near_ref[b, c].astype(jnp.float32)
            patch[b, c] = jnp.where(row == slot - first, new, old).astype(jnp.bfloat16)
        store(b, owner, slot, first).start()

    each_slot(tokens, owner_ref, index_ref, length_ref, change)
    each_slot(tokens, owner_ref, index_ref, length_ref, lambda *at: store(*at).wait())


def output_kernel(count, place_ref, *rest):
    pieces, w_ref, states_ref, own_ref = rest[:count], rest[count], rest[count + 1], rest[count + 3]
    sends, product = rest[count + 4 : -1], rest[-1]
    heads = HEADS
    blocks, wide = pieces[0].shape
    columns = wide - LANES
    requests = states_ref.shape[0]
    total_blocks = count * blocks
    both = [piece[...].astype(jnp.float32) for piece in pieces]
    both = jnp.concatenate(both, axis=0).astype(jnp.bfloat16)
    parts, stat = both[:, :columns], both[:, columns:]
    row = lax.broadcasted_iota(jnp.int32, (3 * heads, LANES), 0)
    lane = lax.broadcasted_iota(jnp.int32, (3 * heads, LANES), 1)
    wanted = (row // heads == lane // (3 * heads)) & (row % heads == lane % heads)
    wanted = (wanted & (row < 2 * heads)) | ((row >= 2 * heads) & (lane == 6 * heads))
    stat = lax.dot_general(
        wanted.astype(jnp.float32).astype(jnp.bfloat16),
        stat,
        (((1,), (1,)), ((), ())),
        preferred_element_type=jnp.float32,
    )
    owner = stat[2 * heads : 2 * heads + 1]
    request = lax.broadcasted_iota(jnp.int32, (requests, total_blocks), 0).astype(jnp.float32)
    member = owner == request
    lane_head = lax.broadcasted_iota(jnp.int32, (requests, columns), 1) // HEAD_DIM
    factors = []
    for h in range(heads):
        top = jnp.where(member, stat[h : h + 1], NEG_FLOOR)
        highest = jnp.max(top, axis=1, keepdims=True)
        factor = jnp.where(member, jnp.exp(top - highest) * stat[heads + h : heads + h + 1], 0.0)
        factors.append(factor / jnp.sum(factor, axis=1, keepdims=True))
    factors = jnp.concatenate(factors, axis=0).astype(jnp.bfloat16)
    joined = jnp.dot(factors, parts, preferred_element_type=jnp.float32)
    attended = joined[:requests]
    for h in range(1, heads):
        attended = jnp.where(lane_head == h, joined[h * requests : (h + 1) * requests], attended)
    product[...] = jnp.dot(
        attended.astype(jnp.bfloat16), w_ref[...], preferred_element_type=jnp.float32
    )
    place = place_ref[0]
    share = own_ref.shape[0]
    mine = pl.ds(pl.multiple_of(place * share, share), share)
    own_ref[...] = product[mine, :] + states_ref[mine, :].astype(jnp.float32)
    for m, send in enumerate(sends, 1):
        theirs = pl.ds(pl.multiple_of((place ^ m) * share, share), share)
        send[...] = product[theirs, :].astype(send.dtype)


def shards(states, norm_gain, w_qkv, w_out, cache, context_len, block_owner, block_index):
    requests, depth = states.shape
    peers = lax.axis_size("seq")
    ranks = lax.axis_size("tp")
    parts, _, columns = w_qkv.shape
    blocks, _, tokens, _ = cache.shape
    half = requests // 2
    share = requests // peers
    lines = peers // 2
    out_columns = w_out.shape[1]
    rows = blocks * HEADS
    steps = blocks // GROUP
    limit = pltpu.CompilerParams(vmem_limit_bytes=24 * 1024 * 1024)
    most_room = pltpu.CompilerParams(vmem_limit_bytes=50 * 1024 * 1024)
    all_room = pltpu.CompilerParams(vmem_limit_bytes=60 * 1024 * 1024)
    in_vmem = pl.BlockSpec(memory_space=VMEM)
    in_hbm = pl.BlockSpec(memory_space=HBM)
    in_smem = pl.BlockSpec(memory_space=SMEM)
    anywhere = pl.BlockSpec(memory_space=pl.ANY)
    place = lax.axis_index("seq")
    at = place.reshape(1).astype(jnp.int32)

    def array(*shape, dtype=jnp.bfloat16):
        return jax.ShapeDtypeStruct(shape, dtype)

    def to_peer(value, m):
        return lax.ppermute(value, "seq", [(i, i ^ m) for i in range(peers)])

    def moves(size):
        return pl.CostEstimate(flops=0, bytes_accessed=size, transcendentals=0)

    sent, kept = pl.pallas_call(
        project_kernel,
        out_shape=(
            array(half, parts * columns + LANES),
            array(half, parts * columns + LANES, dtype=jnp.float32),
        ),
        in_specs=[in_smem] + [in_hbm] * 3,
        out_specs=(in_vmem, in_vmem),
        scratch_shapes=[
            pltpu.VMEM(states.shape, jnp.bfloat16),
            pltpu.VMEM(norm_gain.shape, jnp.bfloat16),
            pltpu.VMEM((parts, depth, columns), jnp.bfloat16),
            pltpu.SemaphoreType.DMA((parts + 2,)),
        ],
        compiler_params=all_room,
        name="project",
    )(at, states, norm_gain, w_qkv)
    received = to_peer(sent, 1)

    positions = lax.dynamic_slice_in_dim(context_len, place % 2 * half, half) - 1
    pair = (jnp.arange(columns, dtype=jnp.int32) % (HEAD_DIM // 2)).astype(jnp.float32)
    frequency = 10000.0 ** (-pair * 2.0 / HEAD_DIM)
    angles = positions.astype(jnp.float32)[:, None] * frequency[None, :]

    table = (block_owner, block_index, context_len)
    plan = pl.pallas_call(
        functools.partial(plan_kernel, tokens),
        out_shape=(
            array(rows, half),
            array(rows, half),
            array(rows, LANES, dtype=jnp.int32),
            array(rows, LANES, dtype=jnp.float32),
        ),
        in_specs=[in_smem] * 4,
        compiler_params=limit,
        name="plan",
    )(at, *table)
    keys, updated = pl.pallas_call(
        stage_keys_kernel,
        out_shape=(array(blocks, tokens, columns), array(*cache.shape)),
        in_specs=[in_hbm],
        out_specs=(in_vmem, in_hbm),
        scratch_shapes=[pltpu.SemaphoreType.DMA((steps,))] * 2,
        compiler_params=most_room,
        cost_estimate=moves(cache.size * 2),
        name="stage_keys",
    )(cache)

    message = columns // LANES * (half + 2 * share) + ROWS * pl.cdiv(half, LANES)
    *sends, query, fresh = pl.pallas_call(
        halve_kernel,
        out_shape=(
            *(array(message, LANES) for _ in range(1, lines)),
            array(half, columns + LANES, dtype=jnp.float32),
            array(share, 2 * columns, dtype=jnp.float32),
        ),
        in_specs=[in_smem, in_vmem, in_vmem, anywhere],
        scratch_shapes=[pltpu.VMEM((half, parts * columns + LANES), jnp.float32)],
        compiler_params=limit,
        name="halve",
    )(at, kept, received, keys)
    received = [to_peer(sends[m - 1], 2 * m) for m in sorted(range(1, lines), key=lambda m: (m == 1, m))]
    values, updated = pl.pallas_call(
        stage_values_kernel,
        out_shape=(array(blocks, tokens, columns), array(*cache.shape)),
        in_specs=[in_hbm, in_hbm],
        out_specs=(in_vmem, in_hbm),
        scratch_shapes=[pltpu.SemaphoreType.DMA((steps,))] * 2,
        input_output_aliases={1: 1},
        compiler_params=pltpu.CompilerParams(vmem_limit_bytes=47 * 1024 * 1024),
        cost_estimate=moves(cache.size * 2),
        name="stage_values",
    )(cache, updated)
    mine, news = pl.pallas_call(
        functools.partial(finish_kernel, depth * peers),
        out_shape=(array(half, columns), array(2 * share, columns + LANES)),
        in_specs=[in_smem, anywhere] + [in_vmem] * (4 + len(received)),
        compiler_params=pltpu.CompilerParams(vmem_limit_bytes=47 * 1024 * 1024),
        name="finish",
    )(at, values, query, fresh, jnp.cos(angles), jnp.sin(angles), *received)
    other = to_peer(mine, 1)

    piece = pl.pallas_call(
        attend_kernel,
        out_shape=array(2 * share + blocks, columns + LANES),
        in_specs=[in_vmem] * 9,
        compiler_params=pltpu.CompilerParams(vmem_limit_bytes=47 * 1024 * 1024),
        name="attend",
    )(mine, other, *plan, news, keys, values)
    pieces = [piece] * peers
    far = sorted(range(1, lines), key=lambda m: m)
    for m in far:
        pieces[2 * m] = to_peer(piece, 2 * m)
    for m in (*far, 0):
        pieces[2 * m + 1] = to_peer(pieces[2 * m], 1)

    near = pl.pallas_call(
        fetch_kernel,
        out_shape=array(blocks, 2, ROWS, columns),
        in_specs=[in_smem] * 3 + [anywhere, in_hbm],
        out_specs=in_vmem,
        scratch_shapes=[pltpu.SemaphoreType.DMA((blocks,))],
        compiler_params=most_room,
        cost_estimate=moves(blocks * ROWS * columns * 8),
        name="fetch",
    )(*table, piece, cache)
    rank = lax.axis_index("tp")
    kept_rows = requests // ranks
    own, *sends = pl.pallas_call(
        functools.partial(output_kernel, peers),
        out_shape=(
            array(kept_rows, out_columns, dtype=jnp.float32),
            *(array(kept_rows, out_columns, dtype=jnp.bfloat16) for _ in range(1, ranks)),
        ),
        in_specs=[in_smem] + [in_vmem] * (peers + 2) + [anywhere],
        out_specs=(in_vmem,) * ranks,
        scratch_shapes=[pltpu.VMEM((requests, out_columns), jnp.float32)],
        compiler_params=limit,
        name="output",
    )(rank.reshape(1).astype(jnp.int32), *pieces, w_out, states, near)
    total = own
    for m in range(1, ranks):
        moved = lax.ppermute(sends[m - 1], "tp", [(i, i ^ m) for i in range(ranks)])
        total = total + moved.astype(jnp.float32)
    updated = pl.pallas_call(
        functools.partial(patch_kernel, peers),
        out_shape=array(*cache.shape),
        in_specs=[in_smem] * 4 + [anywhere] + [in_vmem] * (peers + 1) + [in_hbm],
        out_specs=in_hbm,
        scratch_shapes=[
            pltpu.VMEM((peers, 2 * share, columns), jnp.float32),
            pltpu.VMEM((blocks, 2, ROWS, columns), jnp.bfloat16),
            pltpu.SemaphoreType.DMA((blocks,)),
        ],
        input_output_aliases={6 + peers: 0},
        compiler_params=most_room,
        cost_estimate=moves(blocks * ROWS * columns * 8),
        name="patch",
    )(at, *table, sends[0], *pieces, near, updated)
    return (total.astype(jnp.bfloat16), updated)


def solution(mesh):
    return jax.shard_map(
        shards,
        mesh=mesh,
        in_specs=(
            P(None, "seq"),
            P("seq"),
            P(None, "seq", "tp"),
            P("tp", "seq"),
            P("seq", None, None, "tp"),
            P(),
            P("seq"),
            P("seq"),
        ),
        out_specs=(P("tp", "seq"), P("seq", None, None, "tp")),
        check_vma=False,
    )
```

```python
import functools

import jax
import jax.numpy as jnp
from jax import lax
from jax.experimental import pallas as pl
from jax.experimental.pallas import tpu as pltpu
from jax.sharding import PartitionSpec as P

HEAD_DIM = 96
EPSILON = 1e-05
NEG_FLOOR = -1e30
LANES = 128
GROUP = 4

VMEM = pltpu.MemorySpace.VMEM
HBM = pltpu.MemorySpace.HBM
SMEM = pltpu.MemorySpace.SMEM
HEADS = 8
ROWS = 16
JOINS = 2


def split3(value):
    high = value.astype(jnp.bfloat16).astype(jnp.float32)
    rest = value - high
    mid = rest.astype(jnp.bfloat16).astype(jnp.float32)
    low = (rest - mid).astype(jnp.bfloat16).astype(jnp.float32)
    return high, mid, low


def lanes_of(terms):
    lane = lax.broadcasted_iota(jnp.int32, (terms[0].shape[0], LANES), 1)
    out = jnp.zeros(lane.shape, jnp.float32)
    for j, term in enumerate(terms):
        out = jnp.where(lane == j, term, out)
    return out


def project_kernel(
    place_ref,
    states_ref,
    gain_ref,
    w_ref,
    sent_ref,
    kept_ref,
    sent_fresh_ref,
    kept_fresh_ref,
    states_buf,
    gain_buf,
    w_buf,
    sems,
):
    parts, _, columns = w_ref.shape
    half = sent_ref.shape[0]
    small = [
        pltpu.make_async_copy(states_ref, states_buf, sems.at[parts]),
        pltpu.make_async_copy(gain_ref, gain_buf, sems.at[parts + 1]),
    ]
    copies = [pltpu.make_async_copy(w_ref.at[c], w_buf.at[c], sems.at[c]) for c in range(parts)]
    for copy in small + copies:
        copy.start()
    for copy in small:
        copy.wait()
    side = place_ref[0] % 2
    rows = [
        states_buf[pl.ds(pl.multiple_of(first * half, half), half), :].astype(jnp.float32)
        for first in (1 - side, side)
    ]
    wide = jnp.concatenate(rows, axis=0)
    gain = gain_buf[...].astype(jnp.float32)
    scaled = (wide * gain.reshape(1, wide.shape[1])).astype(jnp.bfloat16)
    stat = lanes_of(split3(jnp.sum(wide * wide, axis=1, keepdims=True)))
    sent_ref[:, columns:] = stat[:half].astype(jnp.bfloat16)
    kept_ref[:, columns:] = stat[half:]
    places = [(sent_ref, kept_ref, 0), (sent_fresh_ref, kept_fresh_ref, 0)]
    places.append((sent_fresh_ref, kept_fresh_ref, columns))
    for c, (sent, kept, first) in enumerate(places):
        copies[c].wait()
        term = jnp.dot(scaled, w_buf[c], preferred_element_type=jnp.float32)
        here = slice(first, first + columns)
        sent[:, here] = term[:half].astype(jnp.bfloat16)
        kept[:, here] = term[half:]


def flat(value):
    chunks = value.shape[1] // LANES
    return [value[:, c * LANES : (c + 1) * LANES] for c in range(chunks)]


def sum_plan(lines):
    masks = [1 << k for k in range(lines.bit_length() - 1)]
    steps = []
    for k, mask in enumerate(masks):
        kept = [0]
        for later in masks[k + 1 :]:
            kept = kept + [offset ^ later for offset in kept]
        steps.append((mask, [mask ^ offset for offset in kept], kept))
    return steps


def halve_query_kernel(kept_ref, recv_ref, after_ref, planned_ref, send, query_ref):
    columns = query_ref.shape[1] - LANES
    half = kept_ref.shape[0]
    total = kept_ref[...] + recv_ref[...].astype(jnp.float32)
    squares = jnp.sum(total[:, columns:], axis=1, keepdims=True)
    query_ref[:, :columns] = total[:, :columns]
    query_ref[:, columns:] = lanes_of([squares])
    pads = -half % LANES
    stat = [jnp.pad(term, ((0, pads), (0, 0))) for term in split3(squares)]
    lane = lax.broadcasted_iota(jnp.int32, (half + pads, half + pads), 1)
    row = lax.broadcasted_iota(jnp.int32, (half + pads, half + pads), 0)
    stat = [jnp.sum(jnp.where(lane == row, t, 0.0), axis=0, keepdims=True) for t in stat]
    stat = jnp.concatenate(stat + [jnp.zeros((ROWS - 3, half + pads), jnp.float32)], axis=0)
    chunks = columns // LANES
    send[: chunks * half, :] = jnp.concatenate(flat(total[:, :columns]), axis=0).astype(jnp.bfloat16)
    send[chunks * half :, :] = jnp.concatenate(flat(stat), axis=0).astype(jnp.bfloat16)


def halve_fresh_kernel(sent, held, place_ref, kept_ref, recv_ref, send_ref, fresh_ref, total):
    share = fresh_ref.shape[0] // len(held)
    total[...] = kept_ref[...] + recv_ref[...].astype(jnp.float32)
    line = place_ref[0] // 2

    def rows_of(offsets):
        rows = [
            total[pl.ds(pl.multiple_of((line ^ offset) * share, share), share), :]
            for offset in offsets
        ]
        return jnp.concatenate(rows, axis=0)

    fresh_ref[...] = rows_of(held)
    send_ref[...] = rows_of(sent).astype(jnp.bfloat16)


def fold_kernel(offsets, sent, held, fresh_in, recv_ref, send_ref, fresh_ref):
    share = fresh_ref.shape[0] // len(held)
    fresh = fresh_in[...] + recv_ref[...].astype(jnp.float32)

    def rows_of(wanted):
        at = [offsets.index(offset) * share for offset in wanted]
        return jnp.concatenate([fresh[first : first + share] for first in at], axis=0)

    fresh_ref[...] = rows_of(held)
    send_ref[...] = rows_of(sent).astype(jnp.bfloat16)


def rotated(x, cosine, sine):
    columns = x.shape[1]
    span = HEAD_DIM // 2
    front = lax.broadcasted_iota(jnp.int32, x.shape, 1) % HEAD_DIM < span
    other = jnp.where(front, -pltpu.roll(x, columns - span, 1), pltpu.roll(x, span, 1))
    return x * cosine + other * sine


def query_kernel(width, after_ref, query_ref, cos_ref, sin_ref, *rest):
    received, out_ref, scale_ref = rest[:-2], rest[-2], rest[-1]
    half, columns = out_ref.shape
    chunks = columns // LANES
    total = flat(query_ref[:, :columns])
    squares = query_ref[:, columns : columns + 1]
    stat = jnp.zeros((received[0].shape[0] - chunks * half, LANES), jnp.float32)
    for piece in received:
        for c in range(chunks):
            total[c] = total[c] + piece[c * half : (c + 1) * half, :].astype(jnp.float32)
        stat = stat + piece[chunks * half :, :].astype(jnp.float32)
    stat = [jnp.sum(stat[r : r + ROWS], axis=0, keepdims=True) for r in range(0, stat.shape[0], ROWS)]
    stat = jnp.concatenate(stat, axis=1)
    lane = lax.broadcasted_iota(jnp.int32, (half, stat.shape[1]), 1)
    row = lax.broadcasted_iota(jnp.int32, (half, stat.shape[1]), 0)
    squares = squares + jnp.sum(jnp.where(lane == row, stat, 0.0), axis=1, keepdims=True)
    inverse = lax.rsqrt(squares * (1.0 / width) + EPSILON)
    query = rotated(jnp.concatenate(total, axis=1) * inverse, cos_ref[...], sin_ref[...])
    out_ref[...] = (query * HEAD_DIM ** (-0.5)).astype(jnp.bfloat16)
    scale_ref[...] = jnp.broadcast_to(inverse, scale_ref.shape)


def news_kernel(
    place_ref,
    query_ref,
    scale_ref,
    cos_ref,
    sin_ref,
    fresh_ref,
    recv_ref,
    part_ref,
    stat_ref,
    out_ref,
    wide,
):
    half, columns = query_ref.shape
    share = fresh_ref.shape[0]
    line = place_ref[0] // 2
    here = pl.ds(pl.multiple_of(line * share, share), share)
    wide[...] = query_ref[...].astype(jnp.float32)
    fresh = (fresh_ref[...] + recv_ref[...].astype(jnp.float32)) * scale_ref[here, 0:1]
    key = rotated(fresh[:, :columns], cos_ref[here, :], sin_ref[here, :])
    product = wide[here, :] * key.astype(jnp.bfloat16).astype(jnp.float32)
    lane_head = lax.broadcasted_iota(jnp.int32, product.shape, 1) // HEAD_DIM
    lane = lax.broadcasted_iota(jnp.int32, (share, LANES), 1)
    first = (place_ref[0] % 2) * half + line * share
    owner = lax.broadcasted_iota(jnp.int32, (share, LANES), 0) + first
    stat = jnp.where(lane == 6 * HEADS, owner.astype(jnp.float32), 0.0)
    for h in range(HEADS):
        score = jnp.sum(jnp.where(lane_head == h, product, 0.0), axis=1, keepdims=True)
        for j, term in enumerate(split3(score)):
            stat = jnp.where(lane == j * HEADS + h, term, stat)
        stat = jnp.where(lane == 3 * HEADS + h, 1.0, stat)
    part = part_ref[...]
    part = jnp.concatenate([fresh[:, columns:], part[share:]], axis=0)
    stat = jnp.concatenate([stat_ref[:share, :] + stat, stat_ref[share:, :]], axis=0)
    first = 0
    for value in (part[:ROWS], part[ROWS:], key, stat):
        value = jnp.concatenate(flat(value), axis=0).astype(jnp.bfloat16)
        out_ref[first : first + value.shape[0], :] = value
        first += value.shape[0]


def stage(part, cache_ref, near_ref, updated_ref, loads, stores):
    spans = [pl.ds(first, GROUP) for first in range(0, cache_ref.shape[0], GROUP)]
    load = [
        pltpu.make_async_copy(cache_ref.at[span, part], near_ref.at[span], loads.at[i])
        for i, span in enumerate(spans)
    ]
    store = [
        pltpu.make_async_copy(near_ref.at[span], updated_ref.at[span, part], stores.at[i])
        for i, span in enumerate(spans)
    ]
    for copy in load:
        copy.start()
    for arriving, leaving in zip(load, store):
        arriving.wait()
        leaving.start()
    for copy in store:
        copy.wait()


def stage_keys_kernel(cache_ref, keys_ref, updated_ref, loads, stores):
    stage(0, cache_ref, keys_ref, updated_ref, loads, stores)


def stage_values_kernel(cache_ref, values_ref, loads):
    copies = [
        pltpu.make_async_copy(
            cache_ref.at[pl.ds(first, GROUP), 1], values_ref.at[pl.ds(first, GROUP)], loads.at[i]
        )
        for i, first in enumerate(range(0, cache_ref.shape[0], GROUP))
    ]
    for copy in copies:
        copy.start()
    for copy in copies:
        copy.wait()


def read_block(b, owner_ref, index_ref, length_ref, tokens):
    requests = length_ref.shape[0]
    owner = owner_ref[b]
    reach = length_ref[jnp.minimum(owner, requests - 1)] - index_ref[b] * tokens
    live = owner < requests
    old = jnp.where(live, jnp.clip(reach - 1, 0, tokens), 0)
    slot = jnp.where(live & (reach >= 1) & (reach <= tokens), reach - 1, -1)
    return owner, old, slot


def plan_kernel(
    tokens,
    place_ref,
    owner_ref,
    index_ref,
    length_ref,
    mine_ref,
    other_ref,
    seen_ref,
    name_ref,
):
    blocks = owner_ref.shape[0]
    half = mine_ref.shape[1]
    side = place_ref[0] % 2
    lane = lax.broadcasted_iota(jnp.int32, (HEADS, half), 1)
    picks = [], []
    for b in range(blocks):
        owner, old, _ = read_block(b, owner_ref, index_ref, length_ref, tokens)
        here = pl.ds(b * HEADS, HEADS)
        for pick, first in zip(picks, (side, 1 - side)):
            pick.append((lane == owner - first * half).astype(jnp.float32))
        seen_ref[here, :] = jnp.full((HEADS, LANES), old, jnp.int32)
        name_ref[here, :] = jnp.full((HEADS, LANES), owner, jnp.int32).astype(jnp.float32)
    mine_ref[...] = jnp.concatenate(picks[0], axis=0).astype(jnp.bfloat16)
    other_ref[...] = jnp.concatenate(picks[1], axis=0).astype(jnp.bfloat16)


def attend_kernel(
    mine_ref,
    other_ref,
    pick_mine_ref,
    pick_other_ref,
    seen_ref,
    name_ref,
    keys_ref,
    values_ref,
    part_ref,
    stat_ref,
):
    blocks, tokens, columns = keys_ref.shape
    steps = blocks // GROUP

    def iota(shape, dim):
        return lax.broadcasted_iota(jnp.int32, shape, dim)

    rows = blocks * HEADS
    size = GROUP * HEADS
    width = GROUP * tokens
    own = jnp.dot(pick_mine_ref[...], mine_ref[...], preferred_element_type=jnp.float32)
    own = own + jnp.dot(pick_other_ref[...], other_ref[...], preferred_element_type=jnp.float32)
    head_mask = iota((rows, columns), 1) // HEAD_DIM == iota((rows, columns), 0) % HEADS
    queries = jnp.where(head_mask, own, 0.0).astype(jnp.bfloat16)
    scores = []
    for step in range(steps):
        keys = keys_ref[step * GROUP : (step + 1) * GROUP].reshape(width, columns)
        scores.append(
            lax.dot_general(
                queries[step * size : (step + 1) * size],
                keys,
                (((1,), (1,)), ((), ())),
                preferred_element_type=jnp.float32,
            )
        )
    scores = jnp.concatenate(scores, axis=0)
    column = iota((rows, width), 1)
    same = column // tokens == iota((rows, width), 0) // HEADS % GROUP
    place = jnp.where(same, column % tokens, tokens)
    visible = place < jnp.concatenate([seen_ref[...]] * (width // LANES), axis=1)
    masked = jnp.where(visible, scores, NEG_FLOOR)
    top = jnp.max(masked, axis=1, keepdims=True)
    weights = jnp.where(visible, jnp.exp(masked - top), 0.0).astype(jnp.bfloat16)
    mass = jnp.sum(weights.astype(jnp.float32), axis=1, keepdims=True)
    parts = []
    for step in range(steps):
        values = values_ref[step * GROUP : (step + 1) * GROUP].reshape(width, columns)
        parts.append(
            jnp.dot(
                weights[step * size : (step + 1) * size],
                values,
                preferred_element_type=jnp.float32,
            )
        )
    part = jnp.concatenate(parts, axis=0) * jnp.where(mass > 0.0, 1.0 / mass, 0.0)
    part = jnp.where(head_mask, part, 0.0).astype(jnp.bfloat16)
    fresh = part_ref.shape[0] - blocks
    lane = iota((rows, LANES), 1)
    head = iota((rows, LANES), 0) % HEADS
    spot = iota((rows, LANES), 0) // HEADS + fresh
    lane = lane - spot // ROWS * (LANES // 2)
    stat = jnp.where((lane == 6 * HEADS) & (head == 0), name_ref[...], 0.0)
    for j, term in enumerate(split3(top) + split3(mass)):
        stat = jnp.where(lane == head + j * HEADS, term, stat)
    spot = iota((2 * ROWS, rows), 1) // HEADS + fresh
    fold = (spot == iota((2 * ROWS, rows), 0)).astype(jnp.float32).astype(jnp.bfloat16)
    part_ref[...] = jnp.dot(fold, part, preferred_element_type=jnp.float32)
    spot = iota((ROWS, rows), 1) // HEADS + fresh
    fold = (spot % ROWS == iota((ROWS, rows), 0)).astype(jnp.float32).astype(jnp.bfloat16)
    stat_ref[...] = jnp.dot(fold, stat.astype(jnp.bfloat16), preferred_element_type=jnp.float32)


def slots(tokens, owner_ref, index_ref, length_ref):
    found = []
    for b in range(owner_ref.shape[0]):
        owner, _, slot = read_block(b, owner_ref, index_ref, length_ref, tokens)
        first = pl.multiple_of(jnp.maximum(slot, 0) // ROWS * ROWS, ROWS)
        found.append((b, owner, slot, first))
    return found


def each(found, do):
    for spot in found:
        pl.when(spot[2] >= 0)(functools.partial(do, *spot))


def fetch_kernel(
    owner_ref,
    index_ref,
    length_ref,
    after_ref,
    cache_ref,
    held_ref,
    updated_ref,
    near_ref,
    values,
    loads,
    stores,
    fetches,
):
    found = slots(cache_ref.shape[2], owner_ref, index_ref, length_ref)

    def fetch(b, owner, slot, first):
        return pltpu.make_async_copy(
            cache_ref.at[b, :, pl.ds(first, ROWS), :], near_ref.at[b], fetches.at[b]
        )

    spans = [pl.ds(first, GROUP) for first in range(0, cache_ref.shape[0], GROUP)]
    load = [
        pltpu.make_async_copy(cache_ref.at[span, 1], values.at[span], loads.at[i])
        for i, span in enumerate(spans)
    ]
    store = [
        pltpu.make_async_copy(values.at[span], updated_ref.at[span, 1], stores.at[i])
        for i, span in enumerate(spans)
    ]
    for copy in load:
        copy.start()
    each(found, lambda *at: fetch(*at).start())
    for arriving, leaving in zip(load, store):
        arriving.wait()
        leaving.start()
    each(found, lambda *at: fetch(*at).wait())
    for copy in store:
        copy.wait()


def join_kernel(*refs):
    out_ref = refs[-1]
    rows = refs[0].shape[0]
    for i, ref in enumerate(refs[:-1]):
        out_ref[i * rows : (i + 1) * rows, :] = ref[...]


def line_order(lines):
    return [0, *range(lines - 1, 0, -1)]


def pieces_of(column, crossed):
    rows = column[0].shape[0]
    each = len(column) // len(crossed)
    pieces = [None] * (2 * len(column))
    for i, m in enumerate(line_order(len(column))):
        first = i % each * rows
        pieces[2 * m] = column[i]
        pieces[2 * m + 1] = crossed[i // each].at[first : first + rows]
    return pieces


def patch_kernel(count, place_ref, owner_ref, index_ref, length_ref, after_ref, *rest):
    lines = count // 2
    pieces = pieces_of(rest[:lines], rest[lines : lines + JOINS])
    near_ref, held_ref, updated_ref, fresh, patch, stores = rest[lines + JOINS :]
    _, _, tokens, columns = updated_ref.shape
    requests = length_ref.shape[0]
    share = fresh.shape[1] // 2
    half = requests // 2

    def store(b, owner, slot, first):
        return pltpu.make_async_copy(
            patch.at[b], updated_ref.at[b, :, pl.ds(first, ROWS), :], stores.at[b]
        )

    for m in range(count):
        for c in range(columns // LANES):
            here = slice(c * LANES, (c + 1) * LANES)
            keys = 2 * columns // LANES * ROWS + c * share
            fresh[m, :share, here] = pieces[m][c * ROWS : c * ROWS + share, :].astype(jnp.float32)
            fresh[m, share:, here] = pieces[m][keys : keys + share, :].astype(jnp.float32)
    row = lax.broadcasted_iota(jnp.int32, (ROWS, columns), 0)

    def change(b, owner, slot, first):
        request = jnp.minimum(owner, requests - 1)
        device = request % half // share * 2 + request // half
        piece = place_ref[0] ^ device
        line = request % share
        for c in range(2):
            new = fresh[piece, pl.ds(line + (1 - c) * share, 1), :]
            old = near_ref[b, c].astype(jnp.float32)
            patch[b, c] = jnp.where(row == slot - first, new, old).astype(jnp.bfloat16)
        store(b, owner, slot, first).start()

    found = slots(tokens, owner_ref, index_ref, length_ref)
    each(found, change)
    each(found, lambda *at: store(*at).wait())


def output_kernel(count, place_ref, *rest):
    lines = count // 2
    pieces = pieces_of(rest[:lines], rest[lines : lines + JOINS])
    w_ref, states_ref, after_ref, own_ref, *sends, product = rest[lines + JOINS :]
    heads = HEADS
    columns = w_ref.shape[0]
    chunks = columns // LANES
    requests = states_ref.shape[0]
    total_blocks = count * 2 * ROWS

    def rows_of(first):
        rows = [
            jnp.concatenate(
                [piece[first + c * ROWS : first + (c + 1) * ROWS, :] for c in range(chunks)], axis=1
            )
            for piece in pieces
        ]
        return jnp.concatenate(rows, axis=0)

    parts = jnp.concatenate([rows_of(0), rows_of(chunks * ROWS)], axis=0)
    stat = jnp.concatenate([piece[-ROWS:, :] for piece in pieces], axis=0)
    row = lax.broadcasted_iota(jnp.int32, (3 * heads, LANES), 0)
    lane = lax.broadcasted_iota(jnp.int32, (3 * heads, LANES), 1)

    def terms(first):
        at = lane - first
        wanted = (row // heads == at // (3 * heads)) & (row % heads == at % heads) & (at >= 0)
        wanted = (wanted & (row < 2 * heads)) | ((row >= 2 * heads) & (at == 6 * heads))
        return lax.dot_general(
            wanted.astype(jnp.float32).astype(jnp.bfloat16),
            stat,
            (((1,), (1,)), ((), ())),
            preferred_element_type=jnp.float32,
        )

    stat = jnp.concatenate([terms(0), terms(LANES // 2)], axis=1)
    owner = stat[2 * heads : 2 * heads + 1]
    request = lax.broadcasted_iota(jnp.int32, (requests, total_blocks), 0).astype(jnp.float32)
    member = owner == request
    lane_head = lax.broadcasted_iota(jnp.int32, (requests, columns), 1) // HEAD_DIM
    factors = []
    for h in range(heads):
        top = jnp.where(member, stat[h : h + 1], NEG_FLOOR)
        highest = jnp.max(top, axis=1, keepdims=True)
        factor = jnp.where(member, jnp.exp(top - highest) * stat[heads + h : heads + h + 1], 0.0)
        factors.append(factor / jnp.sum(factor, axis=1, keepdims=True))
    factors = jnp.concatenate(factors, axis=0).astype(jnp.bfloat16)
    joined = jnp.dot(factors, parts, preferred_element_type=jnp.float32)
    attended = joined[:requests]
    for h in range(1, heads):
        attended = jnp.where(lane_head == h, joined[h * requests : (h + 1) * requests], attended)
    product[...] = jnp.dot(
        attended.astype(jnp.bfloat16), w_ref[...], preferred_element_type=jnp.float32
    )
    place = place_ref[0]
    share = own_ref.shape[0]
    mine = pl.ds(pl.multiple_of(place * share, share), share)
    own_ref[...] = product[mine, :] + states_ref[mine, :].astype(jnp.float32)
    for m, send in enumerate(sends, 1):
        theirs = pl.ds(pl.multiple_of((place ^ m) * share, share), share)
        send[...] = product[theirs, :].astype(send.dtype)


def shards(states, norm_gain, w_qkv, w_out, cache, context_len, block_owner, block_index):
    requests, depth = states.shape
    peers = lax.axis_size("seq")
    ranks = lax.axis_size("tp")
    parts, _, columns = w_qkv.shape
    blocks, _, tokens, _ = cache.shape
    half = requests // 2
    share = requests // peers
    lines = peers // 2
    out_columns = w_out.shape[1]
    rows = blocks * HEADS
    steps = blocks // GROUP
    limit = pltpu.CompilerParams(vmem_limit_bytes=24 * 1024 * 1024)
    most_room = pltpu.CompilerParams(vmem_limit_bytes=50 * 1024 * 1024)
    all_room = pltpu.CompilerParams(vmem_limit_bytes=60 * 1024 * 1024)
    in_vmem = pl.BlockSpec(memory_space=VMEM)
    in_hbm = pl.BlockSpec(memory_space=HBM)
    in_smem = pl.BlockSpec(memory_space=SMEM)
    anywhere = pl.BlockSpec(memory_space=pl.ANY)
    place = lax.axis_index("seq")
    at = place.reshape(1).astype(jnp.int32)

    def array(*shape, dtype=jnp.bfloat16):
        return jax.ShapeDtypeStruct(shape, dtype)

    def to_peer(value, m):
        return lax.ppermute(value, "seq", [(i, i ^ m) for i in range(peers)])

    def moves(size):
        return pl.CostEstimate(flops=0, bytes_accessed=size, transcendentals=0)

    sent, kept, sent_fresh, kept_fresh = pl.pallas_call(
        project_kernel,
        out_shape=(
            array(half, columns + LANES),
            array(half, columns + LANES, dtype=jnp.float32),
            array(half, 2 * columns),
            array(half, 2 * columns, dtype=jnp.float32),
        ),
        in_specs=[in_smem] + [in_hbm] * 3,
        out_specs=(in_vmem,) * 4,
        scratch_shapes=[
            pltpu.VMEM(states.shape, jnp.bfloat16),
            pltpu.VMEM(norm_gain.shape, jnp.bfloat16),
            pltpu.VMEM((parts, depth, columns), jnp.bfloat16),
            pltpu.SemaphoreType.DMA((parts + 2,)),
        ],
        compiler_params=all_room,
        name="project",
    )(at, states, norm_gain, w_qkv)
    received = to_peer(sent, 1)
    fresh_received = to_peer(sent_fresh, 1)

    positions = lax.dynamic_slice_in_dim(context_len, place % 2 * half, half) - 1
    pair = (jnp.arange(columns, dtype=jnp.int32) % (HEAD_DIM // 2)).astype(jnp.float32)
    frequency = 10000.0 ** (-pair * 2.0 / HEAD_DIM)
    angles = positions.astype(jnp.float32)[:, None] * frequency[None, :]

    table = (block_owner, block_index, context_len)
    plan = pl.pallas_call(
        functools.partial(plan_kernel, tokens),
        out_shape=(
            array(rows, half),
            array(rows, half),
            array(rows, LANES, dtype=jnp.int32),
            array(rows, LANES, dtype=jnp.float32),
        ),
        in_specs=[in_smem] * 4,
        compiler_params=limit,
        name="plan",
    )(at, *table)
    keys, updated = pl.pallas_call(
        stage_keys_kernel,
        out_shape=(array(blocks, tokens, columns), array(*cache.shape)),
        in_specs=[in_hbm],
        out_specs=(in_vmem, in_hbm),
        scratch_shapes=[pltpu.SemaphoreType.DMA((steps,))] * 2,
        compiler_params=most_room,
        cost_estimate=moves(cache.size * 2),
        name="stage_keys",
    )(cache)

    values = pl.pallas_call(
        stage_values_kernel,
        out_shape=array(blocks, tokens, columns),
        in_specs=[in_hbm],
        out_specs=in_vmem,
        scratch_shapes=[pltpu.SemaphoreType.DMA((steps,))],
        compiler_params=most_room,
        cost_estimate=moves(cache.size),
        name="stage_values",
    )(cache)
    message = columns // LANES * half + ROWS * pl.cdiv(half, LANES)
    send, query = pl.pallas_call(
        halve_query_kernel,
        out_shape=(array(message, LANES), array(half, columns + LANES, dtype=jnp.float32)),
        in_specs=[in_vmem, in_vmem, anywhere, anywhere],
        compiler_params=pltpu.CompilerParams(vmem_limit_bytes=47 * 1024 * 1024),
        name="halve_query",
    )(kept, received, values, plan[0])
    received = [to_peer(send, 2 * m) for m in line_order(lines)[1:]]
    (mask, sent_to, held), *later = sum_plan(lines)
    fresh_send, fresh = pl.pallas_call(
        functools.partial(halve_fresh_kernel, sent_to, held),
        out_shape=(
            array(share * len(sent_to), 2 * columns),
            array(share * len(held), 2 * columns, dtype=jnp.float32),
        ),
        in_specs=[in_smem, in_vmem, in_vmem],
        scratch_shapes=[pltpu.VMEM((half, 2 * columns), jnp.float32)],
        compiler_params=limit,
        name="halve_fresh",
    )(at, kept_fresh, fresh_received)
    fresh_received = to_peer(fresh_send, 2 * mask)
    for mask, sent_to, still in later:
        fresh_send, fresh = pl.pallas_call(
            functools.partial(fold_kernel, held, sent_to, still),
            out_shape=(
                array(share * len(sent_to), 2 * columns),
                array(share * len(still), 2 * columns, dtype=jnp.float32),
            ),
            compiler_params=limit,
            name="fold",
        )(fresh, fresh_received)
        held = still
        fresh_received = to_peer(fresh_send, 2 * mask)
    cosine, sine = jnp.cos(angles), jnp.sin(angles)
    mine, scale = pl.pallas_call(
        functools.partial(query_kernel, depth * peers),
        out_shape=(array(half, columns), array(half, LANES, dtype=jnp.float32)),
        in_specs=[anywhere] + [in_vmem] * (3 + len(received)),
        compiler_params=pltpu.CompilerParams(vmem_limit_bytes=47 * 1024 * 1024),
        name="query",
    )(keys, query, cosine, sine, *received)
    other = to_peer(mine, 1)

    part, stat = pl.pallas_call(
        attend_kernel,
        out_shape=(
            array(2 * ROWS, columns, dtype=jnp.float32),
            array(ROWS, LANES, dtype=jnp.float32),
        ),
        in_specs=[in_vmem] * 8,
        compiler_params=pltpu.CompilerParams(vmem_limit_bytes=47 * 1024 * 1024),
        name="attend",
    )(mine, other, *plan, keys, values)
    piece = pl.pallas_call(
        news_kernel,
        out_shape=array(columns // LANES * (2 * ROWS + share) + ROWS, LANES),
        in_specs=[in_smem] + [in_vmem] * 8,
        scratch_shapes=[pltpu.VMEM((half, columns), jnp.float32)],
        compiler_params=limit,
        name="news",
    )(at, mine, scale, cosine, sine, fresh, fresh_received, part, stat)
    column = [to_peer(piece, 2 * m) if m else piece for m in line_order(lines)]
    each = lines // JOINS
    pieces = list(column)
    for first in range(0, lines, each):
        joined = pl.pallas_call(
            join_kernel,
            out_shape=array(each * piece.shape[0], LANES),
            compiler_params=limit,
            name="join",
        )(*column[first : first + each])
        pieces.append(to_peer(joined, 1))
    updated, near = pl.pallas_call(
        fetch_kernel,
        out_shape=(array(*cache.shape), array(blocks, 2, ROWS, columns)),
        in_specs=[in_smem] * 3 + [anywhere, in_hbm, in_hbm],
        out_specs=(in_hbm, in_vmem),
        scratch_shapes=[
            pltpu.VMEM((blocks, tokens, columns), jnp.bfloat16),
            pltpu.SemaphoreType.DMA((steps,)),
            pltpu.SemaphoreType.DMA((steps,)),
            pltpu.SemaphoreType.DMA((blocks,)),
        ],
        input_output_aliases={5: 0},
        compiler_params=most_room,
        cost_estimate=moves(cache.size * 2),
        name="fetch",
    )(*table, piece, cache, updated)
    rank = lax.axis_index("tp")
    kept_rows = requests // ranks
    own, *sends = pl.pallas_call(
        functools.partial(output_kernel, peers),
        out_shape=(
            array(kept_rows, out_columns, dtype=jnp.float32),
            *(array(kept_rows, out_columns, dtype=jnp.bfloat16) for _ in range(1, ranks)),
        ),
        in_specs=[in_smem] + [in_vmem] * (len(pieces) + 2) + [anywhere],
        out_specs=(in_vmem,) * ranks,
        scratch_shapes=[pltpu.VMEM((requests, out_columns), jnp.float32)],
        compiler_params=limit,
        name="output",
    )(rank.reshape(1).astype(jnp.int32), *pieces, w_out, states, near)
    total = own
    for m in range(1, ranks):
        moved = lax.ppermute(sends[m - 1], "tp", [(i, i ^ m) for i in range(ranks)])
        total = total + moved.astype(jnp.float32)
    updated = pl.pallas_call(
        functools.partial(patch_kernel, peers),
        out_shape=array(*cache.shape),
        in_specs=[in_smem] * 4 + [anywhere] + [in_vmem] * (len(pieces) + 1) + [in_hbm],
        out_specs=in_hbm,
        scratch_shapes=[
            pltpu.VMEM((peers, 2 * share, columns), jnp.float32),
            pltpu.VMEM((blocks, 2, ROWS, columns), jnp.bfloat16),
            pltpu.SemaphoreType.DMA((blocks,)),
        ],
        input_output_aliases={6 + len(pieces): 0},
        compiler_params=most_room,
        cost_estimate=moves(blocks * ROWS * columns * 8),
        name="patch",
    )(at, *table, sends[0], *pieces, near, updated)
    return (total.astype(jnp.bfloat16), updated)


def solution(mesh):
    return jax.shard_map(
        shards,
        mesh=mesh,
        in_specs=(
            P(None, "seq"),
            P("seq"),
            P(None, "seq", "tp"),
            P("tp", "seq"),
            P("seq", None, None, "tp"),
            P(),
            P("seq"),
            P("seq"),
        ),
        out_specs=(P("tp", "seq"), P("seq", None, None, "tp")),
        check_vma=False,
    )
```

```python
import functools

import jax
import jax.numpy as jnp
from jax import lax
from jax.experimental import pallas as pl
from jax.experimental.pallas import tpu as pltpu
from jax.sharding import PartitionSpec as P

HEAD_DIM = 96
EPSILON = 1e-05
NEG_FLOOR = -1e30
LANES = 128
GROUP = 4

VMEM = pltpu.MemorySpace.VMEM
HBM = pltpu.MemorySpace.HBM
SMEM = pltpu.MemorySpace.SMEM
HEADS = 8
ROWS = 16


def split3(value):
    high = value.astype(jnp.bfloat16).astype(jnp.float32)
    rest = value - high
    mid = rest.astype(jnp.bfloat16).astype(jnp.float32)
    low = (rest - mid).astype(jnp.bfloat16).astype(jnp.float32)
    return high, mid, low


def lanes_of(terms):
    lane = lax.broadcasted_iota(jnp.int32, (terms[0].shape[0], LANES), 1)
    out = jnp.zeros(lane.shape, jnp.float32)
    for j, term in enumerate(terms):
        out = jnp.where(lane == j, term, out)
    return out


def project_kernel(
    place_ref,
    states_ref,
    gain_ref,
    w_ref,
    sent_ref,
    kept_ref,
    sent_fresh_ref,
    kept_fresh_ref,
    states_buf,
    gain_buf,
    w_buf,
    sems,
):
    parts, _, columns = w_ref.shape
    half = sent_ref.shape[0]
    small = [
        pltpu.make_async_copy(states_ref, states_buf, sems.at[parts]),
        pltpu.make_async_copy(gain_ref, gain_buf, sems.at[parts + 1]),
    ]
    copies = [pltpu.make_async_copy(w_ref.at[c], w_buf.at[c], sems.at[c]) for c in range(parts)]
    for copy in small + copies:
        copy.start()
    for copy in small:
        copy.wait()
    side = place_ref[0] % 2
    rows = [
        states_buf[pl.ds(pl.multiple_of(first * half, half), half), :].astype(jnp.float32)
        for first in (1 - side, side)
    ]
    wide = jnp.concatenate(rows, axis=0)
    gain = gain_buf[...].astype(jnp.float32)
    scaled = (wide * gain.reshape(1, wide.shape[1])).astype(jnp.bfloat16)
    stat = lanes_of(split3(jnp.sum(wide * wide, axis=1, keepdims=True)))
    sent_ref[:, columns:] = stat[:half].astype(jnp.bfloat16)
    kept_ref[:, columns:] = stat[half:]
    places = [(sent_ref, kept_ref, 0), (sent_fresh_ref, kept_fresh_ref, 0)]
    places.append((sent_fresh_ref, kept_fresh_ref, columns))
    for c, (sent, kept, first) in enumerate(places):
        copies[c].wait()
        term = jnp.dot(scaled, w_buf[c], preferred_element_type=jnp.float32)
        here = slice(first, first + columns)
        sent[:, here] = term[:half].astype(jnp.bfloat16)
        kept[:, here] = term[half:]


def flat(value):
    chunks = value.shape[1] // LANES
    return [value[:, c * LANES : (c + 1) * LANES] for c in range(chunks)]


def sum_plan(lines):
    masks = [1 << k for k in range(lines.bit_length() - 1)]
    steps = []
    for k, mask in enumerate(masks):
        kept = [0]
        for later in masks[k + 1 :]:
            kept = kept + [offset ^ later for offset in kept]
        steps.append((mask, [mask ^ offset for offset in kept], kept))
    return steps


def halve_query_kernel(kept_ref, recv_ref, after_ref, planned_ref, send, query_ref):
    columns = query_ref.shape[1] - LANES
    half = kept_ref.shape[0]
    total = kept_ref[...] + recv_ref[...].astype(jnp.float32)
    squares = jnp.sum(total[:, columns:], axis=1, keepdims=True)
    query_ref[:, :columns] = total[:, :columns]
    query_ref[:, columns:] = lanes_of([squares])
    pads = -half % LANES
    stat = [jnp.pad(term, ((0, pads), (0, 0))) for term in split3(squares)]
    lane = lax.broadcasted_iota(jnp.int32, (half + pads, half + pads), 1)
    row = lax.broadcasted_iota(jnp.int32, (half + pads, half + pads), 0)
    stat = [jnp.sum(jnp.where(lane == row, t, 0.0), axis=0, keepdims=True) for t in stat]
    stat = jnp.concatenate(stat + [jnp.zeros((ROWS - 3, half + pads), jnp.float32)], axis=0)
    chunks = columns // LANES
    send[: chunks * half, :] = jnp.concatenate(flat(total[:, :columns]), axis=0).astype(jnp.bfloat16)
    send[chunks * half :, :] = jnp.concatenate(flat(stat), axis=0).astype(jnp.bfloat16)


def halve_fresh_kernel(sent, held, place_ref, kept_ref, recv_ref, send_ref, fresh_ref, total):
    share = fresh_ref.shape[0] // len(held)
    total[...] = kept_ref[...] + recv_ref[...].astype(jnp.float32)
    line = place_ref[0] // 2

    def rows_of(offsets):
        rows = [
            total[pl.ds(pl.multiple_of((line ^ offset) * share, share), share), :]
            for offset in offsets
        ]
        return jnp.concatenate(rows, axis=0)

    fresh_ref[...] = rows_of(held)
    send_ref[...] = rows_of(sent).astype(jnp.bfloat16)


def fold_kernel(offsets, sent, held, fresh_in, recv_ref, send_ref, fresh_ref):
    share = fresh_ref.shape[0] // len(held)
    fresh = fresh_in[...] + recv_ref[...].astype(jnp.float32)

    def rows_of(wanted):
        at = [offsets.index(offset) * share for offset in wanted]
        return jnp.concatenate([fresh[first : first + share] for first in at], axis=0)

    fresh_ref[...] = rows_of(held)
    send_ref[...] = rows_of(sent).astype(jnp.bfloat16)


def rotated(x, cosine, sine):
    columns = x.shape[1]
    span = HEAD_DIM // 2
    front = lax.broadcasted_iota(jnp.int32, x.shape, 1) % HEAD_DIM < span
    other = jnp.where(front, -pltpu.roll(x, columns - span, 1), pltpu.roll(x, span, 1))
    return x * cosine + other * sine


def query_kernel(width, after_ref, query_ref, cos_ref, sin_ref, *rest):
    received, out_ref, scale_ref = rest[:-2], rest[-2], rest[-1]
    half, columns = out_ref.shape
    chunks = columns // LANES
    total = flat(query_ref[:, :columns])
    squares = query_ref[:, columns : columns + 1]
    stat = jnp.zeros((received[0].shape[0] - chunks * half, LANES), jnp.float32)
    for piece in received:
        for c in range(chunks):
            total[c] = total[c] + piece[c * half : (c + 1) * half, :].astype(jnp.float32)
        stat = stat + piece[chunks * half :, :].astype(jnp.float32)
    stat = [jnp.sum(stat[r : r + ROWS], axis=0, keepdims=True) for r in range(0, stat.shape[0], ROWS)]
    stat = jnp.concatenate(stat, axis=1)
    lane = lax.broadcasted_iota(jnp.int32, (half, stat.shape[1]), 1)
    row = lax.broadcasted_iota(jnp.int32, (half, stat.shape[1]), 0)
    squares = squares + jnp.sum(jnp.where(lane == row, stat, 0.0), axis=1, keepdims=True)
    inverse = lax.rsqrt(squares * (1.0 / width) + EPSILON)
    query = rotated(jnp.concatenate(total, axis=1) * inverse, cos_ref[...], sin_ref[...])
    out_ref[...] = (query * HEAD_DIM ** (-0.5)).astype(jnp.bfloat16)
    scale_ref[...] = jnp.broadcast_to(inverse, scale_ref.shape)


def news_kernel(
    place_ref,
    query_ref,
    scale_ref,
    cos_ref,
    sin_ref,
    fresh_ref,
    recv_ref,
    part_ref,
    stat_ref,
    out_ref,
    wide,
):
    half, columns = query_ref.shape
    share = fresh_ref.shape[0]
    line = place_ref[0] // 2
    here = pl.ds(pl.multiple_of(line * share, share), share)
    wide[...] = query_ref[...].astype(jnp.float32)
    fresh = (fresh_ref[...] + recv_ref[...].astype(jnp.float32)) * scale_ref[here, 0:1]
    key = rotated(fresh[:, :columns], cos_ref[here, :], sin_ref[here, :])
    product = wide[here, :] * key.astype(jnp.bfloat16).astype(jnp.float32)
    lane_head = lax.broadcasted_iota(jnp.int32, product.shape, 1) // HEAD_DIM
    lane = lax.broadcasted_iota(jnp.int32, (share, LANES), 1)
    first = (place_ref[0] % 2) * half + line * share
    owner = lax.broadcasted_iota(jnp.int32, (share, LANES), 0) + first
    stat = jnp.where(lane == 6 * HEADS, owner.astype(jnp.float32), 0.0)
    for h in range(HEADS):
        score = jnp.sum(jnp.where(lane_head == h, product, 0.0), axis=1, keepdims=True)
        for j, term in enumerate(split3(score)):
            stat = jnp.where(lane == j * HEADS + h, term, stat)
        stat = jnp.where(lane == 3 * HEADS + h, 1.0, stat)
    part = part_ref[...]
    part = jnp.concatenate([fresh[:, columns:], part[share:]], axis=0)
    stat = jnp.concatenate([stat_ref[:share, :] + stat, stat_ref[share:, :]], axis=0)
    first = 0
    for value in (part[:ROWS], part[ROWS:], key, stat):
        value = jnp.concatenate(flat(value), axis=0).astype(jnp.bfloat16)
        out_ref[first : first + value.shape[0], :] = value
        first += value.shape[0]


def stage_kernel(part, cache_ref, near_ref, sems):
    copies = [
        pltpu.make_async_copy(
            cache_ref.at[pl.ds(first, GROUP), part], near_ref.at[pl.ds(first, GROUP)], sems.at[i]
        )
        for i, first in enumerate(range(0, cache_ref.shape[0], GROUP))
    ]
    for copy in copies:
        copy.start()
    for copy in copies:
        copy.wait()


def store(part, near_ref, updated_ref, token_ref, sems):
    copies = [
        pltpu.make_async_copy(
            near_ref.at[pl.ds(first, GROUP)], updated_ref.at[pl.ds(first, GROUP), part], sems.at[i]
        )
        for i, first in enumerate(range(0, near_ref.shape[0], GROUP))
    ]
    for copy in copies:
        copy.start()
    token_ref[...] = jnp.zeros_like(token_ref)
    for copy in copies:
        copy.wait()


def store_keys_kernel(after_ref, keys_ref, updated_ref, token_ref, sems):
    store(0, keys_ref, updated_ref, token_ref, sems)


def store_values_kernel(after_ref, values_ref, held_ref, updated_ref, token_ref, sems):
    store(1, values_ref, updated_ref, token_ref, sems)


def read_block(b, owner_ref, index_ref, length_ref, tokens):
    requests = length_ref.shape[0]
    owner = owner_ref[b]
    reach = length_ref[jnp.minimum(owner, requests - 1)] - index_ref[b] * tokens
    live = owner < requests
    old = jnp.where(live, jnp.clip(reach - 1, 0, tokens), 0)
    slot = jnp.where(live & (reach >= 1) & (reach <= tokens), reach - 1, -1)
    return owner, old, slot


def plan_kernel(
    tokens,
    place_ref,
    owner_ref,
    index_ref,
    length_ref,
    mine_ref,
    other_ref,
    seen_ref,
    name_ref,
):
    blocks = owner_ref.shape[0]
    half = mine_ref.shape[1]
    side = place_ref[0] % 2
    lane = lax.broadcasted_iota(jnp.int32, (HEADS, half), 1)
    picks = [], []
    for b in range(blocks):
        owner, old, _ = read_block(b, owner_ref, index_ref, length_ref, tokens)
        here = pl.ds(b * HEADS, HEADS)
        for pick, first in zip(picks, (side, 1 - side)):
            pick.append((lane == owner - first * half).astype(jnp.float32))
        seen_ref[here, :] = jnp.full((HEADS, LANES), old, jnp.int32)
        name_ref[here, :] = jnp.full((HEADS, LANES), owner, jnp.int32).astype(jnp.float32)
    mine_ref[...] = jnp.concatenate(picks[0], axis=0).astype(jnp.bfloat16)
    other_ref[...] = jnp.concatenate(picks[1], axis=0).astype(jnp.bfloat16)


def attend_kernel(
    mine_ref,
    other_ref,
    pick_mine_ref,
    pick_other_ref,
    seen_ref,
    name_ref,
    keys_ref,
    values_ref,
    after_ref,
    part_ref,
    stat_ref,
):
    blocks, tokens, columns = keys_ref.shape
    steps = blocks // GROUP

    def iota(shape, dim):
        return lax.broadcasted_iota(jnp.int32, shape, dim)

    rows = blocks * HEADS
    size = GROUP * HEADS
    width = GROUP * tokens
    own = jnp.dot(pick_mine_ref[...], mine_ref[...], preferred_element_type=jnp.float32)
    own = own + jnp.dot(pick_other_ref[...], other_ref[...], preferred_element_type=jnp.float32)
    head_mask = iota((rows, columns), 1) // HEAD_DIM == iota((rows, columns), 0) % HEADS
    queries = jnp.where(head_mask, own, 0.0).astype(jnp.bfloat16)
    scores = []
    for step in range(steps):
        keys = keys_ref[step * GROUP : (step + 1) * GROUP].reshape(width, columns)
        scores.append(
            lax.dot_general(
                queries[step * size : (step + 1) * size],
                keys,
                (((1,), (1,)), ((), ())),
                preferred_element_type=jnp.float32,
            )
        )
    scores = jnp.concatenate(scores, axis=0)
    column = iota((rows, width), 1)
    same = column // tokens == iota((rows, width), 0) // HEADS % GROUP
    place = jnp.where(same, column % tokens, tokens)
    visible = place < jnp.concatenate([seen_ref[...]] * (width // LANES), axis=1)
    masked = jnp.where(visible, scores, NEG_FLOOR)
    top = jnp.max(masked, axis=1, keepdims=True)
    weights = jnp.where(visible, jnp.exp(masked - top), 0.0).astype(jnp.bfloat16)
    mass = jnp.sum(weights.astype(jnp.float32), axis=1, keepdims=True)
    parts = []
    for step in range(steps):
        values = values_ref[step * GROUP : (step + 1) * GROUP].reshape(width, columns)
        parts.append(
            jnp.dot(
                weights[step * size : (step + 1) * size],
                values,
                preferred_element_type=jnp.float32,
            )
        )
    part = jnp.concatenate(parts, axis=0) * jnp.where(mass > 0.0, 1.0 / mass, 0.0)
    part = jnp.where(head_mask, part, 0.0).astype(jnp.bfloat16)
    fresh = part_ref.shape[0] - blocks
    lane = iota((rows, LANES), 1)
    head = iota((rows, LANES), 0) % HEADS
    spot = iota((rows, LANES), 0) // HEADS + fresh
    lane = lane - spot // ROWS * (LANES // 2)
    stat = jnp.where((lane == 6 * HEADS) & (head == 0), name_ref[...], 0.0)
    for j, term in enumerate(split3(top) + split3(mass)):
        stat = jnp.where(lane == head + j * HEADS, term, stat)
    spot = iota((2 * ROWS, rows), 1) // HEADS + fresh
    fold = (spot == iota((2 * ROWS, rows), 0)).astype(jnp.float32).astype(jnp.bfloat16)
    part_ref[...] = jnp.dot(fold, part, preferred_element_type=jnp.float32)
    spot = iota((ROWS, rows), 1) // HEADS + fresh
    fold = (spot % ROWS == iota((ROWS, rows), 0)).astype(jnp.float32).astype(jnp.bfloat16)
    stat_ref[...] = jnp.dot(fold, stat.astype(jnp.bfloat16), preferred_element_type=jnp.float32)


def slots(tokens, owner_ref, index_ref, length_ref):
    found = []
    for b in range(owner_ref.shape[0]):
        owner, _, slot = read_block(b, owner_ref, index_ref, length_ref, tokens)
        first = pl.multiple_of(jnp.maximum(slot, 0) // ROWS * ROWS, ROWS)
        found.append((b, owner, slot, first))
    return found


def each(found, do):
    for spot in found:
        pl.when(spot[2] >= 0)(functools.partial(do, *spot))


def fetch_kernel(owner_ref, index_ref, length_ref, after_ref, cache_ref, near_ref, sems):
    found = slots(cache_ref.shape[2], owner_ref, index_ref, length_ref)

    def fetch(b, owner, slot, first):
        return pltpu.make_async_copy(
            cache_ref.at[b, :, pl.ds(first, ROWS), :], near_ref.at[b], sems.at[b]
        )

    each(found, lambda *at: fetch(*at).start())
    each(found, lambda *at: fetch(*at).wait())


def join_kernel(after_ref, *refs):
    out_ref = refs[-1]
    rows = refs[0].shape[0]
    for i, ref in enumerate(refs[:-1]):
        out_ref[i * rows : (i + 1) * rows, :] = ref[...]


def line_order(lines):
    return [0, *range(lines - 1, 0, -1)]


def line_groups(lines):
    return [[0, 1], *([i] for i in range(2, lines))]


def pieces_of(column, crossed):
    rows = column[0].shape[0]
    order = line_order(len(column))
    pieces = [None] * (2 * len(column))
    for ref, group in zip(crossed, line_groups(len(column))):
        for k, i in enumerate(group):
            pieces[2 * order[i]] = column[i]
            pieces[2 * order[i] + 1] = ref.at[k * rows : (k + 1) * rows]
    return pieces


def patch_kernel(count, place_ref, owner_ref, index_ref, length_ref, after_ref, *rest):
    lines = count // 2
    pieces = pieces_of(rest[:lines], rest[lines : lines + len(line_groups(lines))])
    near_ref, held_ref, updated_ref, fresh, patch, stores = rest[lines + len(line_groups(lines)) :]
    _, _, tokens, columns = updated_ref.shape
    requests = length_ref.shape[0]
    share = fresh.shape[1] // 2
    half = requests // 2

    def store(b, owner, slot, first):
        return pltpu.make_async_copy(
            patch.at[b], updated_ref.at[b, :, pl.ds(first, ROWS), :], stores.at[b]
        )

    for m in range(count):
        for c in range(columns // LANES):
            here = slice(c * LANES, (c + 1) * LANES)
            keys = 2 * columns // LANES * ROWS + c * share
            fresh[m, :share, here] = pieces[m][c * ROWS : c * ROWS + share, :].astype(jnp.float32)
            fresh[m, share:, here] = pieces[m][keys : keys + share, :].astype(jnp.float32)
    row = lax.broadcasted_iota(jnp.int32, (ROWS, columns), 0)

    def change(b, owner, slot, first):
        request = jnp.minimum(owner, requests - 1)
        device = request % half // share * 2 + request // half
        piece = place_ref[0] ^ device
        line = request % share
        for c in range(2):
            new = fresh[piece, pl.ds(line + (1 - c) * share, 1), :]
            old = near_ref[b, c].astype(jnp.float32)
            patch[b, c] = jnp.where(row == slot - first, new, old).astype(jnp.bfloat16)
        store(b, owner, slot, first).start()

    found = slots(tokens, owner_ref, index_ref, length_ref)
    each(found, change)
    each(found, lambda *at: store(*at).wait())


def output_kernel(count, place_ref, *rest):
    lines = count // 2
    pieces = pieces_of(rest[:lines], rest[lines : lines + len(line_groups(lines))])
    w_ref, states_ref, after_ref, own_ref, *sends, product = rest[lines + len(line_groups(lines)) :]
    heads = HEADS
    columns = w_ref.shape[0]
    chunks = columns // LANES
    requests = states_ref.shape[0]
    total_blocks = count * 2 * ROWS

    def rows_of(first):
        rows = [
            jnp.concatenate(
                [piece[first + c * ROWS : first + (c + 1) * ROWS, :] for c in range(chunks)], axis=1
            )
            for piece in pieces
        ]
        return jnp.concatenate(rows, axis=0)

    parts = jnp.concatenate([rows_of(0), rows_of(chunks * ROWS)], axis=0)
    stat = jnp.concatenate([piece[-ROWS:, :] for piece in pieces], axis=0)
    row = lax.broadcasted_iota(jnp.int32, (3 * heads, LANES), 0)
    lane = lax.broadcasted_iota(jnp.int32, (3 * heads, LANES), 1)

    def terms(first):
        at = lane - first
        wanted = (row // heads == at // (3 * heads)) & (row % heads == at % heads) & (at >= 0)
        wanted = (wanted & (row < 2 * heads)) | ((row >= 2 * heads) & (at == 6 * heads))
        return lax.dot_general(
            wanted.astype(jnp.float32).astype(jnp.bfloat16),
            stat,
            (((1,), (1,)), ((), ())),
            preferred_element_type=jnp.float32,
        )

    stat = jnp.concatenate([terms(0), terms(LANES // 2)], axis=1)
    owner = stat[2 * heads : 2 * heads + 1]
    request = lax.broadcasted_iota(jnp.int32, (requests, total_blocks), 0).astype(jnp.float32)
    member = owner == request
    lane_head = lax.broadcasted_iota(jnp.int32, (requests, columns), 1) // HEAD_DIM
    factors = []
    for h in range(heads):
        top = jnp.where(member, stat[h : h + 1], NEG_FLOOR)
        highest = jnp.max(top, axis=1, keepdims=True)
        factor = jnp.where(member, jnp.exp(top - highest) * stat[heads + h : heads + h + 1], 0.0)
        factors.append(factor / jnp.sum(factor, axis=1, keepdims=True))
    factors = jnp.concatenate(factors, axis=0).astype(jnp.bfloat16)
    joined = jnp.dot(factors, parts, preferred_element_type=jnp.float32)
    attended = joined[:requests]
    for h in range(1, heads):
        attended = jnp.where(lane_head == h, joined[h * requests : (h + 1) * requests], attended)
    product[...] = jnp.dot(
        attended.astype(jnp.bfloat16), w_ref[...], preferred_element_type=jnp.float32
    )
    place = place_ref[0]
    share = own_ref.shape[0]
    mine = pl.ds(pl.multiple_of(place * share, share), share)
    own_ref[...] = product[mine, :] + states_ref[mine, :].astype(jnp.float32)
    for m, send in enumerate(sends, 1):
        theirs = pl.ds(pl.multiple_of((place ^ m) * share, share), share)
        send[...] = product[theirs, :].astype(send.dtype)


def shards(states, norm_gain, w_qkv, w_out, cache, context_len, block_owner, block_index):
    requests, depth = states.shape
    peers = lax.axis_size("seq")
    ranks = lax.axis_size("tp")
    parts, _, columns = w_qkv.shape
    blocks, _, tokens, _ = cache.shape
    half = requests // 2
    share = requests // peers
    lines = peers // 2
    out_columns = w_out.shape[1]
    rows = blocks * HEADS
    steps = blocks // GROUP
    limit = pltpu.CompilerParams(vmem_limit_bytes=24 * 1024 * 1024)
    most_room = pltpu.CompilerParams(vmem_limit_bytes=50 * 1024 * 1024)
    all_room = pltpu.CompilerParams(vmem_limit_bytes=60 * 1024 * 1024)
    in_vmem = pl.BlockSpec(memory_space=VMEM)
    in_hbm = pl.BlockSpec(memory_space=HBM)
    in_smem = pl.BlockSpec(memory_space=SMEM)
    anywhere = pl.BlockSpec(memory_space=pl.ANY)
    place = lax.axis_index("seq")
    at = place.reshape(1).astype(jnp.int32)

    def array(*shape, dtype=jnp.bfloat16):
        return jax.ShapeDtypeStruct(shape, dtype)

    def to_peer(value, m):
        return lax.ppermute(value, "seq", [(i, i ^ m) for i in range(peers)])

    def moves(size):
        return pl.CostEstimate(flops=0, bytes_accessed=size, transcendentals=0)

    sent, kept, sent_fresh, kept_fresh = pl.pallas_call(
        project_kernel,
        out_shape=(
            array(half, columns + LANES),
            array(half, columns + LANES, dtype=jnp.float32),
            array(half, 2 * columns),
            array(half, 2 * columns, dtype=jnp.float32),
        ),
        in_specs=[in_smem] + [in_hbm] * 3,
        out_specs=(in_vmem,) * 4,
        scratch_shapes=[
            pltpu.VMEM(states.shape, jnp.bfloat16),
            pltpu.VMEM(norm_gain.shape, jnp.bfloat16),
            pltpu.VMEM((parts, depth, columns), jnp.bfloat16),
            pltpu.SemaphoreType.DMA((parts + 2,)),
        ],
        compiler_params=all_room,
        name="project",
    )(at, states, norm_gain, w_qkv)
    received = to_peer(sent, 1)
    fresh_received = to_peer(sent_fresh, 1)

    positions = lax.dynamic_slice_in_dim(context_len, place % 2 * half, half) - 1
    pair = (jnp.arange(columns, dtype=jnp.int32) % (HEAD_DIM // 2)).astype(jnp.float32)
    frequency = 10000.0 ** (-pair * 2.0 / HEAD_DIM)
    angles = positions.astype(jnp.float32)[:, None] * frequency[None, :]

    table = (block_owner, block_index, context_len)
    plan = pl.pallas_call(
        functools.partial(plan_kernel, tokens),
        out_shape=(
            array(rows, half),
            array(rows, half),
            array(rows, LANES, dtype=jnp.int32),
            array(rows, LANES, dtype=jnp.float32),
        ),
        in_specs=[in_smem] * 4,
        compiler_params=limit,
        name="plan",
    )(at, *table)
    def stage(part, name):
        return pl.pallas_call(
            functools.partial(stage_kernel, part),
            out_shape=array(blocks, tokens, columns),
            in_specs=[in_hbm],
            out_specs=in_vmem,
            scratch_shapes=[pltpu.SemaphoreType.DMA((steps,))],
            compiler_params=most_room,
            cost_estimate=moves(cache.size),
            name=name,
        )(cache)

    keys, values = stage(0, "stage_keys"), stage(1, "stage_values")
    message = columns // LANES * half + ROWS * pl.cdiv(half, LANES)
    send, query = pl.pallas_call(
        halve_query_kernel,
        out_shape=(array(message, LANES), array(half, columns + LANES, dtype=jnp.float32)),
        in_specs=[in_vmem, in_vmem, anywhere, anywhere],
        compiler_params=pltpu.CompilerParams(vmem_limit_bytes=47 * 1024 * 1024),
        name="halve_query",
    )(kept, received, values, plan[0])
    received = [to_peer(send, 2 * m) for m in (1, *range(lines - 1, 1, -1))]
    (mask, sent_to, held), *later = sum_plan(lines)
    fresh_send, fresh = pl.pallas_call(
        functools.partial(halve_fresh_kernel, sent_to, held),
        out_shape=(
            array(share * len(sent_to), 2 * columns),
            array(share * len(held), 2 * columns, dtype=jnp.float32),
        ),
        in_specs=[in_smem, in_vmem, in_vmem],
        scratch_shapes=[pltpu.VMEM((half, 2 * columns), jnp.float32)],
        compiler_params=limit,
        name="halve_fresh",
    )(at, kept_fresh, fresh_received)
    fresh_received = to_peer(fresh_send, 2 * mask)
    for mask, sent_to, still in later:
        fresh_send, fresh = pl.pallas_call(
            functools.partial(fold_kernel, held, sent_to, still),
            out_shape=(
                array(share * len(sent_to), 2 * columns),
                array(share * len(still), 2 * columns, dtype=jnp.float32),
            ),
            compiler_params=limit,
            name="fold",
        )(fresh, fresh_received)
        held = still
        fresh_received = to_peer(fresh_send, 2 * mask)
    cosine, sine = jnp.cos(angles), jnp.sin(angles)
    mine, scale = pl.pallas_call(
        functools.partial(query_kernel, depth * peers),
        out_shape=(array(half, columns), array(half, LANES, dtype=jnp.float32)),
        in_specs=[anywhere] + [in_vmem] * (3 + len(received)),
        compiler_params=pltpu.CompilerParams(vmem_limit_bytes=47 * 1024 * 1024),
        name="query",
    )(keys, query, cosine, sine, *received)
    other = to_peer(mine, 1)
    updated, token = pl.pallas_call(
        store_keys_kernel,
        out_shape=(array(*cache.shape), array(8, LANES, dtype=jnp.float32)),
        in_specs=[anywhere, in_vmem],
        out_specs=(in_hbm, in_vmem),
        scratch_shapes=[pltpu.SemaphoreType.DMA((steps,))],
        compiler_params=most_room,
        cost_estimate=moves(cache.size),
        name="store_keys",
    )(mine, keys)

    part, stat = pl.pallas_call(
        attend_kernel,
        out_shape=(
            array(2 * ROWS, columns, dtype=jnp.float32),
            array(ROWS, LANES, dtype=jnp.float32),
        ),
        in_specs=[in_vmem] * 8 + [anywhere],
        compiler_params=pltpu.CompilerParams(vmem_limit_bytes=47 * 1024 * 1024),
        name="attend",
    )(mine, other, *plan, keys, values, token)
    piece = pl.pallas_call(
        news_kernel,
        out_shape=array(columns // LANES * (2 * ROWS + share) + ROWS, LANES),
        in_specs=[in_smem] + [in_vmem] * 8,
        scratch_shapes=[pltpu.VMEM((half, columns), jnp.float32)],
        compiler_params=limit,
        name="news",
    )(at, mine, scale, cosine, sine, fresh, fresh_received, part, stat)
    updated, token = pl.pallas_call(
        store_values_kernel,
        out_shape=(array(*cache.shape), array(8, LANES, dtype=jnp.float32)),
        in_specs=[anywhere, in_vmem, in_hbm],
        out_specs=(in_hbm, in_vmem),
        scratch_shapes=[pltpu.SemaphoreType.DMA((steps,))],
        input_output_aliases={2: 0},
        compiler_params=most_room,
        cost_estimate=moves(cache.size),
        name="store_values",
    )(piece, values, updated)
    column = [to_peer(piece, 2 * m) if m else piece for m in line_order(lines)]
    pieces = list(column)
    for group in line_groups(lines):
        joined = column[group[0]]
        if len(group) > 1:
            joined = pl.pallas_call(
                join_kernel,
                out_shape=array(len(group) * piece.shape[0], LANES),
                in_specs=[anywhere] + [in_vmem] * len(group),
                compiler_params=limit,
                name="join",
            )(token, *[column[i] for i in group])
        pieces.append(to_peer(joined, 1))
    near = pl.pallas_call(
        fetch_kernel,
        out_shape=array(blocks, 2, ROWS, columns),
        in_specs=[in_smem] * 3 + [anywhere, in_hbm],
        out_specs=in_vmem,
        scratch_shapes=[pltpu.SemaphoreType.DMA((blocks,))],
        compiler_params=most_room,
        cost_estimate=moves(blocks * ROWS * columns * 8),
        name="fetch",
    )(*table, piece, cache)
    rank = lax.axis_index("tp")
    kept_rows = requests // ranks
    own, *sends = pl.pallas_call(
        functools.partial(output_kernel, peers),
        out_shape=(
            array(kept_rows, out_columns, dtype=jnp.float32),
            *(array(kept_rows, out_columns, dtype=jnp.bfloat16) for _ in range(1, ranks)),
        ),
        in_specs=[in_smem] + [in_vmem] * (len(pieces) + 2) + [anywhere],
        out_specs=(in_vmem,) * ranks,
        scratch_shapes=[pltpu.VMEM((requests, out_columns), jnp.float32)],
        compiler_params=limit,
        name="output",
    )(rank.reshape(1).astype(jnp.int32), *pieces, w_out, states, near)
    total = own
    for m in range(ranks - 1, 0, -1):
        moved = lax.ppermute(sends[m - 1], "tp", [(i, i ^ m) for i in range(ranks)])
        total = total + moved.astype(jnp.float32)
    updated = pl.pallas_call(
        functools.partial(patch_kernel, peers),
        out_shape=array(*cache.shape),
        in_specs=[in_smem] * 4 + [anywhere] + [in_vmem] * (len(pieces) + 1) + [in_hbm],
        out_specs=in_hbm,
        scratch_shapes=[
            pltpu.VMEM((peers, 2 * share, columns), jnp.float32),
            pltpu.VMEM((blocks, 2, ROWS, columns), jnp.bfloat16),
            pltpu.SemaphoreType.DMA((blocks,)),
        ],
        input_output_aliases={6 + len(pieces): 0},
        compiler_params=most_room,
        cost_estimate=moves(blocks * ROWS * columns * 8),
        name="patch",
    )(at, *table, sends[0], *pieces, near, updated)
    return (total.astype(jnp.bfloat16), updated)


def solution(mesh):
    return jax.shard_map(
        shards,
        mesh=mesh,
        in_specs=(
            P(None, "seq"),
            P("seq"),
            P(None, "seq", "tp"),
            P("tp", "seq"),
            P("seq", None, None, "tp"),
            P(),
            P("seq"),
            P("seq"),
        ),
        out_specs=(P("tp", "seq"), P("seq", None, None, "tp")),
        check_vma=False,
    )
```

```python
import functools

import jax
import jax.numpy as jnp
from jax import lax
from jax.experimental import pallas as pl
from jax.experimental.pallas import tpu as pltpu
from jax.sharding import PartitionSpec as P

HEAD_DIM = 96
EPSILON = 1e-05
NEG_FLOOR = -1e30
LANES = 128
GROUP = 4

VMEM = pltpu.MemorySpace.VMEM
HBM = pltpu.MemorySpace.HBM
SMEM = pltpu.MemorySpace.SMEM
HEADS = 8
ROWS = 16


def split3(value):
    high = value.astype(jnp.bfloat16).astype(jnp.float32)
    rest = value - high
    mid = rest.astype(jnp.bfloat16).astype(jnp.float32)
    low = (rest - mid).astype(jnp.bfloat16).astype(jnp.float32)
    return high, mid, low


def lanes_of(terms):
    lane = lax.broadcasted_iota(jnp.int32, (terms[0].shape[0], LANES), 1)
    out = jnp.zeros(lane.shape, jnp.float32)
    for j, term in enumerate(terms):
        out = jnp.where(lane == j, term, out)
    return out


def project_kernel(
    place_ref,
    states_ref,
    gain_ref,
    w_ref,
    sent_ref,
    kept_ref,
    sent_fresh_ref,
    kept_fresh_ref,
    states_buf,
    gain_buf,
    w_buf,
    sems,
):
    parts, _, columns = w_ref.shape
    half = sent_ref.shape[0]
    small = [
        pltpu.make_async_copy(states_ref, states_buf, sems.at[parts]),
        pltpu.make_async_copy(gain_ref, gain_buf, sems.at[parts + 1]),
    ]
    copies = [pltpu.make_async_copy(w_ref.at[c], w_buf.at[c], sems.at[c]) for c in range(parts)]
    for copy in small + copies:
        copy.start()
    for copy in small:
        copy.wait()
    side = place_ref[0] % 2
    rows = [
        states_buf[pl.ds(pl.multiple_of(first * half, half), half), :].astype(jnp.float32)
        for first in (1 - side, side)
    ]
    wide = jnp.concatenate(rows, axis=0)
    gain = gain_buf[...].astype(jnp.float32)
    scaled = (wide * gain.reshape(1, wide.shape[1])).astype(jnp.bfloat16)
    stat = lanes_of(split3(jnp.sum(wide * wide, axis=1, keepdims=True)))
    sent_ref[:, columns:] = stat[:half].astype(jnp.bfloat16)
    kept_ref[:, columns:] = stat[half:]
    places = [(sent_ref, kept_ref, 0), (sent_fresh_ref, kept_fresh_ref, 0)]
    places.append((sent_fresh_ref, kept_fresh_ref, columns))
    for c, (sent, kept, first) in enumerate(places):
        copies[c].wait()
        term = jnp.dot(scaled, w_buf[c], preferred_element_type=jnp.float32)
        here = slice(first, first + columns)
        sent[:, here] = term[:half].astype(jnp.bfloat16)
        kept[:, here] = term[half:]


def flat(value):
    chunks = value.shape[1] // LANES
    return [value[:, c * LANES : (c + 1) * LANES] for c in range(chunks)]


def sum_plan(lines):
    masks = [1 << k for k in range(lines.bit_length() - 1)]
    steps = []
    for k, mask in enumerate(masks):
        kept = [0]
        for later in masks[k + 1 :]:
            kept = kept + [offset ^ later for offset in kept]
        steps.append((mask, [mask ^ offset for offset in kept], kept))
    return steps


def halve_query_kernel(kept_ref, recv_ref, after_ref, planned_ref, send, query_ref):
    columns = query_ref.shape[1] - LANES
    half = kept_ref.shape[0]
    total = kept_ref[...] + recv_ref[...].astype(jnp.float32)
    squares = jnp.sum(total[:, columns:], axis=1, keepdims=True)
    query_ref[:, :columns] = total[:, :columns]
    query_ref[:, columns:] = lanes_of([squares])
    pads = -half % LANES
    stat = [jnp.pad(term, ((0, pads), (0, 0))) for term in split3(squares)]
    lane = lax.broadcasted_iota(jnp.int32, (half + pads, half + pads), 1)
    row = lax.broadcasted_iota(jnp.int32, (half + pads, half + pads), 0)
    stat = [jnp.sum(jnp.where(lane == row, t, 0.0), axis=0, keepdims=True) for t in stat]
    stat = jnp.concatenate(stat + [jnp.zeros((ROWS - 3, half + pads), jnp.float32)], axis=0)
    chunks = columns // LANES
    send[: chunks * half, :] = jnp.concatenate(flat(total[:, :columns]), axis=0).astype(jnp.bfloat16)
    send[chunks * half :, :] = jnp.concatenate(flat(stat), axis=0).astype(jnp.bfloat16)


def halve_fresh_kernel(sent, held, place_ref, kept_ref, recv_ref, send_ref, fresh_ref, total):
    share = fresh_ref.shape[0] // len(held)
    total[...] = kept_ref[...] + recv_ref[...].astype(jnp.float32)
    line = place_ref[0] // 2

    def rows_of(offsets):
        rows = [
            total[pl.ds(pl.multiple_of((line ^ offset) * share, share), share), :]
            for offset in offsets
        ]
        return jnp.concatenate(rows, axis=0)

    fresh_ref[...] = rows_of(held)
    send_ref[...] = rows_of(sent).astype(jnp.bfloat16)


def fold_kernel(offsets, sent, held, fresh_in, recv_ref, send_ref, fresh_ref):
    share = fresh_ref.shape[0] // len(held)
    fresh = fresh_in[...] + recv_ref[...].astype(jnp.float32)

    def rows_of(wanted):
        at = [offsets.index(offset) * share for offset in wanted]
        return jnp.concatenate([fresh[first : first + share] for first in at], axis=0)

    fresh_ref[...] = rows_of(held)
    send_ref[...] = rows_of(sent).astype(jnp.bfloat16)


def rotated(x, cosine, sine):
    columns = x.shape[1]
    span = HEAD_DIM // 2
    front = lax.broadcasted_iota(jnp.int32, x.shape, 1) % HEAD_DIM < span
    other = jnp.where(front, -pltpu.roll(x, columns - span, 1), pltpu.roll(x, span, 1))
    return x * cosine + other * sine


def query_kernel(width, after_ref, query_ref, cos_ref, sin_ref, *rest):
    received, out_ref, scale_ref = rest[:-2], rest[-2], rest[-1]
    half, columns = out_ref.shape
    chunks = columns // LANES
    total = flat(query_ref[:, :columns])
    squares = query_ref[:, columns : columns + 1]
    stat = jnp.zeros((received[0].shape[0] - chunks * half, LANES), jnp.float32)
    for piece in received:
        for c in range(chunks):
            total[c] = total[c] + piece[c * half : (c + 1) * half, :].astype(jnp.float32)
        stat = stat + piece[chunks * half :, :].astype(jnp.float32)
    stat = [jnp.sum(stat[r : r + ROWS], axis=0, keepdims=True) for r in range(0, stat.shape[0], ROWS)]
    stat = jnp.concatenate(stat, axis=1)
    lane = lax.broadcasted_iota(jnp.int32, (half, stat.shape[1]), 1)
    row = lax.broadcasted_iota(jnp.int32, (half, stat.shape[1]), 0)
    squares = squares + jnp.sum(jnp.where(lane == row, stat, 0.0), axis=1, keepdims=True)
    inverse = lax.rsqrt(squares * (1.0 / width) + EPSILON)
    query = rotated(jnp.concatenate(total, axis=1) * inverse, cos_ref[...], sin_ref[...])
    out_ref[...] = (query * HEAD_DIM ** (-0.5)).astype(jnp.bfloat16)
    scale_ref[...] = jnp.broadcast_to(inverse, scale_ref.shape)


def news_kernel(
    place_ref,
    query_ref,
    scale_ref,
    cos_ref,
    sin_ref,
    fresh_ref,
    recv_ref,
    part_ref,
    stat_ref,
    out_ref,
    wide,
):
    half, columns = query_ref.shape
    share = fresh_ref.shape[0]
    line = place_ref[0] // 2
    here = pl.ds(pl.multiple_of(line * share, share), share)
    wide[...] = query_ref[...].astype(jnp.float32)
    fresh = (fresh_ref[...] + recv_ref[...].astype(jnp.float32)) * scale_ref[here, 0:1]
    key = rotated(fresh[:, :columns], cos_ref[here, :], sin_ref[here, :])
    product = wide[here, :] * key.astype(jnp.bfloat16).astype(jnp.float32)
    lane_head = lax.broadcasted_iota(jnp.int32, product.shape, 1) // HEAD_DIM
    lane = lax.broadcasted_iota(jnp.int32, (share, LANES), 1)
    first = (place_ref[0] % 2) * half + line * share
    owner = lax.broadcasted_iota(jnp.int32, (share, LANES), 0) + first
    stat = jnp.where(lane == 6 * HEADS, owner.astype(jnp.float32), 0.0)
    for h in range(HEADS):
        score = jnp.sum(jnp.where(lane_head == h, product, 0.0), axis=1, keepdims=True)
        for j, term in enumerate(split3(score)):
            stat = jnp.where(lane == j * HEADS + h, term, stat)
        stat = jnp.where(lane == 3 * HEADS + h, 1.0, stat)
    part = part_ref[...]
    part = jnp.concatenate([fresh[:, columns:], part[share:]], axis=0)
    stat = jnp.concatenate([stat_ref[:share, :] + stat, stat_ref[share:, :]], axis=0)
    first = 0
    for value in (part[:ROWS], part[ROWS:], key, stat):
        value = jnp.concatenate(flat(value), axis=0).astype(jnp.bfloat16)
        out_ref[first : first + value.shape[0], :] = value
        first += value.shape[0]


def stage_kernel(part, cache_ref, near_ref, sems):
    copies = [
        pltpu.make_async_copy(
            cache_ref.at[pl.ds(first, GROUP), part], near_ref.at[pl.ds(first, GROUP)], sems.at[i]
        )
        for i, first in enumerate(range(0, cache_ref.shape[0], GROUP))
    ]
    for copy in copies:
        copy.start()
    for copy in copies:
        copy.wait()


def store(part, near_ref, updated_ref, token_ref, sems):
    copies = [
        pltpu.make_async_copy(
            near_ref.at[pl.ds(first, GROUP)], updated_ref.at[pl.ds(first, GROUP), part], sems.at[i]
        )
        for i, first in enumerate(range(0, near_ref.shape[0], GROUP))
    ]
    for copy in copies:
        copy.start()
    token_ref[...] = jnp.zeros_like(token_ref)
    for copy in copies:
        copy.wait()


def store_keys_kernel(after_ref, keys_ref, updated_ref, token_ref, sems):
    store(0, keys_ref, updated_ref, token_ref, sems)


def store_values_kernel(after_ref, values_ref, held_ref, updated_ref, token_ref, sems):
    store(1, values_ref, updated_ref, token_ref, sems)


def read_block(b, owner_ref, index_ref, length_ref, tokens):
    requests = length_ref.shape[0]
    owner = owner_ref[b]
    reach = length_ref[jnp.minimum(owner, requests - 1)] - index_ref[b] * tokens
    live = owner < requests
    old = jnp.where(live, jnp.clip(reach - 1, 0, tokens), 0)
    slot = jnp.where(live & (reach >= 1) & (reach <= tokens), reach - 1, -1)
    return owner, old, slot


def plan_kernel(
    tokens,
    place_ref,
    owner_ref,
    index_ref,
    length_ref,
    mine_ref,
    other_ref,
    seen_ref,
    name_ref,
):
    blocks = owner_ref.shape[0]
    half = mine_ref.shape[1]
    side = place_ref[0] % 2
    lane = lax.broadcasted_iota(jnp.int32, (HEADS, half), 1)
    picks = [], []
    for b in range(blocks):
        owner, old, _ = read_block(b, owner_ref, index_ref, length_ref, tokens)
        here = pl.ds(b * HEADS, HEADS)
        for pick, first in zip(picks, (side, 1 - side)):
            pick.append((lane == owner - first * half).astype(jnp.float32))
        seen_ref[here, :] = jnp.full((HEADS, LANES), old, jnp.int32)
        name_ref[here, :] = jnp.full((HEADS, LANES), owner, jnp.int32).astype(jnp.float32)
    mine_ref[...] = jnp.concatenate(picks[0], axis=0).astype(jnp.bfloat16)
    other_ref[...] = jnp.concatenate(picks[1], axis=0).astype(jnp.bfloat16)


def attend_kernel(
    mine_ref,
    other_ref,
    pick_mine_ref,
    pick_other_ref,
    seen_ref,
    name_ref,
    keys_ref,
    values_ref,
    after_ref,
    part_ref,
    stat_ref,
):
    blocks, tokens, columns = keys_ref.shape
    steps = blocks // GROUP

    def iota(shape, dim):
        return lax.broadcasted_iota(jnp.int32, shape, dim)

    rows = blocks * HEADS
    size = GROUP * HEADS
    width = GROUP * tokens
    own = jnp.dot(pick_mine_ref[...], mine_ref[...], preferred_element_type=jnp.float32)
    own = own + jnp.dot(pick_other_ref[...], other_ref[...], preferred_element_type=jnp.float32)
    head_mask = iota((rows, columns), 1) // HEAD_DIM == iota((rows, columns), 0) % HEADS
    queries = jnp.where(head_mask, own, 0.0).astype(jnp.bfloat16)
    scores = []
    for step in range(steps):
        keys = keys_ref[step * GROUP : (step + 1) * GROUP].reshape(width, columns)
        scores.append(
            lax.dot_general(
                queries[step * size : (step + 1) * size],
                keys,
                (((1,), (1,)), ((), ())),
                preferred_element_type=jnp.float32,
            )
        )
    scores = jnp.concatenate(scores, axis=0)
    column = iota((rows, width), 1)
    same = column // tokens == iota((rows, width), 0) // HEADS % GROUP
    place = jnp.where(same, column % tokens, tokens)
    visible = place < jnp.concatenate([seen_ref[...]] * (width // LANES), axis=1)
    masked = jnp.where(visible, scores, NEG_FLOOR)
    top = jnp.max(masked, axis=1, keepdims=True)
    weights = jnp.where(visible, jnp.exp(masked - top), 0.0).astype(jnp.bfloat16)
    mass = jnp.sum(weights.astype(jnp.float32), axis=1, keepdims=True)
    parts = []
    for step in range(steps):
        values = values_ref[step * GROUP : (step + 1) * GROUP].reshape(width, columns)
        parts.append(
            jnp.dot(
                weights[step * size : (step + 1) * size],
                values,
                preferred_element_type=jnp.float32,
            )
        )
    part = jnp.concatenate(parts, axis=0) * jnp.where(mass > 0.0, 1.0 / mass, 0.0)
    part = jnp.where(head_mask, part, 0.0).astype(jnp.bfloat16)
    fresh = part_ref.shape[0] - blocks
    lane = iota((rows, LANES), 1)
    head = iota((rows, LANES), 0) % HEADS
    spot = iota((rows, LANES), 0) // HEADS + fresh
    lane = lane - spot // ROWS * (LANES // 2)
    stat = jnp.where((lane == 6 * HEADS) & (head == 0), name_ref[...], 0.0)
    for j, term in enumerate(split3(top) + split3(mass)):
        stat = jnp.where(lane == head + j * HEADS, term, stat)
    spot = iota((2 * ROWS, rows), 1) // HEADS + fresh
    fold = (spot == iota((2 * ROWS, rows), 0)).astype(jnp.float32).astype(jnp.bfloat16)
    part_ref[...] = jnp.dot(fold, part, preferred_element_type=jnp.float32)
    spot = iota((ROWS, rows), 1) // HEADS + fresh
    fold = (spot % ROWS == iota((ROWS, rows), 0)).astype(jnp.float32).astype(jnp.bfloat16)
    stat_ref[...] = jnp.dot(fold, stat.astype(jnp.bfloat16), preferred_element_type=jnp.float32)


def slots(tokens, owner_ref, index_ref, length_ref):
    found = []
    for b in range(owner_ref.shape[0]):
        owner, _, slot = read_block(b, owner_ref, index_ref, length_ref, tokens)
        first = pl.multiple_of(jnp.maximum(slot, 0) // ROWS * ROWS, ROWS)
        found.append((b, owner, slot, first))
    return found


def each(found, do):
    for spot in found:
        pl.when(spot[2] >= 0)(functools.partial(do, *spot))


def fetch_kernel(owner_ref, index_ref, length_ref, after_ref, cache_ref, near_ref, sems):
    found = slots(cache_ref.shape[2], owner_ref, index_ref, length_ref)

    def fetch(b, owner, slot, first):
        return pltpu.make_async_copy(
            cache_ref.at[b, :, pl.ds(first, ROWS), :], near_ref.at[b], sems.at[b]
        )

    each(found, lambda *at: fetch(*at).start())
    each(found, lambda *at: fetch(*at).wait())


def join_kernel(after_ref, *refs):
    out_ref = refs[-1]
    rows = refs[0].shape[0]
    for i, ref in enumerate(refs[:-1]):
        out_ref[i * rows : (i + 1) * rows, :] = ref[...]


def line_order(lines):
    return [0, *range(lines - 1, 0, -1)]


def line_groups(lines):
    return [[0, 1], *([i] for i in range(2, lines))]


def pieces_of(column, crossed):
    rows = column[0].shape[0]
    order = line_order(len(column))
    pieces = [None] * (2 * len(column))
    for ref, group in zip(crossed, line_groups(len(column))):
        for k, i in enumerate(group):
            pieces[2 * order[i]] = column[i]
            pieces[2 * order[i] + 1] = ref.at[k * rows : (k + 1) * rows]
    return pieces


def patch_kernel(count, place_ref, owner_ref, index_ref, length_ref, after_ref, *rest):
    lines = count // 2
    pieces = pieces_of(rest[:lines], rest[lines : lines + len(line_groups(lines))])
    near_ref, held_ref, updated_ref, fresh, patch, stores = rest[lines + len(line_groups(lines)) :]
    _, _, tokens, columns = updated_ref.shape
    requests = length_ref.shape[0]
    share = fresh.shape[1] // 2
    half = requests // 2

    def store(b, owner, slot, first):
        return pltpu.make_async_copy(
            patch.at[b], updated_ref.at[b, :, pl.ds(first, ROWS), :], stores.at[b]
        )

    for m in range(count):
        for c in range(columns // LANES):
            here = slice(c * LANES, (c + 1) * LANES)
            keys = 2 * columns // LANES * ROWS + c * share
            fresh[m, :share, here] = pieces[m][c * ROWS : c * ROWS + share, :].astype(jnp.float32)
            fresh[m, share:, here] = pieces[m][keys : keys + share, :].astype(jnp.float32)
    row = lax.broadcasted_iota(jnp.int32, (ROWS, columns), 0)

    def change(b, owner, slot, first):
        request = jnp.minimum(owner, requests - 1)
        device = request % half // share * 2 + request // half
        piece = place_ref[0] ^ device
        line = request % share
        for c in range(2):
            new = fresh[piece, pl.ds(line + (1 - c) * share, 1), :]
            old = near_ref[b, c].astype(jnp.float32)
            patch[b, c] = jnp.where(row == slot - first, new, old).astype(jnp.bfloat16)
        store(b, owner, slot, first).start()

    found = slots(tokens, owner_ref, index_ref, length_ref)
    each(found, change)
    each(found, lambda *at: store(*at).wait())


def output_kernel(count, place_ref, *rest):
    lines = count // 2
    pieces = pieces_of(rest[:lines], rest[lines : lines + len(line_groups(lines))])
    w_ref, states_ref, after_ref, own_ref, *sends, product = rest[lines + len(line_groups(lines)) :]
    heads = HEADS
    columns = w_ref.shape[0]
    chunks = columns // LANES
    requests = states_ref.shape[0]
    total_blocks = count * 2 * ROWS

    def rows_of(first):
        rows = [
            jnp.concatenate(
                [piece[first + c * ROWS : first + (c + 1) * ROWS, :] for c in range(chunks)], axis=1
            )
            for piece in pieces
        ]
        return jnp.concatenate(rows, axis=0)

    parts = jnp.concatenate([rows_of(0), rows_of(chunks * ROWS)], axis=0)
    stat = jnp.concatenate([piece[-ROWS:, :] for piece in pieces], axis=0)
    row = lax.broadcasted_iota(jnp.int32, (3 * heads, LANES), 0)
    lane = lax.broadcasted_iota(jnp.int32, (3 * heads, LANES), 1)

    def terms(first):
        at = lane - first
        wanted = (row // heads == at // (3 * heads)) & (row % heads == at % heads) & (at >= 0)
        wanted = (wanted & (row < 2 * heads)) | ((row >= 2 * heads) & (at == 6 * heads))
        return lax.dot_general(
            wanted.astype(jnp.float32).astype(jnp.bfloat16),
            stat,
            (((1,), (1,)), ((), ())),
            preferred_element_type=jnp.float32,
        )

    stat = jnp.concatenate([terms(0), terms(LANES // 2)], axis=1)
    owner = stat[2 * heads : 2 * heads + 1]
    request = lax.broadcasted_iota(jnp.int32, (requests, total_blocks), 0).astype(jnp.float32)
    member = owner == request
    lane_head = lax.broadcasted_iota(jnp.int32, (requests, columns), 1) // HEAD_DIM
    factors = []
    for h in range(heads):
        top = jnp.where(member, stat[h : h + 1], NEG_FLOOR)
        highest = jnp.max(top, axis=1, keepdims=True)
        factor = jnp.where(member, jnp.exp(top - highest) * stat[heads + h : heads + h + 1], 0.0)
        factors.append(factor / jnp.sum(factor, axis=1, keepdims=True))
    factors = jnp.concatenate(factors, axis=0).astype(jnp.bfloat16)
    joined = jnp.dot(factors, parts, preferred_element_type=jnp.float32)
    attended = joined[:requests]
    for h in range(1, heads):
        attended = jnp.where(lane_head == h, joined[h * requests : (h + 1) * requests], attended)
    product[...] = jnp.dot(
        attended.astype(jnp.bfloat16), w_ref[...], preferred_element_type=jnp.float32
    )
    place = place_ref[0]
    share = own_ref.shape[0]
    mine = pl.ds(pl.multiple_of(place * share, share), share)
    own_ref[...] = product[mine, :] + states_ref[mine, :].astype(jnp.float32)
    for m, send in enumerate(sends, 1):
        theirs = pl.ds(pl.multiple_of((place ^ m) * share, share), share)
        send[...] = product[theirs, :].astype(send.dtype)


def add_kernel(own_ref, *rest):
    total = own_ref[...]
    for ref in rest[:-1]:
        total = total + ref[...].astype(jnp.float32)
    rest[-1][...] = total.astype(jnp.bfloat16)


def shards(states, norm_gain, w_qkv, w_out, cache, context_len, block_owner, block_index):
    requests, depth = states.shape
    peers = lax.axis_size("seq")
    ranks = lax.axis_size("tp")
    parts, _, columns = w_qkv.shape
    blocks, _, tokens, _ = cache.shape
    half = requests // 2
    share = requests // peers
    lines = peers // 2
    out_columns = w_out.shape[1]
    rows = blocks * HEADS
    steps = blocks // GROUP
    limit = pltpu.CompilerParams(vmem_limit_bytes=24 * 1024 * 1024)
    most_room = pltpu.CompilerParams(vmem_limit_bytes=50 * 1024 * 1024)
    all_room = pltpu.CompilerParams(vmem_limit_bytes=60 * 1024 * 1024)
    in_vmem = pl.BlockSpec(memory_space=VMEM)
    in_hbm = pl.BlockSpec(memory_space=HBM)
    in_smem = pl.BlockSpec(memory_space=SMEM)
    anywhere = pl.BlockSpec(memory_space=pl.ANY)
    place = lax.axis_index("seq")
    at = place.reshape(1).astype(jnp.int32)

    def array(*shape, dtype=jnp.bfloat16):
        return jax.ShapeDtypeStruct(shape, dtype)

    def to_peer(value, m):
        return lax.ppermute(value, "seq", [(i, i ^ m) for i in range(peers)])

    def moves(size):
        return pl.CostEstimate(flops=0, bytes_accessed=size, transcendentals=0)

    sent, kept, sent_fresh, kept_fresh = pl.pallas_call(
        project_kernel,
        out_shape=(
            array(half, columns + LANES),
            array(half, columns + LANES, dtype=jnp.float32),
            array(half, 2 * columns),
            array(half, 2 * columns, dtype=jnp.float32),
        ),
        in_specs=[in_smem] + [in_hbm] * 3,
        out_specs=(in_vmem,) * 4,
        scratch_shapes=[
            pltpu.VMEM(states.shape, jnp.bfloat16),
            pltpu.VMEM(norm_gain.shape, jnp.bfloat16),
            pltpu.VMEM((parts, depth, columns), jnp.bfloat16),
            pltpu.SemaphoreType.DMA((parts + 2,)),
        ],
        compiler_params=all_room,
        name="project",
    )(at, states, norm_gain, w_qkv)
    received = to_peer(sent, 1)
    fresh_received = to_peer(sent_fresh, 1)

    positions = lax.dynamic_slice_in_dim(context_len, place % 2 * half, half) - 1
    pair = (jnp.arange(columns, dtype=jnp.int32) % (HEAD_DIM // 2)).astype(jnp.float32)
    frequency = 10000.0 ** (-pair * 2.0 / HEAD_DIM)
    angles = positions.astype(jnp.float32)[:, None] * frequency[None, :]

    table = (block_owner, block_index, context_len)
    plan = pl.pallas_call(
        functools.partial(plan_kernel, tokens),
        out_shape=(
            array(rows, half),
            array(rows, half),
            array(rows, LANES, dtype=jnp.int32),
            array(rows, LANES, dtype=jnp.float32),
        ),
        in_specs=[in_smem] * 4,
        compiler_params=limit,
        name="plan",
    )(at, *table)
    def stage(part, name):
        return pl.pallas_call(
            functools.partial(stage_kernel, part),
            out_shape=array(blocks, tokens, columns),
            in_specs=[in_hbm],
            out_specs=in_vmem,
            scratch_shapes=[pltpu.SemaphoreType.DMA((steps,))],
            compiler_params=most_room,
            cost_estimate=moves(cache.size),
            name=name,
        )(cache)

    keys, values = stage(0, "stage_keys"), stage(1, "stage_values")
    message = columns // LANES * half + ROWS * pl.cdiv(half, LANES)
    send, query = pl.pallas_call(
        halve_query_kernel,
        out_shape=(array(message, LANES), array(half, columns + LANES, dtype=jnp.float32)),
        in_specs=[in_vmem, in_vmem, anywhere, anywhere],
        compiler_params=pltpu.CompilerParams(vmem_limit_bytes=47 * 1024 * 1024),
        name="halve_query",
    )(kept, received, values, plan[0])
    received = [to_peer(send, 2 * m) for m in (1, *range(lines - 1, 1, -1))]
    (mask, sent_to, held), *later = sum_plan(lines)
    fresh_send, fresh = pl.pallas_call(
        functools.partial(halve_fresh_kernel, sent_to, held),
        out_shape=(
            array(share * len(sent_to), 2 * columns),
            array(share * len(held), 2 * columns, dtype=jnp.float32),
        ),
        in_specs=[in_smem, in_vmem, in_vmem],
        scratch_shapes=[pltpu.VMEM((half, 2 * columns), jnp.float32)],
        compiler_params=limit,
        name="halve_fresh",
    )(at, kept_fresh, fresh_received)
    fresh_received = to_peer(fresh_send, 2 * mask)
    for mask, sent_to, still in later:
        fresh_send, fresh = pl.pallas_call(
            functools.partial(fold_kernel, held, sent_to, still),
            out_shape=(
                array(share * len(sent_to), 2 * columns),
                array(share * len(still), 2 * columns, dtype=jnp.float32),
            ),
            compiler_params=limit,
            name="fold",
        )(fresh, fresh_received)
        held = still
        fresh_received = to_peer(fresh_send, 2 * mask)
    cosine, sine = jnp.cos(angles), jnp.sin(angles)
    mine, scale = pl.pallas_call(
        functools.partial(query_kernel, depth * peers),
        out_shape=(array(half, columns), array(half, LANES, dtype=jnp.float32)),
        in_specs=[anywhere] + [in_vmem] * (3 + len(received)),
        compiler_params=pltpu.CompilerParams(vmem_limit_bytes=47 * 1024 * 1024),
        name="query",
    )(keys, query, cosine, sine, *received)
    other = to_peer(mine, 1)
    updated, token = pl.pallas_call(
        store_keys_kernel,
        out_shape=(array(*cache.shape), array(8, LANES, dtype=jnp.float32)),
        in_specs=[anywhere, in_vmem],
        out_specs=(in_hbm, in_vmem),
        scratch_shapes=[pltpu.SemaphoreType.DMA((steps,))],
        compiler_params=most_room,
        cost_estimate=moves(cache.size),
        name="store_keys",
    )(mine, keys)

    part, stat = pl.pallas_call(
        attend_kernel,
        out_shape=(
            array(2 * ROWS, columns, dtype=jnp.float32),
            array(ROWS, LANES, dtype=jnp.float32),
        ),
        in_specs=[in_vmem] * 8 + [anywhere],
        compiler_params=pltpu.CompilerParams(vmem_limit_bytes=47 * 1024 * 1024),
        name="attend",
    )(mine, other, *plan, keys, values, token)
    piece = pl.pallas_call(
        news_kernel,
        out_shape=array(columns // LANES * (2 * ROWS + share) + ROWS, LANES),
        in_specs=[in_smem] + [in_vmem] * 8,
        scratch_shapes=[pltpu.VMEM((half, columns), jnp.float32)],
        compiler_params=limit,
        name="news",
    )(at, mine, scale, cosine, sine, fresh, fresh_received, part, stat)
    updated, token = pl.pallas_call(
        store_values_kernel,
        out_shape=(array(*cache.shape), array(8, LANES, dtype=jnp.float32)),
        in_specs=[anywhere, in_vmem, in_hbm],
        out_specs=(in_hbm, in_vmem),
        scratch_shapes=[pltpu.SemaphoreType.DMA((steps,))],
        input_output_aliases={2: 0},
        compiler_params=most_room,
        cost_estimate=moves(cache.size),
        name="store_values",
    )(piece, values, updated)
    column = [to_peer(piece, 2 * m) if m else piece for m in line_order(lines)]
    pieces = list(column)
    for group in line_groups(lines):
        joined = column[group[0]]
        if len(group) > 1:
            joined = pl.pallas_call(
                join_kernel,
                out_shape=array(len(group) * piece.shape[0], LANES),
                in_specs=[anywhere] + [in_vmem] * len(group),
                compiler_params=limit,
                name="join",
            )(token, *[column[i] for i in group])
        pieces.append(to_peer(joined, 1))
    near = pl.pallas_call(
        fetch_kernel,
        out_shape=array(blocks, 2, ROWS, columns),
        in_specs=[in_smem] * 3 + [anywhere, in_hbm],
        out_specs=in_vmem,
        scratch_shapes=[pltpu.SemaphoreType.DMA((blocks,))],
        compiler_params=most_room,
        cost_estimate=moves(blocks * ROWS * columns * 8),
        name="fetch",
    )(*table, piece, cache)
    rank = lax.axis_index("tp")
    kept_rows = requests // ranks
    own, *sends = pl.pallas_call(
        functools.partial(output_kernel, peers),
        out_shape=(
            array(kept_rows, out_columns, dtype=jnp.float32),
            *(array(kept_rows, out_columns, dtype=jnp.bfloat16) for _ in range(1, ranks)),
        ),
        in_specs=[in_smem] + [in_vmem] * (len(pieces) + 2) + [anywhere],
        out_specs=(in_vmem,) * ranks,
        scratch_shapes=[pltpu.VMEM((requests, out_columns), jnp.float32)],
        compiler_params=limit,
        name="output",
    )(rank.reshape(1).astype(jnp.int32), *pieces, w_out, states, near)
    moved = [
        lax.ppermute(sends[m - 1], "tp", [(i, i ^ m) for i in range(ranks)])
        for m in (1, *range(ranks - 1, 1, -1))
    ]
    hidden = pl.pallas_call(
        add_kernel,
        out_shape=array(kept_rows, out_columns),
        compiler_params=limit,
        name="add",
    )(own, *moved)
    updated = pl.pallas_call(
        functools.partial(patch_kernel, peers),
        out_shape=array(*cache.shape),
        in_specs=[in_smem] * 4 + [anywhere] + [in_vmem] * (len(pieces) + 1) + [in_hbm],
        out_specs=in_hbm,
        scratch_shapes=[
            pltpu.VMEM((peers, 2 * share, columns), jnp.float32),
            pltpu.VMEM((blocks, 2, ROWS, columns), jnp.bfloat16),
            pltpu.SemaphoreType.DMA((blocks,)),
        ],
        input_output_aliases={6 + len(pieces): 0},
        compiler_params=most_room,
        cost_estimate=moves(blocks * ROWS * columns * 8),
        name="patch",
    )(at, *table, sends[0], *pieces, near, updated)
    return (hidden, updated)


def solution(mesh):
    return jax.shard_map(
        shards,
        mesh=mesh,
        in_specs=(
            P(None, "seq"),
            P("seq"),
            P(None, "seq", "tp"),
            P("tp", "seq"),
            P("seq", None, None, "tp"),
            P(),
            P("seq"),
            P("seq"),
        ),
        out_specs=(P("tp", "seq"), P("seq", None, None, "tp")),
        check_vma=False,
    )
```
